32 devices in a mesh: dp: 16 (over z, y, core), rep: 2 (over x).
Axes of the slice: x: 2, y: 2, z: 4, core: 2. Of those that a mesh axis runs over, the one named last changes fastest.
Arguments:
- tokens: bfloat16 [2048, 1664], P('dp'), may hold values from -6 to 6
- expert_ids: int32 [2048, 2], P('dp'), may hold values from 0 to 3, all different within a row; in each aligned block of 128 rows (0 to 127, 128 to 255, ...) at most 72 rows name the same one
- priority: int32 [2048], P('dp'), may hold values from 0 to 63
- gate_values: float32 [2048, 2], P('dp'), may hold values from 0.05 to 1
- weight_in: bfloat16 [16, 1664, 1024], P('dp', None, 'rep'), may hold values from -0.15625 to 0.15625
- weight_out: bfloat16 [16, 1024, 1664], P('dp', 'rep'), may hold values from -0.09375 to 0.09375
- cotangent: bfloat16 [2048, 1664], P('dp'), may hold values from -6 to 6
Outputs:
- output: bfloat16 [2048, 1664], P('dp', 'rep')
- grad_tokens: bfloat16 [2048, 1664], P('dp', 'rep')
- grad_gates: float32 [2048, 2], P(('dp', 'rep'))
- grad_weight_in: bfloat16 [16, 1664, 1024], P('dp', None, 'rep')
- grad_weight_out: bfloat16 [16, 1024, 1664], P('dp', 'rep')
The draws below stay inside these ranges and needn't reach their ends.
Inputs may be any that keep to these rules, and one draw needn't show every extreme that they name: `expert_ids`: the two ids of a token differ. Among the 128 tokens of one index of dp no expert is named more than 72 times, and 72 is reached.
All inputs are finite; a program needn't handle non-finite values.
Results may differ from the reference program's by a relative error of at most 0.017.
Values may be sent and summed in bfloat16 or wider, within the bound.
No kernel may reach another device: no remote copies, remote signals or barrier semaphores. Data moves between devices by JAX's collectives and lax.ppermute only.
A program may use at most 128 MiB of HBM per device.

```python
import math
import jax
import jax.numpy as jnp
import numpy as np
from jax import lax

D = 1664
HID = 4096
HBLK = 4
PRIO = 64
TOK_DEV = 128
EXPERTS = 4
TOKENS = 2048
SLOT = 72
CAP = 1024
N_REP = 2


def with_ends(result, key, smallest, largest):
    spot = [jax.random.randint(jax.random.fold_in(key, axis), (), 0, length) for axis, length in enumerate(result.shape)]
    widest = result.shape.index(max(result.shape))
    beside = spot[:widest] + [(spot[widest] + 1) % result.shape[widest]] + spot[widest + 1:]
    return result.at[tuple(spot)].set(smallest).at[tuple(beside)].set(largest)


def block_scale(key, extent, pieces, least, top_value):
    loudness, own = 1.0, jax.random.fold_in(key, 6)
    for dim, blocks in pieces:
        steps = jnp.exp(jax.random.uniform(jax.random.fold_in(own, dim), (blocks,), jnp.float32, least / len(pieces), top_value / len(pieces)))
        loudness = loudness * jnp.repeat(steps, extent[dim] // blocks).reshape([-1 if axis == dim else 1 for axis in range(len(extent))])
    return loudness


def deal_out(rng, own, number, rows, amount, top, limit, skew):
    sequence = jax.random.permutation(rng, amount)
    packed, ordinary = portions_of(amount, rows * top, limit, skew, True), portions_of(amount, rows * top, limit, skew, False)
    places = jnp.arange(amount)

    def named(lengths, rotation):
        used = int((lengths > 0).sum())
        fixed = max(1, used // 4)
        passed = fixed + (places - fixed + rotation * (used - fixed)) % max(1, amount - fixed)
        return jnp.zeros((amount,), jnp.int32).at[sequence[jnp.where(places < fixed, places, passed)]].set(jnp.asarray(lengths, jnp.int32))

    lengths = jnp.where(number % 4 == 0, named(packed, number // 4), named(ordinary, number - number // 4 - 1))
    mixed = jax.random.permutation(jax.random.fold_in(own, 3), amount)
    source_of, receiver = mixed[0:amount // 2 * 2:2], mixed[1:amount // 2 * 2:2]
    slack = jnp.minimum(lengths[source_of] - 1, limit - lengths[receiver]) // 2
    slack = jnp.where((source_of == sequence[0]) | (receiver == sequence[0]) | (lengths[receiver] == 0), 0, jnp.maximum(slack, 0))
    passed = jax.random.randint(jax.random.fold_in(own, 4), (amount // 2,), 0, 1 << 20) % (slack + 1)
    lengths = lengths.at[source_of].add(-passed).at[receiver].add(passed)
    labels = jnp.searchsorted(jnp.cumsum(lengths), jnp.arange(rows * top), side="right").astype(jnp.int32)
    table = labels.reshape(top, rows).T
    table = table[jax.random.permutation(jax.random.fold_in(own, 1), rows)]
    rotation = jax.random.randint(jax.random.fold_in(own, 2), (rows, 1), 0, top)
    return jnp.take_along_axis(table, (jnp.arange(top)[None, :] + rotation) % top, axis=1)


def portions_of(count, total, bound, skew, full):
    portions = [(1 << 20) // math.isqrt(standing ** skew) + 1 for standing in range(1, count + 1)]
    largest = bound if full else min(bound, max(-(-total // count), total * portions[0] // sum(portions)))
    least = 1 if total - largest >= count - 1 else 0
    given, rest = [largest] + [least] * (count - 1), total - largest - least * (count - 1)
    while rest > 0:
        movable = [i for i in range(1, count) if given[i] < largest] or [i for i in range(1, count) if given[i] < bound]
        whole, budget = sum([portions[i] for i in movable]), rest
        for i in movable:
            addition = min(bound - given[i], max(1, budget * portions[i] // whole), rest)
            given[i] = given[i] + addition
            rest = rest - addition
    return np.array(given)


def normal_values(stream_key, dims, scale, limit, cuts=(), kind=jnp.bfloat16):
    entries = jax.random.normal(stream_key, dims, jnp.float32) * scale
    if len(cuts) > 0:
        entries = block_scale(stream_key, dims, cuts, -0.22, 0.18) * entries
    return jnp.clip(entries, min=-limit, max=limit).astype(kind)


def setup_inputs(seed: int = 0) -> dict:
    arg_keys = jax.random.split(jax.random.key(seed), 8)
    tokens = normal_values(arg_keys[0], (TOKENS, D), 1.0, 6.0, ((0, 16),))
    expert_ids_keys = jax.random.split(jax.random.fold_in(arg_keys[1], 1), TOKENS // TOK_DEV)
    expert_ids_turns = jax.random.permutation(jax.random.fold_in(arg_keys[1], 3), TOKENS // TOK_DEV)
    expert_ids = jax.vmap(lambda own, number: deal_out(jax.random.fold_in(arg_keys[1], 2), own, number, TOK_DEV, EXPERTS, 2, SLOT, 2))(expert_ids_keys, expert_ids_turns).reshape((TOKENS, 2))
    priority = with_ends(jax.random.randint(arg_keys[2], (TOKENS,), 0, PRIO), jax.random.fold_in(arg_keys[2], 1), 0, PRIO - 1).astype(jnp.int32)
    gate_values = jnp.clip(0.05 + 0.95 * jax.random.uniform(arg_keys[3], (TOKENS, 2), jnp.float32) ** block_scale(arg_keys[3], (TOKENS, 2), ((0, 16),), -0.2, 0.2), 0.05, 1.0)
    weight_in = normal_values(arg_keys[4], (HBLK * EXPERTS, D, HID // HBLK), D ** -0.5, 0.15625, ((0, 16), (2, 2)))
    weight_out = normal_values(arg_keys[5], (HBLK * EXPERTS, HID // HBLK, D), HID ** -0.5, 0.09375, ((0, 16), (1, 2)))
    cotangent = normal_values(arg_keys[6], (TOKENS, D), 1.0, 6.0, ((0, 16),))
    return {"tokens": tokens, "expert_ids": expert_ids, "priority": priority, "gate_values": gate_values, "weight_in": weight_in, "weight_out": weight_out, "cotangent": cotangent}


def gelu_parts(hidden_pre):
    normal_cdf = 0.5 * (1.0 + jax.scipy.special.erf(hidden_pre * (1.0 / math.sqrt(2.0))))
    density = jnp.exp(-0.5 * hidden_pre * hidden_pre) * (1.0 / math.sqrt(2.0 * math.pi))
    return (hidden_pre * normal_cdf, normal_cdf + hidden_pre * density)

def reference(tokens, expert_ids, priority, gate_values, weight_in, weight_out, cotangent):
    token_count = tokens.shape[0]
    model_width = tokens.shape[1]
    blocks = HBLK * N_REP
    block_width = HID // blocks
    assignments = 2 * token_count
    priority_key = (priority[:, None] + PRIO * (1 - jnp.arange(2, dtype=jnp.int32))[None, :]).reshape(-1)
    flat_expert = expert_ids.reshape(-1)
    expert_hot = (flat_expert[:, None] == jnp.arange(EXPERTS, dtype=jnp.int32)[None, :]).astype(jnp.int32)
    key_hot = (priority_key[:, None] == jnp.arange(2 * PRIO, dtype=jnp.int32)[None, :]).astype(jnp.int32)
    counts = jnp.dot(expert_hot.T, key_hot, preferred_element_type=jnp.int32)
    above_count = jnp.cumsum(counts[:, ::-1], axis=1)[:, ::-1]
    cutoff_key = lax.optimization_barrier(jnp.sum((above_count > CAP).astype(jnp.int32), axis=1))
    kept_mask = priority_key >= lax.optimization_barrier(jnp.sum(expert_hot * cutoff_key[None, :], axis=1))
    kept_hot = expert_hot * kept_mask.astype(jnp.int32)[:, None]
    position = lax.optimization_barrier(jnp.sum(kept_hot * (jnp.cumsum(kept_hot, axis=0) - kept_hot), axis=1))
    target = jnp.where(kept_mask, flat_expert * CAP + position, EXPERTS * CAP).astype(jnp.int32)
    table = jnp.full((EXPERTS * CAP + 1,), assignments, jnp.int32)
    table = table.at[target].set(jnp.arange(assignments, dtype=jnp.int32))
    members_all = table[:EXPERTS * CAP]
    in_full = weight_in.reshape(EXPERTS, HBLK, model_width, HID // HBLK).transpose(0, 2, 1, 3).reshape(EXPERTS, model_width, HID)
    out_full = weight_out.reshape(EXPERTS, HID, model_width)
    flat_gate = gate_values.reshape(-1)

    def one_expert(operands):
        members, matrix_in, matrix_out = operands
        valid = members < assignments
        safe_index = jnp.where(valid, members, 0)
        token_id = safe_index // 2
        rows = jnp.where(valid[:, None], tokens[token_id], jnp.zeros((), tokens.dtype))
        scale = jnp.where(valid, flat_gate[safe_index], jnp.zeros((), flat_gate.dtype))
        grad_rows = (scale[:, None] * cotangent[token_id].astype(jnp.float32)).astype(jnp.bfloat16)
        hidden_pre = jnp.dot(rows, matrix_in, preferred_element_type=jnp.float32)
        activation, slope = gelu_parts(hidden_pre)
        activation = activation.astype(jnp.bfloat16)
        partial_out = jnp.einsum('rbh,bhd->rbd', activation.reshape(CAP, blocks, block_width).astype(jnp.float32), matrix_out.reshape(blocks, block_width, model_width).astype(jnp.float32)).astype(jnp.bfloat16)
        expert_out = lax.optimization_barrier(jnp.sum(partial_out.astype(jnp.float32), axis=1))
        grad_act = jnp.dot(grad_rows, matrix_out.T, preferred_element_type=jnp.float32)
        grad_pre = (grad_act * slope).astype(jnp.bfloat16)
        grad_in = jnp.dot(rows.T, grad_pre, preferred_element_type=jnp.float32).astype(jnp.bfloat16)
        grad_out = jnp.dot(activation.T, grad_rows, preferred_element_type=jnp.float32).astype(jnp.bfloat16)
        partial_dx = jnp.einsum('rbh,dbh->rbd', grad_pre.reshape(CAP, blocks, block_width).astype(jnp.float32), matrix_in.reshape(model_width, blocks, block_width).astype(jnp.float32)).astype(jnp.bfloat16)
        expert_dx = lax.optimization_barrier(jnp.sum(partial_dx.astype(jnp.float32), axis=1))
        return (expert_out, expert_dx, grad_in, grad_out)
    expert_out, expert_dx, grad_in, grad_out = lax.map(one_expert, (members_all.reshape(EXPERTS, CAP), in_full, out_full))
    out_rows = jnp.zeros((assignments + 1, model_width), jnp.float32)
    out_rows = out_rows.at[members_all].set(expert_out.reshape(-1, model_width))
    out_rows = out_rows[:assignments].reshape(token_count, 2, model_width)
    dx_rows = jnp.zeros((assignments + 1, model_width), jnp.float32)
    dx_rows = dx_rows.at[members_all].set(expert_dx.reshape(-1, model_width))
    dx_rows = dx_rows[:assignments].reshape(token_count, 2, model_width)
    output = lax.optimization_barrier(jnp.sum(gate_values[:, :, None] * out_rows, axis=1)).astype(jnp.bfloat16)
    grad_tokens = lax.optimization_barrier(jnp.sum(dx_rows, axis=1)).astype(jnp.bfloat16)
    grad_gates = lax.optimization_barrier(jnp.sum(cotangent.astype(jnp.float32)[:, None, :] * out_rows, axis=2))
    grad_weight_in = grad_in.reshape(EXPERTS, model_width, HBLK, HID // HBLK).transpose(0, 2, 1, 3).reshape(EXPERTS * HBLK, model_width, HID // HBLK)
    grad_weight_out = grad_out.reshape(EXPERTS * HBLK, HID // HBLK, model_width)
    return (output, grad_tokens, grad_gates, grad_weight_in, grad_weight_out)
```

```python
import math

import jax
import jax.numpy as jnp
from jax import lax
from jax.sharding import PartitionSpec as P

HBLK = 4
PRIO = 64


def gelu_parts(hidden_pre):
    normal_cdf = 0.5 * (1.0 + jax.scipy.special.erf(hidden_pre * (1.0 / math.sqrt(2.0))))
    density = jnp.exp(-0.5 * hidden_pre * hidden_pre) * (1.0 / math.sqrt(2.0 * math.pi))
    return (hidden_pre * normal_cdf, normal_cdf + hidden_pre * density)


def general_body(tokens, expert_ids, priority, gate_values, weight_in, weight_out, cotangent):
    token_count = tokens.shape[0]
    dp_count = lax.axis_size("dp")
    experts = dp_count // HBLK
    slot_count = min(token_count, 2 * token_count // experts + max(1, token_count // (4 * experts)))
    capacity = 2 * token_count * dp_count // experts
    row_total = dp_count * slot_count
    contract_first = (((0,), (0,)), ((), ()))
    contract_last = (((1,), (1,)), ((), ()))
    priority_key = (
        priority[:, None] + PRIO * (1 - jnp.arange(2, dtype=jnp.int32))[None, :]
    ).reshape(-1)
    flat_expert = expert_ids.reshape(-1)
    expert_hot = (flat_expert[:, None] == jnp.arange(experts, dtype=jnp.int32)[None, :]).astype(
        jnp.int32
    )
    key_hot = (priority_key[:, None] == jnp.arange(2 * PRIO, dtype=jnp.int32)[None, :]).astype(
        jnp.int32
    )
    local_counts = jnp.dot(expert_hot.T, key_hot, preferred_element_type=jnp.int32)
    counts = lax.psum(local_counts, "dp")
    above_count = jnp.cumsum(counts[:, ::-1], axis=1)[:, ::-1]
    cutoff_key = jnp.sum((above_count > capacity).astype(jnp.int32), axis=1)
    kept_mask = priority_key >= jnp.sum(expert_hot * cutoff_key[None, :], axis=1)
    before_count = jnp.cumsum(expert_hot, axis=0) - expert_hot
    slot_index = jnp.sum(expert_hot * before_count, axis=1)
    slot_hot = (slot_index[:, None] == jnp.arange(slot_count, dtype=jnp.int32)[None, :]).astype(
        jnp.int32
    )
    place_map = (
        expert_hot[:, :, None] * slot_hot[:, None, :] * kept_mask.astype(jnp.int32)[:, None, None]
    )
    place_map = place_map.astype(jnp.bfloat16).reshape(2 * token_count, experts * slot_count)
    token_place = jnp.sum(place_map.reshape(token_count, 2, experts * slot_count), axis=1)
    grad_source = (
        gate_values.reshape(-1)[:, None] * jnp.repeat(cotangent, 2, axis=0).astype(jnp.float32)
    ).astype(jnp.bfloat16)
    wide_index = jnp.arange(row_total, dtype=jnp.int32)
    wide_index = wide_index // (HBLK * slot_count) * slot_count + wide_index % slot_count

    def widen(matrix):
        return jnp.take(matrix, wide_index, axis=0)

    send_rows = lax.dot_general(
        token_place, tokens, contract_first, preferred_element_type=jnp.float32
    ).astype(jnp.bfloat16)
    send_grads = lax.dot_general(
        place_map, grad_source, contract_first, preferred_element_type=jnp.float32
    ).astype(jnp.bfloat16)
    rows, grad_rows = (
        lax.all_to_all(widen(send_rows), "dp", split_axis=0, concat_axis=0, tiled=True),
        lax.all_to_all(widen(send_grads), "dp", split_axis=0, concat_axis=0, tiled=True),
    )
    matrix_in = weight_in[0]
    matrix_out = weight_out[0]
    hidden_pre = jnp.dot(rows, matrix_in, preferred_element_type=jnp.float32)
    activation, slope = gelu_parts(hidden_pre)
    activation = activation.astype(jnp.bfloat16)
    partial_out = jnp.dot(activation, matrix_out, preferred_element_type=jnp.float32).astype(
        jnp.bfloat16
    )
    grad_act = lax.dot_general(
        grad_rows, matrix_out, contract_last, preferred_element_type=jnp.float32
    )
    grad_pre = (grad_act * slope).astype(jnp.bfloat16)
    grad_in = lax.dot_general(
        rows, grad_pre, contract_first, preferred_element_type=jnp.float32
    ).astype(jnp.bfloat16)
    grad_out = lax.dot_general(
        activation, grad_rows, contract_first, preferred_element_type=jnp.float32
    ).astype(jnp.bfloat16)
    partial_dx = lax.dot_general(
        grad_pre, matrix_in, contract_last, preferred_element_type=jnp.float32
    ).astype(jnp.bfloat16)
    block_range = jnp.arange(HBLK, dtype=jnp.int32)
    pick_index = (
        (flat_expert[:, None] * HBLK + block_range[None, :]) * slot_count + slot_index[:, None]
    ).reshape(-1)

    def pick_rows(returned):
        width = returned.shape[-1]
        picked = jnp.take(returned, pick_index, axis=0)
        summed = jnp.sum(picked.reshape(2 * token_count, HBLK, width).astype(jnp.float32), axis=1)
        return jnp.where(kept_mask[:, None], summed, 0.0).reshape(token_count, 2, width)

    back_out, back_dx = (
        lax.all_to_all(partial_out, "dp", split_axis=0, concat_axis=0, tiled=True),
        lax.all_to_all(partial_dx, "dp", split_axis=0, concat_axis=0, tiled=True),
    )
    out_rows = pick_rows(back_out)
    dx_rows = pick_rows(back_dx)
    mixed = jnp.sum(gate_values[:, :, None] * out_rows, axis=1)
    token_grad = jnp.sum(dx_rows, axis=1)
    gate_grad = jnp.sum(cotangent.astype(jnp.float32)[:, None, :] * out_rows, axis=2)
    gate_grad = lax.psum_scatter(gate_grad, "rep", scatter_dimension=0, tiled=True)
    mixed, token_grad = (
        lax.psum_scatter(mixed.astype(jnp.bfloat16), "rep", scatter_dimension=1, tiled=True).astype(
            jnp.float32
        ),
        lax.psum_scatter(
            token_grad.astype(jnp.bfloat16), "rep", scatter_dimension=1, tiled=True
        ).astype(jnp.float32),
    )
    return (
        mixed.astype(jnp.bfloat16),
        token_grad.astype(jnp.bfloat16),
        gate_grad,
        grad_in[None],
        grad_out[None],
    )


GROUPS = ((0,), (1, 3), (2,))


def plane_body(tokens, expert_ids, priority, gate_values, weight_in, weight_out, cotangent):
    token_count, width = tokens.shape
    dp_count = lax.axis_size("dp")
    experts = dp_count // HBLK
    slot_count = min(token_count, 2 * token_count // experts + max(1, token_count // (4 * experts)))
    capacity = 2 * token_count * dp_count // experts
    contract_first = (((0,), (0,)), ((), ()))
    contract_last = (((1,), (1,)), ((), ()))
    place_dp = lax.axis_index("dp")
    first_half = lax.axis_index("rep") == 0
    plane, quarter = place_dp // HBLK, place_dp % HBLK
    core_zero = quarter % 2 == 0

    def dp_index(z, q):
        return z * HBLK + q

    def permutation(move):
        pairs = []
        for z in range(experts):
            for q in range(HBLK):
                for x in range(2):
                    z2, q2, x2 = move(z, q, x)
                    pairs.append((2 * dp_index(z, q) + x, 2 * dp_index(z2, q2) + x2))
        return pairs

    def send(array, move):
        return lax.ppermute(array, ("dp", "rep"), permutation(move))

    def along_first(z, q, x):
        return (z, q, 1 - x) if q % 2 == 0 else (z, q ^ 2, x)

    def along_second(z, q, x):
        return (z, q ^ 2, x) if q % 2 == 0 else (z, q, 1 - x)

    def other_core(z, q, x):
        return (z, q ^ 1, x)

    def planes_on(k):
        return lambda z, q, x: ((z + k) % experts, q, x)

    groups = GROUPS if experts == 4 else tuple((k,) for k in range(experts))

    ids = [expert_ids[:, 0:1], expert_ids[:, 1:2]]
    near = (plane + jnp.arange(experts, dtype=jnp.int32)) % experts
    chosen = [(one == near[None, :]) for one in ids]
    chosen_any = (chosen[0] | chosen[1]).astype(jnp.bfloat16)
    before = (
        jnp.arange(token_count, dtype=jnp.int32)[:, None]
        > jnp.arange(token_count, dtype=jnp.int32)[None, :]
    ).astype(jnp.bfloat16)
    rank = jnp.dot(before, chosen_any, preferred_element_type=jnp.float32).astype(jnp.int32)
    slots = jnp.arange(slot_count, dtype=jnp.int32)[None, :]
    at_slot = [rank[:, k : k + 1] == slots for k in range(experts)]
    place = [[at_slot[k] & chosen[j][:, k : k + 1] for k in range(experts)] for j in range(2)]
    place_any = [(place[0][k] | place[1][k]).astype(jnp.bfloat16) for k in range(experts)]
    source = jnp.where(first_half, tokens, cotangent)
    blocks = [
        lax.dot_general(
            place_any[k], source, contract_first, preferred_element_type=jnp.float32
        ).astype(jnp.bfloat16)
        for k in range(experts)
    ]
    arrived = [blocks[0]] + [send(blocks[k], planes_on(k)) for k in range(1, experts)]

    keys = [priority + PRIO, priority]
    slot_gate = []
    slot_key = []
    for k in range(experts):
        slot_gate.append(
            sum(
                jnp.sum(jnp.where(place[j][k], gate_values[:, j : j + 1], 0.0), axis=0)
                for j in range(2)
            )
        )
        slot_key.append(
            sum(
                jnp.sum(jnp.where(place[j][k], keys[j][:, None].astype(jnp.float32) + 1.0, 0.0), axis=0)
                for j in range(2)
            )
            - 1.0
        )
    to_whole = (jnp.arange(experts, dtype=jnp.int32) - plane) % experts
    card = jnp.concatenate(
        [jnp.take(jnp.stack(slot_gate), to_whole, axis=0), jnp.take(jnp.stack(slot_key), to_whole, axis=0)], axis=0
    )
    cards = lax.all_gather(card, "dp", axis=0, tiled=False)
    all_gates, all_keys = cards[:, :experts], cards[:, experts:]
    levels = jnp.arange(2 * PRIO, dtype=jnp.float32)
    above = jnp.sum(
        (all_keys[:, :, None, :] >= levels[None, None, :, None]).astype(jnp.float32), axis=(0, 3)
    )
    cutoff = jnp.sum((above > capacity).astype(jnp.float32), axis=1)
    own_keys = lax.dynamic_index_in_dim(all_keys, plane, 1, keepdims=False)
    own_gates = lax.dynamic_index_in_dim(all_gates, plane, 1, keepdims=False)
    own_cutoff = lax.dynamic_index_in_dim(cutoff, plane, 0, keepdims=False)
    own_gates = jnp.where(own_keys >= own_cutoff, own_gates, 0.0)
    near_cutoff = jnp.take(cutoff, near, axis=0)

    matrix_in = weight_in[0]
    matrix_out = weight_out[0]

    all_rows, all_grads, all_act, all_pre = [], [], [], []
    returned = [None] * experts
    for group in groups:
        count = len(group) * slot_count
        own = [arrived[k] for k in group]
        b00 = own[0] if len(own) == 1 else jnp.concatenate(own, axis=0)
        r1 = send(b00, along_first)
        r2 = send(b00, along_second)
        b11 = send(r1, along_second)
        b10 = jnp.where(core_zero, r2, r1)
        b01 = jnp.where(core_zero, r1, r2)
        near_rows = jnp.concatenate(
            [
                jnp.where(first_half, b00, b01),
                jnp.where(first_half, b10, b11),
                jnp.where(first_half, b01, b00),
                jnp.where(first_half, b11, b10),
            ],
            axis=0,
        )
        far_rows = send(near_rows, other_core)
        partial = []
        for far, both in ((0, near_rows), (1, far_rows)):
            rows, grads = both[: 2 * count], both[2 * count :]
            index = jnp.stack(
                [
                    dp_index((plane - k) % experts, quarter ^ (2 * other_y + far))
                    for other_y in range(2)
                    for k in group
                ]
            )
            gate = jnp.take(own_gates, index, axis=0).reshape(2 * count, 1)
            hidden_pre = jnp.dot(rows, matrix_in, preferred_element_type=jnp.float32)
            activation, slope = gelu_parts(hidden_pre)
            gated = (activation * gate).astype(jnp.bfloat16)
            activation = activation.astype(jnp.bfloat16)
            grad_act = lax.dot_general(
                grads, matrix_out, contract_last, preferred_element_type=jnp.float32
            )
            grad_pre = (grad_act * slope * gate).astype(jnp.bfloat16)
            part_out = jnp.dot(activation, matrix_out, preferred_element_type=jnp.float32)
            part_dx = lax.dot_general(
                grad_pre, matrix_in, contract_last, preferred_element_type=jnp.float32
            )
            partial.append((part_out.astype(jnp.bfloat16), part_dx.astype(jnp.bfloat16)))
            all_rows.append(rows)
            all_grads.append(grads)
            all_act.append(gated)
            all_pre.append(grad_pre)

        def add(*terms):
            return sum(term.astype(jnp.float32) for term in terms).astype(jnp.bfloat16)

        sum_out = add(partial[0][0], send(partial[1][0], other_core))
        sum_dx = add(partial[0][1], send(partial[1][1], other_core))
        own_sum = jnp.where(first_half, sum_out, sum_dx)
        other_sum = jnp.where(first_half, sum_dx, sum_out)
        a00, a10 = own_sum[:count], own_sum[count:]
        a01, a11 = other_sum[:count], other_sum[count:]
        back = send(
            jnp.concatenate([jnp.where(core_zero, a01, a10), a11], axis=0), along_first
        )
        last = add(jnp.where(core_zero, a10, a01), back[count:])
        done = add(a00, back[:count], send(last, along_second))
        for spot, k in enumerate(group):
            piece = done[spot * slot_count : (spot + 1) * slot_count]
            returned[k] = piece if k == 0 else send(piece, planes_on(experts - k))

    grad_in = lax.dot_general(
        jnp.concatenate(all_rows, axis=0),
        jnp.concatenate(all_pre, axis=0),
        contract_first,
        preferred_element_type=jnp.float32,
    ).astype(jnp.bfloat16)
    grad_out = lax.dot_general(
        jnp.concatenate(all_act, axis=0),
        jnp.concatenate(all_grads, axis=0),
        contract_first,
        preferred_element_type=jnp.float32,
    ).astype(jnp.bfloat16)

    back_rows = jnp.concatenate(returned, axis=0)
    mixed = 0.0
    gate_grads = []
    for j in range(2):
        key = keys[j][:, None].astype(jnp.float32)
        kept = chosen[j] & (key >= near_cutoff[None, :])
        picker = jnp.concatenate(
            [(at_slot[k] & kept[:, k : k + 1]).astype(jnp.bfloat16) for k in range(experts)], axis=1
        )
        picked = jnp.dot(picker, back_rows, preferred_element_type=jnp.float32)
        mixed = mixed + picked * jnp.where(first_half, gate_values[:, j : j + 1], 1.0)
        gate_grads.append(jnp.sum(picked * cotangent.astype(jnp.float32), axis=1, keepdims=True))
    mixed = mixed.astype(jnp.bfloat16)
    gate_grad = jnp.concatenate(gate_grads, axis=1)
    half = width // 2
    swap = [(0, 1), (1, 0)]
    left, right = mixed[:, :half], mixed[:, half:]
    kept_part = jnp.where(first_half, left, right)
    got_part = lax.ppermute(jnp.where(first_half, right, left), "rep", swap)
    rows_half = token_count // 2
    got_gate = lax.ppermute(gate_grad[rows_half:], "rep", swap)
    return (
        jnp.where(first_half, kept_part, got_part),
        jnp.where(first_half, got_part, kept_part),
        jnp.where(first_half, gate_grad[:rows_half], got_gate),
        grad_in[None],
        grad_out[None],
    )


def solution(mesh):
    placed = (
        P("dp", None),
        P("dp", None),
        P("dp"),
        P("dp", None),
        P("dp", None, "rep"),
        P("dp", "rep", None),
        P("dp", None),
    )
    body = plane_body if mesh.shape["rep"] == 2 else general_body
    return jax.shard_map(
        body,
        mesh=mesh,
        in_specs=placed,
        out_specs=(
            P("dp", "rep"),
            P("dp", "rep"),
            P(("dp", "rep"), None),
            P("dp", None, "rep"),
            P("dp", "rep", None),
        ),
        check_vma=False,
    )
```

```python
import math

import jax
import jax.numpy as jnp
from jax import lax
from jax.sharding import PartitionSpec as P

HBLK = 4
PRIO = 64


def gelu_parts(hidden_pre):
    normal_cdf = 0.5 * (1.0 + jax.scipy.special.erf(hidden_pre * (1.0 / math.sqrt(2.0))))
    density = jnp.exp(-0.5 * hidden_pre * hidden_pre) * (1.0 / math.sqrt(2.0 * math.pi))
    return (hidden_pre * normal_cdf, normal_cdf + hidden_pre * density)


def general_body(tokens, expert_ids, priority, gate_values, weight_in, weight_out, cotangent):
    token_count = tokens.shape[0]
    dp_count = lax.axis_size("dp")
    experts = dp_count // HBLK
    slot_count = min(token_count, 2 * token_count // experts + max(1, token_count // (4 * experts)))
    capacity = 2 * token_count * dp_count // experts
    row_total = dp_count * slot_count
    contract_first = (((0,), (0,)), ((), ()))
    contract_last = (((1,), (1,)), ((), ()))
    priority_key = (
        priority[:, None] + PRIO * (1 - jnp.arange(2, dtype=jnp.int32))[None, :]
    ).reshape(-1)
    flat_expert = expert_ids.reshape(-1)
    expert_hot = (flat_expert[:, None] == jnp.arange(experts, dtype=jnp.int32)[None, :]).astype(
        jnp.int32
    )
    key_hot = (priority_key[:, None] == jnp.arange(2 * PRIO, dtype=jnp.int32)[None, :]).astype(
        jnp.int32
    )
    local_counts = jnp.dot(expert_hot.T, key_hot, preferred_element_type=jnp.int32)
    counts = lax.psum(local_counts, "dp")
    above_count = jnp.cumsum(counts[:, ::-1], axis=1)[:, ::-1]
    cutoff_key = jnp.sum((above_count > capacity).astype(jnp.int32), axis=1)
    kept_mask = priority_key >= jnp.sum(expert_hot * cutoff_key[None, :], axis=1)
    before_count = jnp.cumsum(expert_hot, axis=0) - expert_hot
    slot_index = jnp.sum(expert_hot * before_count, axis=1)
    slot_hot = (slot_index[:, None] == jnp.arange(slot_count, dtype=jnp.int32)[None, :]).astype(
        jnp.int32
    )
    place_map = (
        expert_hot[:, :, None] * slot_hot[:, None, :] * kept_mask.astype(jnp.int32)[:, None, None]
    )
    place_map = place_map.astype(jnp.bfloat16).reshape(2 * token_count, experts * slot_count)
    token_place = jnp.sum(place_map.reshape(token_count, 2, experts * slot_count), axis=1)
    grad_source = (
        gate_values.reshape(-1)[:, None] * jnp.repeat(cotangent, 2, axis=0).astype(jnp.float32)
    ).astype(jnp.bfloat16)
    wide_index = jnp.arange(row_total, dtype=jnp.int32)
    wide_index = wide_index // (HBLK * slot_count) * slot_count + wide_index % slot_count

    def widen(matrix):
        return jnp.take(matrix, wide_index, axis=0)

    send_rows = lax.dot_general(
        token_place, tokens, contract_first, preferred_element_type=jnp.float32
    ).astype(jnp.bfloat16)
    send_grads = lax.dot_general(
        place_map, grad_source, contract_first, preferred_element_type=jnp.float32
    ).astype(jnp.bfloat16)
    rows, grad_rows = (
        lax.all_to_all(widen(send_rows), "dp", split_axis=0, concat_axis=0, tiled=True),
        lax.all_to_all(widen(send_grads), "dp", split_axis=0, concat_axis=0, tiled=True),
    )
    matrix_in = weight_in[0]
    matrix_out = weight_out[0]
    hidden_pre = jnp.dot(rows, matrix_in, preferred_element_type=jnp.float32)
    activation, slope = gelu_parts(hidden_pre)
    activation = activation.astype(jnp.bfloat16)
    partial_out = jnp.dot(activation, matrix_out, preferred_element_type=jnp.float32).astype(
        jnp.bfloat16
    )
    grad_act = lax.dot_general(
        grad_rows, matrix_out, contract_last, preferred_element_type=jnp.float32
    )
    grad_pre = (grad_act * slope).astype(jnp.bfloat16)
    grad_in = lax.dot_general(
        rows, grad_pre, contract_first, preferred_element_type=jnp.float32
    ).astype(jnp.bfloat16)
    grad_out = lax.dot_general(
        activation, grad_rows, contract_first, preferred_element_type=jnp.float32
    ).astype(jnp.bfloat16)
    partial_dx = lax.dot_general(
        grad_pre, matrix_in, contract_last, preferred_element_type=jnp.float32
    ).astype(jnp.bfloat16)
    block_range = jnp.arange(HBLK, dtype=jnp.int32)
    pick_index = (
        (flat_expert[:, None] * HBLK + block_range[None, :]) * slot_count + slot_index[:, None]
    ).reshape(-1)

    def pick_rows(returned):
        width = returned.shape[-1]
        picked = jnp.take(returned, pick_index, axis=0)
        summed = jnp.sum(picked.reshape(2 * token_count, HBLK, width).astype(jnp.float32), axis=1)
        return jnp.where(kept_mask[:, None], summed, 0.0).reshape(token_count, 2, width)

    back_out, back_dx = (
        lax.all_to_all(partial_out, "dp", split_axis=0, concat_axis=0, tiled=True),
        lax.all_to_all(partial_dx, "dp", split_axis=0, concat_axis=0, tiled=True),
    )
    out_rows = pick_rows(back_out)
    dx_rows = pick_rows(back_dx)
    mixed = jnp.sum(gate_values[:, :, None] * out_rows, axis=1)
    token_grad = jnp.sum(dx_rows, axis=1)
    gate_grad = jnp.sum(cotangent.astype(jnp.float32)[:, None, :] * out_rows, axis=2)
    gate_grad = lax.psum_scatter(gate_grad, "rep", scatter_dimension=0, tiled=True)
    mixed, token_grad = (
        lax.psum_scatter(mixed.astype(jnp.bfloat16), "rep", scatter_dimension=1, tiled=True).astype(
            jnp.float32
        ),
        lax.psum_scatter(
            token_grad.astype(jnp.bfloat16), "rep", scatter_dimension=1, tiled=True
        ).astype(jnp.float32),
    )
    return (
        mixed.astype(jnp.bfloat16),
        token_grad.astype(jnp.bfloat16),
        gate_grad,
        grad_in[None],
        grad_out[None],
    )


GROUPS = ((0,), (1,), (3,), (2,))
PLAN = (
    "Z 1",
    "D1 0",
    "Z 3",
    "Z 2",
    "D2 0",
    "K 0",
    "D1 1",
    "SEL 0",
    "D2 1",
    "D1 2",
    "CN 0",
    "CF 0",
    "SEL 1",
    "D2 2",
    "D1 3",
    "K 1",
    "CN 1",
    "CF 1",
    "SEL 2",
    "D2 3",
    "K 2",
    "R1 1",
    "CN 2",
    "CF 2",
    "SEL 3",
    "R2 1",
    "R1 2",
    "K 3",
    "CN 3",
    "CF 3",
    "H 1",
    "R2 2",
    "R1 3",
    "H 2",
    "R1 0",
    "R2 3",
    "CUT 0",
    "W1 0",
    "H 3",
    "R2 0",
    "W2 0",
    "H 0",
)


def plane_body(tokens, expert_ids, priority, gate_values, weight_in, weight_out, cotangent):
    token_count, width = tokens.shape
    dp_count = lax.axis_size("dp")
    experts = dp_count // HBLK
    slot_count = min(token_count, 2 * token_count // experts + max(1, token_count // (4 * experts)))
    capacity = 2 * token_count * dp_count // experts
    contract_first = (((0,), (0,)), ((), ()))
    contract_last = (((1,), (1,)), ((), ()))
    place_dp = lax.axis_index("dp")
    first_half = lax.axis_index("rep") == 0
    plane, quarter = place_dp // HBLK, place_dp % HBLK
    core_zero = quarter % 2 == 0
    groups = GROUPS

    def permutation(move):
        pairs = []
        for z in range(experts):
            for q in range(HBLK):
                for x in range(2):
                    z2, q2, x2 = move(z, q, x)
                    pairs.append((2 * (z * HBLK + q) + x, 2 * (z2 * HBLK + q2) + x2))
        return pairs

    def send(array, move):
        return lax.ppermute(array, ("dp", "rep"), permutation(move))

    def along_first(z, q, x):
        return (z, q, 1 - x) if q % 2 == 0 else (z, q ^ 2, x)

    def along_second(z, q, x):
        return (z, q ^ 2, x) if q % 2 == 0 else (z, q, 1 - x)

    def other_core(z, q, x):
        return (z, q ^ 1, x)

    def other_row(z, q, x):
        return (z, q ^ 2, x)

    def planes_on(k):
        return lambda z, q, x: ((z + k) % experts, q, x)

    def add(*terms):
        return sum(term.astype(jnp.float32) for term in terms).astype(jnp.bfloat16)

    def step(made, *values):
        if made:
            values, _ = lax.optimization_barrier((values, made))
        return values if len(values) > 1 else values[0]

    def join(parts):
        return parts[0] if len(parts) == 1 else jnp.concatenate(parts, axis=0)

    ids = [expert_ids[:, j][None, :] for j in range(2)]
    gates = [gate_values[:, j][None, :] for j in range(2)]
    keys = [(priority + PRIO)[None, :], priority[None, :]]
    near = ((plane + jnp.arange(experts, dtype=jnp.int32)) % experts)[:, None]
    chosen = [one == near for one in ids]
    chosen_any = (chosen[0] | chosen[1]).astype(jnp.bfloat16)
    token_index = jnp.arange(token_count, dtype=jnp.int32)
    before = (token_index[:, None] < token_index[None, :]).astype(jnp.bfloat16)
    rank = jnp.dot(chosen_any, before, preferred_element_type=jnp.float32).astype(jnp.int32)
    slots = jnp.arange(slot_count, dtype=jnp.int32)[:, None]
    place = [
        [(rank[k : k + 1] == slots) & chosen[j][k : k + 1] for k in range(experts)] for j in range(2)
    ]
    source = jnp.where(first_half, tokens, cotangent)

    spread = jnp.concatenate(
        [(place[0][k] | place[1][k]).astype(jnp.bfloat16) for k in range(experts)], axis=0
    )
    near_gate = sum(jnp.where(chosen[j], gates[j], 0.0) for j in range(2))
    slot_gate = jnp.concatenate(
        [
            jnp.sum(
                jnp.where(place[0][k] | place[1][k], near_gate[k : k + 1], 0.0), axis=1, keepdims=True
            )
            for k in range(experts)
        ],
        axis=0,
    )
    slot_gate = jnp.where(first_half, 1.0, slot_gate)
    spread, slot_gate, source = lax.optimization_barrier((spread, slot_gate, source))

    def rows_for(k, made):
        span = slice(k * slot_count, (k + 1) * slot_count)
        rows = jnp.dot(
            step(made, spread)[span], source, preferred_element_type=jnp.float32
        )
        return (rows * slot_gate[span]).astype(jnp.bfloat16)

    matrix_in = weight_in[0]
    matrix_out = weight_out[0]
    state = [dict(count=slot_count * len(group)) for group in groups]
    home = {}

    def spread_first(g, block):
        one = state[g]
        one["b00"] = block
        one["r1"] = send(block, along_first)
        one["r2"] = send(block, along_second)

    def spread_second(g, made):
        one = state[g]
        one["r1"] = step(made, one["r1"])
        one["b11"] = send(one["r1"], along_second)

    def gather_near(g, made):
        one = state[g]
        b00, r1, r2, b11 = step(made, one["b00"], one["r1"], one["r2"], one["b11"])
        b10 = jnp.where(core_zero, r2, r1)
        b01 = jnp.where(core_zero, r1, r2)
        one["near"] = jnp.concatenate(
            [
                jnp.where(first_half, b00, b01),
                jnp.where(first_half, b10, b11),
                jnp.where(first_half, b01, b00),
                jnp.where(first_half, b11, b10),
            ],
            axis=0,
        )
        one["far"] = send(one["near"], other_core)
        return [one["near"]]

    def expert_work(g, name, made):
        one = state[g]
        both = step(made, one[name])
        rows, grads = both[: 2 * one["count"]], both[2 * one["count"] :]
        hidden_pre = jnp.dot(rows, matrix_in, preferred_element_type=jnp.float32)
        activation, slope = gelu_parts(hidden_pre)
        activation = activation.astype(jnp.bfloat16)
        grad_act = lax.dot_general(
            grads, matrix_out, contract_last, preferred_element_type=jnp.float32
        )
        grad_pre = (grad_act * slope).astype(jnp.bfloat16)
        part_out = jnp.dot(activation, matrix_out, preferred_element_type=jnp.float32)
        part_dx = lax.dot_general(
            grad_pre, matrix_in, contract_last, preferred_element_type=jnp.float32
        )
        parts = (part_out.astype(jnp.bfloat16), part_dx.astype(jnp.bfloat16))
        one[name + "_saved"] = (rows, grads, activation, grad_pre)
        parts = jnp.concatenate(parts, axis=0)
        one[name + "_parts"] = send(parts, other_core) if name == "far" else parts
        return [parts]

    def reduce_first(g, made):
        one = state[g]
        count = one["count"]
        sums = add(*step(made, one["near_parts"], one["far_parts"]))
        sum_out, sum_dx = sums[: 2 * count], sums[2 * count :]
        own_sum = jnp.where(first_half, sum_out, sum_dx)
        other_sum = jnp.where(first_half, sum_dx, sum_out)
        a00, a10 = own_sum[:count], own_sum[count:]
        a01, a11 = other_sum[:count], other_sum[count:]
        away = jnp.concatenate([jnp.where(core_zero, a01, a10), a11], axis=0)
        one["a00"], one["rest"] = a00, jnp.where(core_zero, a10, a01)
        one["back"] = send(away, along_first)
        return [away]

    def reduce_second(g, made):
        one = state[g]
        one["back"], rest = step(made, one["back"], one["rest"])
        last = add(rest, one["back"][one["count"] :])
        one["last"] = send(last, along_second)
        return [last]

    def go_home(g, made):
        one = state[g]
        a00, back, last = step(made, one["a00"], one["back"], one["last"])
        done = add(a00, back[: one["count"]], last)
        for spot, k in enumerate(groups[g]):
            piece = done[spot * slot_count : (spot + 1) * slot_count]
            home[k] = piece if k == 0 else send(piece, planes_on(experts - k))
        return [done]

    arrived = {}
    made = []
    cards = [
        jnp.stack(
            [
                sum(
                    jnp.sum(jnp.where(place[j][k], keys[j].astype(jnp.float32) + 1.0, 0.0), axis=1)
                    for j in range(2)
                )
                for k in range(experts)
            ]
        )
        - 1.0
    ]
    cards = jnp.concatenate(cards, axis=0)[None, None]

    for entry in PLAN:
        name, g = entry.split()[0], int(entry.split()[1])
        if name == "Z":
            block = rows_for(g, made)
            arrived[g] = send(block, planes_on(g))
            made = [block]
        elif name == "D1" and g == 0:
            block = rows_for(0, made)
            spread_first(0, block)
            made = [block]
        elif name == "D1":
            parts = step(made, *[arrived[k] for k in groups[g]])
            spread_first(g, parts if len(groups[g]) == 1 else join(parts))
        elif name == "D2":
            spread_second(g, made)
        elif name == "SEL":
            made = gather_near(g, made)
        elif name == "CN":
            made = expert_work(g, "near", made)
        elif name == "CF":
            made = expert_work(g, "far", made)
        elif name == "R1":
            made = reduce_first(g, made)
        elif name == "R2":
            made = reduce_second(g, made)
        elif name == "H":
            made = go_home(g, made)
        elif name == "K":
            cards, got = step(made, cards, got) if g else (step(made, cards), None)
            if g:
                cards = jnp.concatenate([cards, got], axis=0 if g < 3 else 1)
            if g == 0:
                got = send(cards, planes_on(1))
            elif g == 1:
                got = send(cards, planes_on(2))
            else:
                got = send(cards, (other_row, other_core)[g - 2])
        elif name == "CUT":
            cards, got = step(made, cards, got)
            cards = jnp.concatenate([cards, got], axis=1)
            near_keys = jnp.stack(
                [
                    jnp.concatenate([cards[d, :, (r + d) % experts] for d in range(experts)], axis=0)
                    for r in range(experts)
                ]
            )
            levels = jnp.arange(2 * PRIO, dtype=jnp.float32)
            above = jnp.sum(
                (near_keys[:, :, None, :] >= levels[None, None, :, None]).astype(jnp.float32),
                axis=(1, 3),
            )
            near_cutoff = jnp.sum((above > capacity).astype(jnp.float32), axis=1)
            kept_rows = jnp.concatenate(
                [
                    (cards[k, 2 * far + other_y, k] >= near_cutoff[0]).astype(jnp.float32)
                    for group in groups
                    for far in range(2)
                    for other_y in range(2)
                    for k in group
                ]
            )[:, None] > 0.0
            made = [kept_rows]
        elif name in ("W1", "W2"):
            saved = [one[half + "_saved"] for one in state for half in ("near", "far")]
            rows, grads, act, pre = [jnp.concatenate(part, axis=0) for part in zip(*saved)]
            if name == "W1":
                pre = step(made, jnp.where(kept_rows, pre, 0))
                grad_in = lax.dot_general(
                    rows, pre, contract_first, preferred_element_type=jnp.float32
                ).astype(jnp.bfloat16)
                made = [grad_in]
            else:
                act = step(made, jnp.where(kept_rows, act, 0))
                grad_out = lax.dot_general(
                    act, grads, contract_first, preferred_element_type=jnp.float32
                ).astype(jnp.bfloat16)
                made = [grad_out]

    back_rows = jnp.concatenate([home[k] for k in range(experts)], axis=0)
    cotangent_columns = cotangent.T.astype(jnp.float32)
    mixed = 0.0
    gate_grads = []
    for j in range(2):
        token_cutoff = jnp.sum(
            chosen[j].astype(jnp.float32) * near_cutoff[:, None], axis=0, keepdims=True
        )
        kept = keys[j].astype(jnp.float32) >= token_cutoff
        picker = jnp.concatenate(
            [(place[j][k] & kept).astype(jnp.bfloat16) for k in range(experts)], axis=0
        )
        picked = lax.dot_general(
            back_rows, picker, contract_first, preferred_element_type=jnp.float32
        )
        mixed = mixed + picked * jnp.where(first_half, gates[j], 1.0)
        gate_grads.append(jnp.sum(picked * cotangent_columns, axis=0, keepdims=True))
    mixed = mixed.astype(jnp.bfloat16)
    gate_grad = jnp.concatenate(gate_grads, axis=0)
    terms, left = [], gate_grad
    for _ in range(3):
        term = lax.reduce_precision(left, exponent_bits=8, mantissa_bits=7)
        terms.append(term.astype(jnp.bfloat16))
        left = left - term
    spare = jnp.zeros((10, token_count), jnp.bfloat16)
    half = width // 2
    upper, lower = mixed[:half], mixed[half:]
    kept_part = jnp.where(first_half, upper, lower)
    got = lax.ppermute(
        jnp.concatenate([jnp.where(first_half, lower, upper)] + terms + [spare], axis=0),
        "rep",
        [(0, 1), (1, 0)],
    )
    got_part = got[:half]
    got_terms = got[half : half + 6].astype(jnp.float32)
    got_gate = got_terms[0:2] + got_terms[2:4] + got_terms[4:6]
    rows_half = token_count // 2
    return (
        jnp.where(first_half, kept_part, got_part).T,
        jnp.where(first_half, got_part, kept_part).T,
        jnp.where(first_half, gate_grad[:, :rows_half], got_gate[:, rows_half:]).T,
        grad_in[None],
        grad_out[None],
    )


def solution(mesh):
    placed = (
        P("dp", None),
        P("dp", None),
        P("dp"),
        P("dp", None),
        P("dp", None, "rep"),
        P("dp", "rep", None),
        P("dp", None),
    )
    body = plane_body if mesh.shape["rep"] == 2 and mesh.shape["dp"] == 4 * HBLK else general_body
    return jax.shard_map(
        body,
        mesh=mesh,
        in_specs=placed,
        out_specs=(
            P("dp", "rep"),
            P("dp", "rep"),
            P(("dp", "rep"), None),
            P("dp", None, "rep"),
            P("dp", "rep", None),
        ),
        check_vma=False,
    )
```

```python
import functools
import math

import jax
import jax.numpy as jnp
from jax import lax
from jax.experimental import pallas as pl
from jax.experimental.pallas import tpu as pltpu
from jax.sharding import PartitionSpec as P

HBLK = 4
PRIO = 64


def gelu_parts(hidden_pre):
    normal_cdf = 0.5 * (1.0 + jax.scipy.special.erf(hidden_pre * (1.0 / math.sqrt(2.0))))
    density = jnp.exp(-0.5 * hidden_pre * hidden_pre) * (1.0 / math.sqrt(2.0 * math.pi))
    return (hidden_pre * normal_cdf, normal_cdf + hidden_pre * density)


def general_body(tokens, expert_ids, priority, gate_values, weight_in, weight_out, cotangent):
    token_count = tokens.shape[0]
    dp_count = lax.axis_size("dp")
    experts = dp_count // HBLK
    slot_count = min(token_count, 2 * token_count // experts + max(1, token_count // (4 * experts)))
    capacity = 2 * token_count * dp_count // experts
    row_total = dp_count * slot_count
    contract_first = (((0,), (0,)), ((), ()))
    contract_last = (((1,), (1,)), ((), ()))
    priority_key = (
        priority[:, None] + PRIO * (1 - jnp.arange(2, dtype=jnp.int32))[None, :]
    ).reshape(-1)
    flat_expert = expert_ids.reshape(-1)
    expert_hot = (flat_expert[:, None] == jnp.arange(experts, dtype=jnp.int32)[None, :]).astype(
        jnp.int32
    )
    key_hot = (priority_key[:, None] == jnp.arange(2 * PRIO, dtype=jnp.int32)[None, :]).astype(
        jnp.int32
    )
    local_counts = jnp.dot(expert_hot.T, key_hot, preferred_element_type=jnp.int32)
    counts = lax.psum(local_counts, "dp")
    above_count = jnp.cumsum(counts[:, ::-1], axis=1)[:, ::-1]
    cutoff_key = jnp.sum((above_count > capacity).astype(jnp.int32), axis=1)
    kept_mask = priority_key >= jnp.sum(expert_hot * cutoff_key[None, :], axis=1)
    before_count = jnp.cumsum(expert_hot, axis=0) - expert_hot
    slot_index = jnp.sum(expert_hot * before_count, axis=1)
    slot_hot = (slot_index[:, None] == jnp.arange(slot_count, dtype=jnp.int32)[None, :]).astype(
        jnp.int32
    )
    place_map = (
        expert_hot[:, :, None] * slot_hot[:, None, :] * kept_mask.astype(jnp.int32)[:, None, None]
    )
    place_map = place_map.astype(jnp.bfloat16).reshape(2 * token_count, experts * slot_count)
    token_place = jnp.sum(place_map.reshape(token_count, 2, experts * slot_count), axis=1)
    grad_source = (
        gate_values.reshape(-1)[:, None] * jnp.repeat(cotangent, 2, axis=0).astype(jnp.float32)
    ).astype(jnp.bfloat16)
    wide_index = jnp.arange(row_total, dtype=jnp.int32)
    wide_index = wide_index // (HBLK * slot_count) * slot_count + wide_index % slot_count

    def widen(matrix):
        return jnp.take(matrix, wide_index, axis=0)

    send_rows = lax.dot_general(
        token_place, tokens, contract_first, preferred_element_type=jnp.float32
    ).astype(jnp.bfloat16)
    send_grads = lax.dot_general(
        place_map, grad_source, contract_first, preferred_element_type=jnp.float32
    ).astype(jnp.bfloat16)
    rows, grad_rows = (
        lax.all_to_all(widen(send_rows), "dp", split_axis=0, concat_axis=0, tiled=True),
        lax.all_to_all(widen(send_grads), "dp", split_axis=0, concat_axis=0, tiled=True),
    )
    matrix_in = weight_in[0]
    matrix_out = weight_out[0]
    hidden_pre = jnp.dot(rows, matrix_in, preferred_element_type=jnp.float32)
    activation, slope = gelu_parts(hidden_pre)
    activation = activation.astype(jnp.bfloat16)
    partial_out = jnp.dot(activation, matrix_out, preferred_element_type=jnp.float32).astype(
        jnp.bfloat16
    )
    grad_act = lax.dot_general(
        grad_rows, matrix_out, contract_last, preferred_element_type=jnp.float32
    )
    grad_pre = (grad_act * slope).astype(jnp.bfloat16)
    grad_in = lax.dot_general(
        rows, grad_pre, contract_first, preferred_element_type=jnp.float32
    ).astype(jnp.bfloat16)
    grad_out = lax.dot_general(
        activation, grad_rows, contract_first, preferred_element_type=jnp.float32
    ).astype(jnp.bfloat16)
    partial_dx = lax.dot_general(
        grad_pre, matrix_in, contract_last, preferred_element_type=jnp.float32
    ).astype(jnp.bfloat16)
    block_range = jnp.arange(HBLK, dtype=jnp.int32)
    pick_index = (
        (flat_expert[:, None] * HBLK + block_range[None, :]) * slot_count + slot_index[:, None]
    ).reshape(-1)

    def pick_rows(returned):
        width = returned.shape[-1]
        picked = jnp.take(returned, pick_index, axis=0)
        summed = jnp.sum(picked.reshape(2 * token_count, HBLK, width).astype(jnp.float32), axis=1)
        return jnp.where(kept_mask[:, None], summed, 0.0).reshape(token_count, 2, width)

    back_out, back_dx = (
        lax.all_to_all(partial_out, "dp", split_axis=0, concat_axis=0, tiled=True),
        lax.all_to_all(partial_dx, "dp", split_axis=0, concat_axis=0, tiled=True),
    )
    out_rows = pick_rows(back_out)
    dx_rows = pick_rows(back_dx)
    mixed = jnp.sum(gate_values[:, :, None] * out_rows, axis=1)
    token_grad = jnp.sum(dx_rows, axis=1)
    gate_grad = jnp.sum(cotangent.astype(jnp.float32)[:, None, :] * out_rows, axis=2)
    gate_grad = lax.psum_scatter(gate_grad, "rep", scatter_dimension=0, tiled=True)
    mixed, token_grad = (
        lax.psum_scatter(mixed.astype(jnp.bfloat16), "rep", scatter_dimension=1, tiled=True).astype(
            jnp.float32
        ),
        lax.psum_scatter(
            token_grad.astype(jnp.bfloat16), "rep", scatter_dimension=1, tiled=True
        ).astype(jnp.float32),
    )
    return (
        mixed.astype(jnp.bfloat16),
        token_grad.astype(jnp.bfloat16),
        gate_grad,
        grad_in[None],
        grad_out[None],
    )


GROUPS = ((0,), (1,), (3,), (2,))
MIB = 1024 * 1024
WLIM = 56
PLAN = (
    "Z 1",
    "D1 0",
    "Z 3",
    "Z 2",
    "D2 0",
    "D1 1",
    "SEL 0",
    "D2 1",
    "D1 2",
    "SEL 1",
    "D2 2",
    "D1 3",
    "D2 3",
    "SEL 2",
    "SEL 3",
    "E 1",
    "E 0 E1",
    "E 2 E0",
    "R1 1 E2",
    "E 3 R11",
    "CUT 0",
    "R1 2 E3",
    "R2 1 R12",
    "R1 3 R21",
    "R2 2 R13",
    "H 1 R22",
    "R1 0 H1",
    "R2 3 R10",
    "H 2 R23",
    "R2 0 H2",
    "H 3 R20",
    "W 0 H3",
    "H 0 W0",
)


def expert_kernel(near, far, matrix_in, matrix_out, near_parts, far_parts, act, pre):
    half = near.shape[0] // 2
    rows = jnp.concatenate([near[:half], far[:half]], axis=0)
    grads = jnp.concatenate([near[half:], far[half:]], axis=0)
    hidden_pre = jnp.dot(rows, matrix_in[...], preferred_element_type=jnp.float32)
    activation, slope = gelu_parts(hidden_pre)
    grad_act = lax.dot_general(
        grads, matrix_out[...], (((1,), (1,)), ((), ())), preferred_element_type=jnp.float32
    )
    act[...] = activation.astype(jnp.bfloat16)
    pre[...] = (grad_act * slope).astype(jnp.bfloat16)
    out = jnp.dot(act[...], matrix_out[...], preferred_element_type=jnp.float32)
    near_parts[:half] = out[:half].astype(jnp.bfloat16)
    far_parts[:half] = out[half:].astype(jnp.bfloat16)
    back = lax.dot_general(
        pre[...], matrix_in[...], (((1,), (1,)), ((), ())), preferred_element_type=jnp.float32
    )
    near_parts[half:] = back[:half].astype(jnp.bfloat16)
    far_parts[half:] = back[half:].astype(jnp.bfloat16)


def expert_call(near, far, matrix_in, matrix_out):
    rows, width = near.shape
    hidden = matrix_in.shape[1]
    vmem = pl.BlockSpec(memory_space=pltpu.VMEM)
    return pl.pallas_call(
        expert_kernel,
        out_shape=(
            jax.ShapeDtypeStruct((rows, width), jnp.bfloat16),
            jax.ShapeDtypeStruct((rows, width), jnp.bfloat16),
            jax.ShapeDtypeStruct((rows, hidden), jnp.bfloat16),
            jax.ShapeDtypeStruct((rows, hidden), jnp.bfloat16),
        ),
        in_specs=[vmem] * 4,
        out_specs=(vmem,) * 4,
        compiler_params=pltpu.CompilerParams(vmem_limit_bytes=16 * MIB),
        cost_estimate=pl.CostEstimate(flops=0, bytes_accessed=0, transcendentals=0),
    )(near, far, matrix_in, matrix_out)


def start_kernel(experts, ids_at, priority_at, gates_at, tokens_at, cotangent_at, places, *rest):
    blocks, (ids, priority, gates, source, sems) = rest[:experts], rest[experts:]
    slot_count, block_rows = places.shape[2], blocks[0].shape[0]
    token_count = source.shape[0]
    place_dp = lax.axis_index("dp")
    first_half = lax.axis_index("rep") == 0
    small = [
        pltpu.make_async_copy(whole, held, sems.at[i])
        for i, (whole, held) in enumerate(((ids_at, ids), (priority_at, priority), (gates_at, gates)))
    ]
    for copy in small:
        copy.start()

    @pl.when(first_half)
    def _():
        pltpu.make_async_copy(tokens_at, source, sems.at[3]).start()

    @pl.when(jnp.logical_not(first_half))
    def _():
        pltpu.make_async_copy(cotangent_at, source, sems.at[3]).start()

    for copy in small:
        copy.wait()
    row = lax.broadcasted_iota(jnp.int32, (experts, 1), 0)
    near = lax.rem(place_dp // HBLK + row, experts)
    chosen = [ids[j : j + 1] == near for j in range(2)]
    chosen_any = chosen[0] | chosen[1]
    early = lax.broadcasted_iota(jnp.int32, (token_count, token_count), 0)
    late = lax.broadcasted_iota(jnp.int32, (token_count, token_count), 1)
    rank = jnp.dot(
        chosen_any.astype(jnp.bfloat16),
        (early < late).astype(jnp.bfloat16),
        preferred_element_type=jnp.float32,
    ).astype(jnp.int32)
    rank = jnp.where(chosen_any, rank, -1)
    near_gate = jnp.where(chosen[0], gates[0:1], gates[1:2])
    slots = lax.broadcasted_iota(jnp.int32, (slot_count, token_count), 0)
    pltpu.make_async_copy(tokens_at, source, sems.at[3]).wait()
    for k in range(experts):
        spread = rank[k : k + 1] == slots
        rows = jnp.dot(spread.astype(jnp.bfloat16), source[...], preferred_element_type=jnp.float32)
        slot_gate = jnp.sum(jnp.where(spread, near_gate[k : k + 1], 0.0), axis=1, keepdims=True)
        key = 1 + priority[...] + jnp.where(chosen[0][k : k + 1], PRIO, 0)
        slot_key = lax.dot_general(
            key.astype(jnp.bfloat16),
            spread.astype(jnp.bfloat16),
            (((1,), (1,)), ((), ())),
            preferred_element_type=jnp.float32,
        )
        whole = (rows * jnp.where(first_half, 1.0, slot_gate)).astype(jnp.bfloat16)
        spare = jnp.zeros((block_rows - slot_count, rows.shape[1]), jnp.bfloat16)
        blocks[k][...] = jnp.concatenate([whole, spare], axis=0)
        blocks[k][slot_count : slot_count + 1, :slot_count] = slot_key.astype(jnp.bfloat16)
        for j in range(2):
            places[j, k] = (spread & chosen[j][k : k + 1]).astype(jnp.bfloat16)


def start_call(ids, priority, gates, tokens, cotangent, experts, slot_count):
    token_count, width = tokens.shape
    block_rows = (slot_count + 1 + 15) // 16 * 16
    vmem = pl.BlockSpec(memory_space=pltpu.VMEM)
    return pl.pallas_call(
        functools.partial(start_kernel, experts),
        out_shape=(
            jax.ShapeDtypeStruct((2, experts, slot_count, token_count), jnp.bfloat16),
        )
        + (jax.ShapeDtypeStruct((block_rows, width), jnp.bfloat16),) * experts,
        in_specs=[pl.BlockSpec(memory_space=pl.ANY)] * 5,
        out_specs=(vmem,) * (1 + experts),
        scratch_shapes=[
            pltpu.VMEM(ids.shape, jnp.int32),
            pltpu.VMEM(priority.shape, jnp.int32),
            pltpu.VMEM(gates.shape, jnp.float32),
            pltpu.VMEM(tokens.shape, jnp.bfloat16),
            pltpu.SemaphoreType.DMA((4,)),
        ],
        compiler_params=pltpu.CompilerParams(vmem_limit_bytes=56 * MIB),
        cost_estimate=pl.CostEstimate(flops=0, bytes_accessed=0, transcendentals=0),
    )(ids, priority, gates, tokens, cotangent)


def cut_kernel(slot_count, block_rows, capacity, *refs):
    group_count = len(refs) // 2 - 2
    pieces, (kept, mine, keys, sems) = refs[: 2 * group_count], refs[2 * group_count :]
    copies, at = [], 0
    for piece in pieces:
        for block in range(piece.shape[0] // 2 // block_rows):
            last = pl.ds((block + 1) * block_rows - 16, 16)
            copies.append(
                pltpu.make_async_copy(piece.at[last, pl.ds(0, 128)], keys.at[at], sems.at[at])
            )
            at += 1
    for copy in copies:
        copy.start()
    for copy in copies:
        copy.wait()
    row = slot_count - (block_rows - 16)
    rows = [keys[i, row : row + 1, :slot_count].astype(jnp.float32) - 1.0 for i in range(at)]
    levels = lax.broadcasted_iota(jnp.int32, (2 * PRIO, 1), 0).astype(jnp.float32)
    above = sum((one >= levels).astype(jnp.float32) for one in rows)
    above = jnp.sum(above, axis=1, keepdims=True)
    cutoff = jnp.sum((above > capacity).astype(jnp.float32), axis=0, keepdims=True)
    diagonal = lax.broadcasted_iota(
        jnp.int32, (block_rows, slot_count), 0
    ) == lax.broadcasted_iota(jnp.int32, (block_rows, slot_count), 1)
    for i, one in enumerate(rows):
        inside = jnp.where(diagonal & (one >= cutoff), 1.0, 0.0)
        column = jnp.sum(inside, axis=1, keepdims=True)
        kept[i * block_rows : (i + 1) * block_rows] = jnp.broadcast_to(column, (block_rows, 128)).astype(jnp.bfloat16)
        if i % (at // group_count) == 0:
            g = i // (at // group_count)
            mine[g] = jnp.broadcast_to(column, (block_rows, 128))


def cut_call(pieces, slot_count, block_rows, capacity):
    total = sum(piece.shape[0] // 2 for piece in pieces)
    vmem = pl.BlockSpec(memory_space=pltpu.VMEM)
    return pl.pallas_call(
        functools.partial(cut_kernel, slot_count, block_rows, capacity),
        out_shape=(
            jax.ShapeDtypeStruct((total, 128), jnp.bfloat16),
            jax.ShapeDtypeStruct((len(pieces) // 2, block_rows, 128), jnp.float32),
        ),
        in_specs=[pl.BlockSpec(memory_space=pl.ANY)] * len(pieces),
        out_specs=(vmem,) * 2,
        scratch_shapes=[
            pltpu.VMEM((total // block_rows, 16, 128), jnp.bfloat16),
            pltpu.SemaphoreType.DMA((total // block_rows,)),
        ],
        compiler_params=pltpu.CompilerParams(vmem_limit_bytes=8 * MIB),
        cost_estimate=pl.CostEstimate(flops=0, bytes_accessed=0, transcendentals=0),
    )(*pieces)


def weight_kernel(kept, *refs):
    group_count = (len(refs) - 4) // 6
    parts, hiddens = refs[: 4 * group_count], refs[4 * group_count : 6 * group_count]
    grad_in, grad_out, act, pre = refs[6 * group_count :]

    @pl.when(pl.program_id(0) == 0)
    def _():
        keep = kept[:, 0:1]
        act[...] = jnp.concatenate([one[...] for one in hiddens[::2]], axis=0) * keep
        pre[...] = jnp.concatenate([one[...] for one in hiddens[1::2]], axis=0) * keep

    contract_first = (((0,), (0,)), ((), ()))
    rows = jnp.concatenate([one[...] for one in parts[::2]], axis=0)
    grads = jnp.concatenate([one[...] for one in parts[1::2]], axis=0)
    grad_in[...] = lax.dot_general(
        rows, pre[...], contract_first, preferred_element_type=jnp.float32
    ).astype(jnp.bfloat16)
    grad_out[...] = lax.dot_general(
        act[...], grads, contract_first, preferred_element_type=jnp.float32
    ).astype(jnp.bfloat16)


def weight_call(kept, saved):
    width, hidden = saved[0][0].shape[1], saved[0][2].shape[1]
    all_rows = sum(one[2].shape[0] for one in saved)
    tile = 256
    operands, specs = [], []
    for near, far, _, _ in saved:
        for whole in (near, far):
            for kind in range(2):
                operands.append(whole)
                specs.append(
                    pl.BlockSpec((whole.shape[0] // 2, tile), functools.partial(lambda kind, j: (kind, j), kind))
                )
    for _, _, act, pre in saved:
        for whole in (act, pre):
            operands.append(whole)
            specs.append(pl.BlockSpec(whole.shape, lambda j: (0, 0)))
    return pl.pallas_call(
        weight_kernel,
        grid=(pl.cdiv(width, tile),),
        out_shape=(
            jax.ShapeDtypeStruct((width, hidden), jnp.bfloat16),
            jax.ShapeDtypeStruct((hidden, width), jnp.bfloat16),
        ),
        in_specs=[pl.BlockSpec(kept.shape, lambda j: (0, 0))] + specs,
        out_specs=(
            pl.BlockSpec((tile, hidden), lambda j: (j, 0)),
            pl.BlockSpec((hidden, tile), lambda j: (0, j)),
        ),
        scratch_shapes=[pltpu.VMEM((all_rows, hidden), jnp.bfloat16)] * 2,
        compiler_params=pltpu.CompilerParams(vmem_limit_bytes=WLIM * MIB),
        cost_estimate=pl.CostEstimate(flops=0, bytes_accessed=0, transcendentals=0),
    )(kept, *operands)


def token_kernel(gates, places, cotangent, *refs):
    homes, (away, stay, gate_grad) = refs[:-3], refs[-3:]
    first_half = lax.axis_index("rep") == 0
    token_count, width = cotangent.shape
    half = width // 2
    diagonal = lax.broadcasted_iota(
        jnp.int32, (token_count, token_count), 0
    ) == lax.broadcasted_iota(jnp.int32, (token_count, token_count), 1)
    back = jnp.concatenate([one[...] for one in homes], axis=0)
    mixed, sums = 0.0, []
    for j in range(2):
        picker = jnp.concatenate([places[j, k] for k in range(len(homes))], axis=0)
        picked = lax.dot_general(
            picker, back, (((0,), (0,)), ((), ())), preferred_element_type=jnp.float32
        )
        gate = jnp.sum(jnp.where(diagonal, gates[j : j + 1], 0.0), axis=1, keepdims=True)
        mixed = mixed + picked * jnp.where(first_half, gate, 1.0)
        inner = jnp.sum(picked * cotangent[...].astype(jnp.float32), axis=1, keepdims=True)
        sums.append(jnp.sum(jnp.where(diagonal, inner, 0.0), axis=0, keepdims=True))
    mixed = mixed.astype(jnp.bfloat16).T
    upper, lower = mixed[:half], mixed[half:]
    away[:half] = jnp.where(first_half, lower, upper)
    stay[...] = jnp.where(first_half, upper, lower)
    left = jnp.concatenate(sums, axis=0)
    gate_grad[...] = left
    terms = []
    for _ in range(3):
        terms.append(left.astype(jnp.bfloat16))
        left = left - terms[-1].astype(jnp.float32)
    terms.append(jnp.zeros((away.shape[0] - half - 6, token_count), jnp.bfloat16))
    away[half:] = jnp.concatenate(terms, axis=0)


def token_call(gates, places, cotangent, homes):
    token_count, width = cotangent.shape
    vmem = pl.BlockSpec(memory_space=pltpu.VMEM)
    return pl.pallas_call(
        token_kernel,
        out_shape=(
            jax.ShapeDtypeStruct((width // 2 + 16, token_count), jnp.bfloat16),
            jax.ShapeDtypeStruct((width // 2, token_count), jnp.bfloat16),
            jax.ShapeDtypeStruct((2, token_count), jnp.float32),
        ),
        in_specs=[vmem] * (3 + len(homes)),
        out_specs=(vmem,) * 3,
        compiler_params=pltpu.CompilerParams(vmem_limit_bytes=16 * MIB),
        cost_estimate=pl.CostEstimate(flops=0, bytes_accessed=0, transcendentals=0),
    )(gates, places, cotangent, *homes)


def end_kernel(stay, got, gate_grad, output, grad_tokens, grad_gates):
    first_half = lax.axis_index("rep") == 0
    half = stay.shape[0]
    mine, theirs = stay[...], got[:half]
    output[...] = jnp.where(first_half, mine, theirs)
    grad_tokens[...] = jnp.where(first_half, theirs, mine)
    terms = got[half:].astype(jnp.float32)
    got_gate = terms[0:2] + terms[2:4] + terms[4:6]
    rows_half = gate_grad.shape[1] // 2
    grad_gates[...] = jnp.where(first_half, gate_grad[:, :rows_half], got_gate[:, rows_half:])


def end_call(stay, got, gate_grad):
    half, token_count = stay.shape
    vmem = pl.BlockSpec(memory_space=pltpu.VMEM)
    return pl.pallas_call(
        end_kernel,
        out_shape=(
            jax.ShapeDtypeStruct((half, token_count), jnp.bfloat16),
            jax.ShapeDtypeStruct((half, token_count), jnp.bfloat16),
            jax.ShapeDtypeStruct((2, token_count // 2), jnp.float32),
        ),
        in_specs=[vmem] * 3,
        out_specs=(vmem,) * 3,
        compiler_params=pltpu.CompilerParams(vmem_limit_bytes=16 * MIB),
    )(stay, got, gate_grad)


def plane_body(tokens, expert_ids, priority, gate_values, weight_in, weight_out, cotangent):
    token_count, width = tokens.shape
    dp_count = lax.axis_size("dp")
    experts = dp_count // HBLK
    slot_count = min(token_count, 2 * token_count // experts + max(1, token_count // (4 * experts)))
    capacity = 2 * token_count * dp_count // experts
    contract_first = (((0,), (0,)), ((), ()))
    contract_last = (((1,), (1,)), ((), ()))
    place_dp = lax.axis_index("dp")
    first_half = lax.axis_index("rep") == 0
    plane, quarter = place_dp // HBLK, place_dp % HBLK
    core_zero = quarter % 2 == 0
    groups = GROUPS

    def permutation(move):
        pairs = []
        for z in range(experts):
            for q in range(HBLK):
                for x in range(2):
                    z2, q2, x2 = move(z, q, x)
                    pairs.append((2 * (z * HBLK + q) + x, 2 * (z2 * HBLK + q2) + x2))
        return pairs

    def send(array, move):
        return lax.ppermute(array, ("dp", "rep"), permutation(move))

    def along_first(z, q, x):
        return (z, q, 1 - x) if q % 2 == 0 else (z, q ^ 2, x)

    def along_second(z, q, x):
        return (z, q ^ 2, x) if q % 2 == 0 else (z, q, 1 - x)

    def other_core(z, q, x):
        return (z, q ^ 1, x)

    def other_row(z, q, x):
        return (z, q ^ 2, x)

    def planes_on(k):
        return lambda z, q, x: ((z + k) % experts, q, x)

    def add(*terms):
        return sum(term.astype(jnp.float32) for term in terms).astype(jnp.bfloat16)

    def step(made, *values):
        if made:
            values, _ = lax.optimization_barrier((values, made))
        return values if len(values) > 1 else values[0]

    def join(parts):
        return parts[0] if len(parts) == 1 else jnp.concatenate(parts, axis=0)

    ids, gates = expert_ids.T, gate_values.T
    places, *blocks = start_call(
        ids, priority[None, :], gates, tokens, cotangent, experts, slot_count
    )
    block_rows = blocks[0].shape[0]

    matrix_in = weight_in[0]
    matrix_out = weight_out[0]
    state = [{} for _ in groups]
    home = {}

    def spread_first(g, block):
        one = state[g]
        one["b00"] = block
        one["r1"] = send(block, along_first)
        one["r2"] = send(block, along_second)
        return [one["r1"]]

    def spread_second(g, made):
        one = state[g]
        one["r1"] = step(made, one["r1"])
        one["b11"] = send(one["r1"], along_second)
        return [one["b11"]]

    def gather_near(g, made):
        one = state[g]
        b00, r1, r2, b11 = step(made, one["b00"], one["r1"], one["r2"], one["b11"])
        b10 = jnp.where(core_zero, r2, r1)
        b01 = jnp.where(core_zero, r1, r2)
        one["near"] = jnp.concatenate(
            [
                jnp.where(first_half, b00, b01),
                jnp.where(first_half, b10, b11),
                jnp.where(first_half, b01, b00),
                jnp.where(first_half, b11, b10),
            ],
            axis=0,
        )
        one["far"] = send(one["near"], other_core)
        return [one["near"]]

    def expert_work(g, made):
        one = state[g]
        near_rows, far_rows = step(made, one["near"], one["far"])
        near_parts, far_parts, act, pre = expert_call(near_rows, far_rows, matrix_in, matrix_out)
        one["saved"] = (near_rows, far_rows, act, pre)
        one["near_parts"], one["far_parts"] = near_parts, send(far_parts, other_core)
        return [act]

    def reduce_first(g, made):
        one = state[g]
        sums = add(*step(made, one["near_parts"], one["far_parts"]))
        out0, out1, dx0, dx1 = [
            sums[at * block_rows : at * block_rows + slot_count] for at in range(4)
        ]
        a00, a10 = jnp.where(first_half, out0, dx0), jnp.where(first_half, out1, dx1)
        a01, a11 = jnp.where(first_half, dx0, out0), jnp.where(first_half, dx1, out1)
        away = jnp.concatenate([jnp.where(core_zero, a01, a10), a11], axis=0)
        one["a00"], one["rest"] = a00, jnp.where(core_zero, a10, a01)
        one["back"] = send(away, along_first)
        return [away]

    def reduce_second(g, made):
        one = state[g]
        one["back"], rest = step(made, one["back"], one["rest"])
        last = add(rest, one["back"][slot_count:])
        one["last"] = send(last, along_second)
        return [last]

    def go_home(g, made):
        one = state[g]
        a00, back, last = step(made, one["a00"], one["back"], one["last"])
        (k,) = groups[g]
        done = (
            (a00.astype(jnp.float32) + back[:slot_count].astype(jnp.float32) + last.astype(jnp.float32))
            * mine[g, :slot_count, 0:1]
        ).astype(jnp.bfloat16)
        home[k] = done if k == 0 else send(done, planes_on(experts - k))
        return [done]

    arrived, events = {}, {}
    for entry in PLAN:
        name, g, *after = entry.split()
        g = int(g)
        made = [value for one in after for value in events[one]]
        if name == "Z":
            arrived[g] = send(step(made, blocks[g]), planes_on(g))
            here = [arrived[g]]
        elif name == "D1":
            (k,) = groups[g]
            here = spread_first(g, step(made, arrived[k] if k else blocks[0]))
        elif name == "D2":
            here = spread_second(g, made)
        elif name == "SEL":
            here = gather_near(g, made)
        elif name == "E":
            here = expert_work(g, made)
        elif name == "CUT":
            pieces = [piece for one in state for piece in one["saved"][:2]]
            kept, mine = cut_call(step(made, *pieces), slot_count, block_rows, capacity)
            here = [mine]
        elif name == "R1":
            here = reduce_first(g, made)
        elif name == "R2":
            here = reduce_second(g, made)
        elif name == "H":
            here = go_home(g, made)
        elif name == "W":
            saved = [step(made, *one["saved"]) for one in state]
            grad_in, grad_out = weight_call(kept, saved)
            here = [grad_in]
        events[name + str(g)] = here

    away, stay, gate_grad = token_call(gates, places, cotangent, [home[k] for k in range(experts)])
    got = lax.ppermute(away, "rep", [(0, 1), (1, 0)])
    output, grad_tokens, grad_gates = end_call(stay, got, gate_grad)
    return output.T, grad_tokens.T, grad_gates.T, grad_in[None], grad_out[None]


def solution(mesh):
    placed = (
        P("dp", None),
        P("dp", None),
        P("dp"),
        P("dp", None),
        P("dp", None, "rep"),
        P("dp", "rep", None),
        P("dp", None),
    )
    body = plane_body if mesh.shape["rep"] == 2 and mesh.shape["dp"] == 4 * HBLK else general_body
    return jax.shard_map(
        body,
        mesh=mesh,
        in_specs=placed,
        out_specs=(
            P("dp", "rep"),
            P("dp", "rep"),
            P(("dp", "rep"), None),
            P("dp", None, "rep"),
            P("dp", "rep", None),
        ),
        check_vma=False,
    )
```

```python
import functools
import math

import jax
import jax.numpy as jnp
from jax import lax
from jax.experimental import pallas as pl
from jax.experimental.pallas import tpu as pltpu
from jax.sharding import PartitionSpec as P

HBLK = 4
PRIO = 64


def gelu_parts(hidden_pre):
    normal_cdf = 0.5 * (1.0 + jax.scipy.special.erf(hidden_pre * (1.0 / math.sqrt(2.0))))
    density = jnp.exp(-0.5 * hidden_pre * hidden_pre) * (1.0 / math.sqrt(2.0 * math.pi))
    return (hidden_pre * normal_cdf, normal_cdf + hidden_pre * density)


def general_body(tokens, expert_ids, priority, gate_values, weight_in, weight_out, cotangent):
    token_count = tokens.shape[0]
    dp_count = lax.axis_size("dp")
    experts = dp_count // HBLK
    slot_count = min(token_count, 2 * token_count // experts + max(1, token_count // (4 * experts)))
    capacity = 2 * token_count * dp_count // experts
    row_total = dp_count * slot_count
    contract_first = (((0,), (0,)), ((), ()))
    contract_last = (((1,), (1,)), ((), ()))
    priority_key = (
        priority[:, None] + PRIO * (1 - jnp.arange(2, dtype=jnp.int32))[None, :]
    ).reshape(-1)
    flat_expert = expert_ids.reshape(-1)
    expert_hot = (flat_expert[:, None] == jnp.arange(experts, dtype=jnp.int32)[None, :]).astype(
        jnp.int32
    )
    key_hot = (priority_key[:, None] == jnp.arange(2 * PRIO, dtype=jnp.int32)[None, :]).astype(
        jnp.int32
    )
    local_counts = jnp.dot(expert_hot.T, key_hot, preferred_element_type=jnp.int32)
    counts = lax.psum(local_counts, "dp")
    above_count = jnp.cumsum(counts[:, ::-1], axis=1)[:, ::-1]
    cutoff_key = jnp.sum((above_count > capacity).astype(jnp.int32), axis=1)
    kept_mask = priority_key >= jnp.sum(expert_hot * cutoff_key[None, :], axis=1)
    before_count = jnp.cumsum(expert_hot, axis=0) - expert_hot
    slot_index = jnp.sum(expert_hot * before_count, axis=1)
    slot_hot = (slot_index[:, None] == jnp.arange(slot_count, dtype=jnp.int32)[None, :]).astype(
        jnp.int32
    )
    place_map = (
        expert_hot[:, :, None] * slot_hot[:, None, :] * kept_mask.astype(jnp.int32)[:, None, None]
    )
    place_map = place_map.astype(jnp.bfloat16).reshape(2 * token_count, experts * slot_count)
    token_place = jnp.sum(place_map.reshape(token_count, 2, experts * slot_count), axis=1)
    grad_source = (
        gate_values.reshape(-1)[:, None] * jnp.repeat(cotangent, 2, axis=0).astype(jnp.float32)
    ).astype(jnp.bfloat16)
    wide_index = jnp.arange(row_total, dtype=jnp.int32)
    wide_index = wide_index // (HBLK * slot_count) * slot_count + wide_index % slot_count

    def widen(matrix):
        return jnp.take(matrix, wide_index, axis=0)

    send_rows = lax.dot_general(
        token_place, tokens, contract_first, preferred_element_type=jnp.float32
    ).astype(jnp.bfloat16)
    send_grads = lax.dot_general(
        place_map, grad_source, contract_first, preferred_element_type=jnp.float32
    ).astype(jnp.bfloat16)
    rows, grad_rows = (
        lax.all_to_all(widen(send_rows), "dp", split_axis=0, concat_axis=0, tiled=True),
        lax.all_to_all(widen(send_grads), "dp", split_axis=0, concat_axis=0, tiled=True),
    )
    matrix_in = weight_in[0]
    matrix_out = weight_out[0]
    hidden_pre = jnp.dot(rows, matrix_in, preferred_element_type=jnp.float32)
    activation, slope = gelu_parts(hidden_pre)
    activation = activation.astype(jnp.bfloat16)
    partial_out = jnp.dot(activation, matrix_out, preferred_element_type=jnp.float32).astype(
        jnp.bfloat16
    )
    grad_act = lax.dot_general(
        grad_rows, matrix_out, contract_last, preferred_element_type=jnp.float32
    )
    grad_pre = (grad_act * slope).astype(jnp.bfloat16)
    grad_in = lax.dot_general(
        rows, grad_pre, contract_first, preferred_element_type=jnp.float32
    ).astype(jnp.bfloat16)
    grad_out = lax.dot_general(
        activation, grad_rows, contract_first, preferred_element_type=jnp.float32
    ).astype(jnp.bfloat16)
    partial_dx = lax.dot_general(
        grad_pre, matrix_in, contract_last, preferred_element_type=jnp.float32
    ).astype(jnp.bfloat16)
    block_range = jnp.arange(HBLK, dtype=jnp.int32)
    pick_index = (
        (flat_expert[:, None] * HBLK + block_range[None, :]) * slot_count + slot_index[:, None]
    ).reshape(-1)

    def pick_rows(returned):
        width = returned.shape[-1]
        picked = jnp.take(returned, pick_index, axis=0)
        summed = jnp.sum(picked.reshape(2 * token_count, HBLK, width).astype(jnp.float32), axis=1)
        return jnp.where(kept_mask[:, None], summed, 0.0).reshape(token_count, 2, width)

    back_out, back_dx = (
        lax.all_to_all(partial_out, "dp", split_axis=0, concat_axis=0, tiled=True),
        lax.all_to_all(partial_dx, "dp", split_axis=0, concat_axis=0, tiled=True),
    )
    out_rows = pick_rows(back_out)
    dx_rows = pick_rows(back_dx)
    mixed = jnp.sum(gate_values[:, :, None] * out_rows, axis=1)
    token_grad = jnp.sum(dx_rows, axis=1)
    gate_grad = jnp.sum(cotangent.astype(jnp.float32)[:, None, :] * out_rows, axis=2)
    gate_grad = lax.psum_scatter(gate_grad, "rep", scatter_dimension=0, tiled=True)
    mixed, token_grad = (
        lax.psum_scatter(mixed.astype(jnp.bfloat16), "rep", scatter_dimension=1, tiled=True).astype(
            jnp.float32
        ),
        lax.psum_scatter(
            token_grad.astype(jnp.bfloat16), "rep", scatter_dimension=1, tiled=True
        ).astype(jnp.float32),
    )
    return (
        mixed.astype(jnp.bfloat16),
        token_grad.astype(jnp.bfloat16),
        gate_grad,
        grad_in[None],
        grad_out[None],
    )


GROUPS = ((0,), (1,), (3,), (2,))
MIB = 1024 * 1024
WLIM = 56
PLAN = (
    "Z 1",
    "D1 0",
    "Z 3",
    "Z 2",
    "D2 0",
    "D1 1",
    "SEL 0",
    "D2 1",
    "D1 2",
    "SEL 1",
    "D2 2",
    "D1 3 SEL0",
    "D2 3",
    "SEL 2",
    "E 0",
    "E 1 E0",
    "SEL 3 E0",
    "E 2 E1",
    "R1 1 E2",
    "E 3 R11",
    "CUT 0",
    "R1 2 E3",
    "R2 1 R12",
    "R1 3 R21",
    "R2 2 R13",
    "H 1 R22",
    "R1 0 H1",
    "R2 3 R10",
    "H 2 R23",
    "R2 0 H2",
    "H 3 R20",
    "W 0 H3",
    "H 0 W0",
)


def expert_kernel(near, far, matrix_in, matrix_out, near_parts, far_parts, act, pre):
    half = near.shape[0] // 2
    rows = jnp.concatenate([near[:half], far[:half]], axis=0)
    grads = jnp.concatenate([near[half:], far[half:]], axis=0)
    hidden_pre = jnp.dot(rows, matrix_in[...], preferred_element_type=jnp.float32)
    activation, slope = gelu_parts(hidden_pre)
    grad_act = lax.dot_general(
        grads, matrix_out[...], (((1,), (1,)), ((), ())), preferred_element_type=jnp.float32
    )
    act[...] = activation.astype(jnp.bfloat16)
    pre[...] = (grad_act * slope).astype(jnp.bfloat16)
    out = jnp.dot(act[...], matrix_out[...], preferred_element_type=jnp.float32)
    near_parts[:half] = out[:half].astype(jnp.bfloat16)
    far_parts[:half] = out[half:].astype(jnp.bfloat16)
    back = lax.dot_general(
        pre[...], matrix_in[...], (((1,), (1,)), ((), ())), preferred_element_type=jnp.float32
    )
    near_parts[half:] = back[:half].astype(jnp.bfloat16)
    far_parts[half:] = back[half:].astype(jnp.bfloat16)


def expert_call(near, far, matrix_in, matrix_out):
    rows, width = near.shape
    hidden = matrix_in.shape[1]
    vmem = pl.BlockSpec(memory_space=pltpu.VMEM)
    return pl.pallas_call(
        expert_kernel,
        out_shape=(
            jax.ShapeDtypeStruct((rows, width), jnp.bfloat16),
            jax.ShapeDtypeStruct((rows, width), jnp.bfloat16),
            jax.ShapeDtypeStruct((rows, hidden), jnp.bfloat16),
            jax.ShapeDtypeStruct((rows, hidden), jnp.bfloat16),
        ),
        in_specs=[vmem] * 4,
        out_specs=(vmem,) * 4,
        compiler_params=pltpu.CompilerParams(vmem_limit_bytes=16 * MIB),
        cost_estimate=pl.CostEstimate(flops=0, bytes_accessed=0, transcendentals=0),
    )(near, far, matrix_in, matrix_out)


def start_kernel(experts, ids_at, priority_at, gates_at, tokens_at, cotangent_at, places, *rest):
    blocks, (ids, priority, gates, source, sems) = rest[:experts], rest[experts:]
    slot_count, block_rows = places.shape[2], blocks[0].shape[0]
    token_count = source.shape[0]
    place_dp = lax.axis_index("dp")
    first_half = lax.axis_index("rep") == 0
    small = [
        pltpu.make_async_copy(whole, held, sems.at[i])
        for i, (whole, held) in enumerate(((ids_at, ids), (priority_at, priority), (gates_at, gates)))
    ]
    for copy in small:
        copy.start()

    @pl.when(first_half)
    def _():
        pltpu.make_async_copy(tokens_at, source, sems.at[3]).start()

    @pl.when(jnp.logical_not(first_half))
    def _():
        pltpu.make_async_copy(cotangent_at, source, sems.at[3]).start()

    for copy in small:
        copy.wait()
    row = lax.broadcasted_iota(jnp.int32, (experts, 1), 0)
    near = lax.rem(place_dp // HBLK + row, experts)
    chosen = [ids[j : j + 1] == near for j in range(2)]
    chosen_any = chosen[0] | chosen[1]
    early = lax.broadcasted_iota(jnp.int32, (token_count, token_count), 0)
    late = lax.broadcasted_iota(jnp.int32, (token_count, token_count), 1)
    rank = jnp.dot(
        chosen_any.astype(jnp.bfloat16),
        (early < late).astype(jnp.bfloat16),
        preferred_element_type=jnp.float32,
    ).astype(jnp.int32)
    rank = jnp.where(chosen_any, rank, -1)
    near_gate = jnp.where(chosen[0], gates[0:1], gates[1:2])
    slots = lax.broadcasted_iota(jnp.int32, (slot_count, token_count), 0)
    pltpu.make_async_copy(tokens_at, source, sems.at[3]).wait()
    for k in range(experts):
        spread = rank[k : k + 1] == slots
        rows = jnp.dot(spread.astype(jnp.bfloat16), source[...], preferred_element_type=jnp.float32)
        slot_gate = jnp.sum(jnp.where(spread, near_gate[k : k + 1], 0.0), axis=1, keepdims=True)
        key = 1 + priority[...] + jnp.where(chosen[0][k : k + 1], PRIO, 0)
        slot_key = lax.dot_general(
            key.astype(jnp.bfloat16),
            spread.astype(jnp.bfloat16),
            (((1,), (1,)), ((), ())),
            preferred_element_type=jnp.float32,
        )
        whole = (rows * jnp.where(first_half, 1.0, slot_gate)).astype(jnp.bfloat16)
        spare = jnp.zeros((block_rows - slot_count, rows.shape[1]), jnp.bfloat16)
        blocks[k][...] = jnp.concatenate([whole, spare], axis=0)
        blocks[k][slot_count : slot_count + 1, :slot_count] = slot_key.astype(jnp.bfloat16)
        for j in range(2):
            places[j, k] = (spread & chosen[j][k : k + 1]).astype(jnp.bfloat16)


def start_call(ids, priority, gates, tokens, cotangent, experts, slot_count):
    token_count, width = tokens.shape
    block_rows = (slot_count + 1 + 15) // 16 * 16
    vmem = pl.BlockSpec(memory_space=pltpu.VMEM)
    return pl.pallas_call(
        functools.partial(start_kernel, experts),
        out_shape=(
            jax.ShapeDtypeStruct((2, experts, slot_count, token_count), jnp.bfloat16),
        )
        + (jax.ShapeDtypeStruct((block_rows, width), jnp.bfloat16),) * experts,
        in_specs=[pl.BlockSpec(memory_space=pl.ANY)] * 5,
        out_specs=(vmem,) * (1 + experts),
        scratch_shapes=[
            pltpu.VMEM(ids.shape, jnp.int32),
            pltpu.VMEM(priority.shape, jnp.int32),
            pltpu.VMEM(gates.shape, jnp.float32),
            pltpu.VMEM(tokens.shape, jnp.bfloat16),
            pltpu.SemaphoreType.DMA((4,)),
        ],
        compiler_params=pltpu.CompilerParams(vmem_limit_bytes=56 * MIB),
        cost_estimate=pl.CostEstimate(flops=0, bytes_accessed=0, transcendentals=0),
    )(ids, priority, gates, tokens, cotangent)


def cut_kernel(slot_count, block_rows, capacity, *refs):
    group_count = len(refs) // 2 - 2
    pieces, (kept, mine, keys, sems) = refs[: 2 * group_count], refs[2 * group_count :]
    copies, at = [], 0
    for piece in pieces:
        for block in range(piece.shape[0] // 2 // block_rows):
            last = pl.ds((block + 1) * block_rows - 16, 16)
            copies.append(
                pltpu.make_async_copy(piece.at[last, pl.ds(0, 128)], keys.at[at], sems.at[at])
            )
            at += 1
    for copy in copies:
        copy.start()
    for copy in copies:
        copy.wait()
    row = slot_count - (block_rows - 16)
    rows = [keys[i, row : row + 1, :slot_count].astype(jnp.float32) - 1.0 for i in range(at)]
    levels = lax.broadcasted_iota(jnp.int32, (2 * PRIO, 1), 0).astype(jnp.float32)
    above = sum((one >= levels).astype(jnp.float32) for one in rows)
    above = jnp.sum(above, axis=1, keepdims=True)
    cutoff = jnp.sum((above > capacity).astype(jnp.float32), axis=0, keepdims=True)
    diagonal = lax.broadcasted_iota(
        jnp.int32, (block_rows, slot_count), 0
    ) == lax.broadcasted_iota(jnp.int32, (block_rows, slot_count), 1)
    for i, one in enumerate(rows):
        inside = jnp.where(diagonal & (one >= cutoff), 1.0, 0.0)
        column = jnp.sum(inside, axis=1, keepdims=True)
        kept[i * block_rows : (i + 1) * block_rows] = jnp.broadcast_to(column, (block_rows, 128)).astype(jnp.bfloat16)
        if i % (at // group_count) == 0:
            g = i // (at // group_count)
            mine[g] = jnp.broadcast_to(column, (block_rows, 128))


def cut_call(pieces, slot_count, block_rows, capacity):
    total = sum(piece.shape[0] // 2 for piece in pieces)
    vmem = pl.BlockSpec(memory_space=pltpu.VMEM)
    return pl.pallas_call(
        functools.partial(cut_kernel, slot_count, block_rows, capacity),
        out_shape=(
            jax.ShapeDtypeStruct((total, 128), jnp.bfloat16),
            jax.ShapeDtypeStruct((len(pieces) // 2, block_rows, 128), jnp.float32),
        ),
        in_specs=[pl.BlockSpec(memory_space=pl.ANY)] * len(pieces),
        out_specs=(vmem,) * 2,
        scratch_shapes=[
            pltpu.VMEM((total // block_rows, 16, 128), jnp.bfloat16),
            pltpu.SemaphoreType.DMA((total // block_rows,)),
        ],
        compiler_params=pltpu.CompilerParams(vmem_limit_bytes=8 * MIB),
        cost_estimate=pl.CostEstimate(flops=0, bytes_accessed=0, transcendentals=0),
    )(*pieces)


def weight_kernel(kept, *refs):
    group_count = (len(refs) - 4) // 6
    parts, hiddens = refs[: 4 * group_count], refs[4 * group_count : 6 * group_count]
    grad_in, grad_out, act, pre = refs[6 * group_count :]

    @pl.when(pl.program_id(0) == 0)
    def _():
        keep = kept[:, 0:1]
        act[...] = jnp.concatenate([one[...] for one in hiddens[::2]], axis=0) * keep
        pre[...] = jnp.concatenate([one[...] for one in hiddens[1::2]], axis=0) * keep

    contract_first = (((0,), (0,)), ((), ()))
    rows = jnp.concatenate([one[...] for one in parts[::2]], axis=0)
    grads = jnp.concatenate([one[...] for one in parts[1::2]], axis=0)
    grad_in[...] = lax.dot_general(
        rows, pre[...], contract_first, preferred_element_type=jnp.float32
    ).astype(jnp.bfloat16)
    grad_out[...] = lax.dot_general(
        act[...], grads, contract_first, preferred_element_type=jnp.float32
    ).astype(jnp.bfloat16)


def weight_call(kept, saved):
    width, hidden = saved[0][0].shape[1], saved[0][2].shape[1]
    all_rows = sum(one[2].shape[0] for one in saved)
    tile = 256
    operands, specs = [], []
    for near, far, _, _ in saved:
        for whole in (near, far):
            for kind in range(2):
                operands.append(whole)
                specs.append(
                    pl.BlockSpec((whole.shape[0] // 2, tile), functools.partial(lambda kind, j: (kind, j), kind))
                )
    for _, _, act, pre in saved:
        for whole in (act, pre):
            operands.append(whole)
            specs.append(pl.BlockSpec(whole.shape, lambda j: (0, 0)))
    return pl.pallas_call(
        weight_kernel,
        grid=(pl.cdiv(width, tile),),
        out_shape=(
            jax.ShapeDtypeStruct((width, hidden), jnp.bfloat16),
            jax.ShapeDtypeStruct((hidden, width), jnp.bfloat16),
        ),
        in_specs=[pl.BlockSpec(kept.shape, lambda j: (0, 0))] + specs,
        out_specs=(
            pl.BlockSpec((tile, hidden), lambda j: (j, 0)),
            pl.BlockSpec((hidden, tile), lambda j: (0, j)),
        ),
        scratch_shapes=[pltpu.VMEM((all_rows, hidden), jnp.bfloat16)] * 2,
        compiler_params=pltpu.CompilerParams(vmem_limit_bytes=WLIM * MIB),
        cost_estimate=pl.CostEstimate(flops=0, bytes_accessed=0, transcendentals=0),
    )(kept, *operands)


def token_kernel(gates, places, cotangent, *refs):
    homes, (away, stay, gate_grad) = refs[:-3], refs[-3:]
    first_half = lax.axis_index("rep") == 0
    token_count, width = cotangent.shape
    half = width // 2
    diagonal = lax.broadcasted_iota(
        jnp.int32, (token_count, token_count), 0
    ) == lax.broadcasted_iota(jnp.int32, (token_count, token_count), 1)
    back = jnp.concatenate([one[...] for one in homes], axis=0)
    mixed, sums = 0.0, []
    for j in range(2):
        picker = jnp.concatenate([places[j, k] for k in range(len(homes))], axis=0)
        picked = lax.dot_general(
            picker, back, (((0,), (0,)), ((), ())), preferred_element_type=jnp.float32
        )
        gate = jnp.sum(jnp.where(diagonal, gates[j : j + 1], 0.0), axis=1, keepdims=True)
        mixed = mixed + picked * jnp.where(first_half, gate, 1.0)
        inner = jnp.sum(picked * cotangent[...].astype(jnp.float32), axis=1, keepdims=True)
        sums.append(jnp.sum(jnp.where(diagonal, inner, 0.0), axis=0, keepdims=True))
    mixed = mixed.astype(jnp.bfloat16).T
    upper, lower = mixed[:half], mixed[half:]
    away[:half] = jnp.where(first_half, lower, upper)
    stay[...] = jnp.where(first_half, upper, lower)
    left = jnp.concatenate(sums, axis=0)
    gate_grad[...] = left
    terms = []
    for _ in range(3):
        terms.append(left.astype(jnp.bfloat16))
        left = left - terms[-1].astype(jnp.float32)
    terms.append(jnp.zeros((away.shape[0] - half - 6, token_count), jnp.bfloat16))
    away[half:] = jnp.concatenate(terms, axis=0)


def token_call(gates, places, cotangent, homes):
    token_count, width = cotangent.shape
    vmem = pl.BlockSpec(memory_space=pltpu.VMEM)
    return pl.pallas_call(
        token_kernel,
        out_shape=(
            jax.ShapeDtypeStruct((width // 2 + 16, token_count), jnp.bfloat16),
            jax.ShapeDtypeStruct((width // 2, token_count), jnp.bfloat16),
            jax.ShapeDtypeStruct((2, token_count), jnp.float32),
        ),
        in_specs=[vmem] * (3 + len(homes)),
        out_specs=(vmem,) * 3,
        compiler_params=pltpu.CompilerParams(vmem_limit_bytes=16 * MIB),
        cost_estimate=pl.CostEstimate(flops=0, bytes_accessed=0, transcendentals=0),
    )(gates, places, cotangent, *homes)


def end_kernel(stay, got, gate_grad, output, grad_tokens, grad_gates):
    first_half = lax.axis_index("rep") == 0
    half = stay.shape[0]
    mine, theirs = stay[...], got[:half]
    output[...] = jnp.where(first_half, mine, theirs)
    grad_tokens[...] = jnp.where(first_half, theirs, mine)
    terms = got[half:].astype(jnp.float32)
    got_gate = terms[0:2] + terms[2:4] + terms[4:6]
    rows_half = gate_grad.shape[1] // 2
    grad_gates[...] = jnp.where(first_half, gate_grad[:, :rows_half], got_gate[:, rows_half:])


def end_call(stay, got, gate_grad):
    half, token_count = stay.shape
    vmem = pl.BlockSpec(memory_space=pltpu.VMEM)
    return pl.pallas_call(
        end_kernel,
        out_shape=(
            jax.ShapeDtypeStruct((half, token_count), jnp.bfloat16),
            jax.ShapeDtypeStruct((half, token_count), jnp.bfloat16),
            jax.ShapeDtypeStruct((2, token_count // 2), jnp.float32),
        ),
        in_specs=[vmem] * 3,
        out_specs=(vmem,) * 3,
        compiler_params=pltpu.CompilerParams(vmem_limit_bytes=16 * MIB),
    )(stay, got, gate_grad)


def plane_body(tokens, expert_ids, priority, gate_values, weight_in, weight_out, cotangent):
    token_count, width = tokens.shape
    dp_count = lax.axis_size("dp")
    experts = dp_count // HBLK
    slot_count = min(token_count, 2 * token_count // experts + max(1, token_count // (4 * experts)))
    capacity = 2 * token_count * dp_count // experts
    contract_first = (((0,), (0,)), ((), ()))
    contract_last = (((1,), (1,)), ((), ()))
    place_dp = lax.axis_index("dp")
    first_half = lax.axis_index("rep") == 0
    plane, quarter = place_dp // HBLK, place_dp % HBLK
    core_zero = quarter % 2 == 0
    groups = GROUPS

    def permutation(move):
        pairs = []
        for z in range(experts):
            for q in range(HBLK):
                for x in range(2):
                    z2, q2, x2 = move(z, q, x)
                    pairs.append((2 * (z * HBLK + q) + x, 2 * (z2 * HBLK + q2) + x2))
        return pairs

    def send(array, move):
        return lax.ppermute(array, ("dp", "rep"), permutation(move))

    def along_first(z, q, x):
        return (z, q, 1 - x) if q % 2 == 0 else (z, q ^ 2, x)

    def along_second(z, q, x):
        return (z, q ^ 2, x) if q % 2 == 0 else (z, q, 1 - x)

    def other_core(z, q, x):
        return (z, q ^ 1, x)

    def other_row(z, q, x):
        return (z, q ^ 2, x)

    def planes_on(k):
        return lambda z, q, x: ((z + k) % experts, q, x)

    def add(*terms):
        return sum(term.astype(jnp.float32) for term in terms).astype(jnp.bfloat16)

    def step(made, *values):
        if made:
            values, _ = lax.optimization_barrier((values, made))
        return values if len(values) > 1 else values[0]

    def join(parts):
        return parts[0] if len(parts) == 1 else jnp.concatenate(parts, axis=0)

    ids, gates = expert_ids.T, gate_values.T
    places, *blocks = start_call(
        ids, priority[None, :], gates, tokens, cotangent, experts, slot_count
    )
    block_rows = blocks[0].shape[0]

    matrix_in = weight_in[0]
    matrix_out = weight_out[0]
    state = [{} for _ in groups]
    home = {}

    def spread_first(g, block):
        one = state[g]
        one["b00"] = block
        one["r1"] = send(block, along_first)
        one["r2"] = send(block, along_second)
        return [one["r1"]]

    def spread_second(g, made):
        one = state[g]
        one["r1"] = step(made, one["r1"])
        one["b11"] = send(one["r1"], along_second)
        return [one["b11"]]

    def gather_near(g, made):
        one = state[g]
        b00, r1, r2, b11 = step(made, one["b00"], one["r1"], one["r2"], one["b11"])
        b10 = jnp.where(core_zero, r2, r1)
        b01 = jnp.where(core_zero, r1, r2)
        one["near"] = jnp.concatenate(
            [
                jnp.where(first_half, b00, b01),
                jnp.where(first_half, b10, b11),
                jnp.where(first_half, b01, b00),
                jnp.where(first_half, b11, b10),
            ],
            axis=0,
        )
        one["far"] = send(one["near"], other_core)
        return [one["near"]]

    def expert_work(g, made):
        one = state[g]
        near_rows, far_rows = step(made, one["near"], one["far"])
        near_parts, far_parts, act, pre = expert_call(near_rows, far_rows, matrix_in, matrix_out)
        one["saved"] = (near_rows, far_rows, act, pre)
        one["near_parts"], one["far_parts"] = near_parts, send(far_parts, other_core)
        return [act]

    def reduce_first(g, made):
        one = state[g]
        sums = add(*step(made, one["near_parts"], one["far_parts"]))
        out0, out1, dx0, dx1 = [
            sums[at * block_rows : at * block_rows + slot_count] for at in range(4)
        ]
        a00, a10 = jnp.where(first_half, out0, dx0), jnp.where(first_half, out1, dx1)
        a01, a11 = jnp.where(first_half, dx0, out0), jnp.where(first_half, dx1, out1)
        away = jnp.concatenate([jnp.where(core_zero, a01, a10), a11], axis=0)
        one["a00"], one["rest"] = a00, jnp.where(core_zero, a10, a01)
        one["back"] = send(away, along_first)
        return [away]

    def reduce_second(g, made):
        one = state[g]
        one["back"], rest = step(made, one["back"], one["rest"])
        last = add(rest, one["back"][slot_count:])
        one["last"] = send(last, along_second)
        return [last]

    def go_home(g, made):
        one = state[g]
        a00, back, last = step(made, one["a00"], one["back"], one["last"])
        (k,) = groups[g]
        done = (
            (a00.astype(jnp.float32) + back[:slot_count].astype(jnp.float32) + last.astype(jnp.float32))
            * mine[g, :slot_count, 0:1]
        ).astype(jnp.bfloat16)
        home[k] = done if k == 0 else send(done, planes_on(experts - k))
        return [done]

    arrived, events = {}, {}
    for entry in PLAN:
        name, g, *after = entry.split()
        g = int(g)
        made = [value for one in after for value in events[one]]
        if name == "Z":
            arrived[g] = send(step(made, blocks[g]), planes_on(g))
            here = [arrived[g]]
        elif name == "D1":
            (k,) = groups[g]
            here = spread_first(g, step(made, arrived[k] if k else blocks[0]))
        elif name == "D2":
            here = spread_second(g, made)
        elif name == "SEL":
            here = gather_near(g, made)
        elif name == "E":
            here = expert_work(g, made)
        elif name == "CUT":
            pieces = [piece for one in state for piece in one["saved"][:2]]
            kept, mine = cut_call(step(made, *pieces), slot_count, block_rows, capacity)
            here = [mine]
        elif name == "R1":
            here = reduce_first(g, made)
        elif name == "R2":
            here = reduce_second(g, made)
        elif name == "H":
            here = go_home(g, made)
        elif name == "W":
            saved = [step(made, *one["saved"]) for one in state]
            grad_in, grad_out = weight_call(kept, saved)
            here = [grad_in]
        events[name + str(g)] = here

    away, stay, gate_grad = token_call(gates, places, cotangent, [home[k] for k in range(experts)])
    got = lax.ppermute(away, "rep", [(0, 1), (1, 0)])
    output, grad_tokens, grad_gates = end_call(stay, got, gate_grad)
    return output.T, grad_tokens.T, grad_gates.T, grad_in[None], grad_out[None]


def solution(mesh):
    placed = (
        P("dp", None),
        P("dp", None),
        P("dp"),
        P("dp", None),
        P("dp", None, "rep"),
        P("dp", "rep", None),
        P("dp", None),
    )
    body = plane_body if mesh.shape["rep"] == 2 and mesh.shape["dp"] == 4 * HBLK else general_body
    return jax.shard_map(
        body,
        mesh=mesh,
        in_specs=placed,
        out_specs=(
            P("dp", "rep"),
            P("dp", "rep"),
            P(("dp", "rep"), None),
            P("dp", None, "rep"),
            P("dp", "rep", None),
        ),
        check_vma=False,
    )
```

```python
import functools
import math

import jax
import jax.numpy as jnp
from jax import lax
from jax.experimental import pallas as pl
from jax.experimental.pallas import tpu as pltpu
from jax.sharding import PartitionSpec as P

HBLK = 4
PRIO = 64


def gelu_parts(hidden_pre):
    normal_cdf = 0.5 * (1.0 + jax.scipy.special.erf(hidden_pre * (1.0 / math.sqrt(2.0))))
    density = jnp.exp(-0.5 * hidden_pre * hidden_pre) * (1.0 / math.sqrt(2.0 * math.pi))
    return (hidden_pre * normal_cdf, normal_cdf + hidden_pre * density)


def general_body(tokens, expert_ids, priority, gate_values, weight_in, weight_out, cotangent):
    token_count = tokens.shape[0]
    dp_count = lax.axis_size("dp")
    experts = dp_count // HBLK
    slot_count = min(token_count, 2 * token_count // experts + max(1, token_count // (4 * experts)))
    capacity = 2 * token_count * dp_count // experts
    row_total = dp_count * slot_count
    contract_first = (((0,), (0,)), ((), ()))
    contract_last = (((1,), (1,)), ((), ()))
    priority_key = (
        priority[:, None] + PRIO * (1 - jnp.arange(2, dtype=jnp.int32))[None, :]
    ).reshape(-1)
    flat_expert = expert_ids.reshape(-1)
    expert_hot = (flat_expert[:, None] == jnp.arange(experts, dtype=jnp.int32)[None, :]).astype(
        jnp.int32
    )
    key_hot = (priority_key[:, None] == jnp.arange(2 * PRIO, dtype=jnp.int32)[None, :]).astype(
        jnp.int32
    )
    local_counts = jnp.dot(expert_hot.T, key_hot, preferred_element_type=jnp.int32)
    counts = lax.psum(local_counts, "dp")
    above_count = jnp.cumsum(counts[:, ::-1], axis=1)[:, ::-1]
    cutoff_key = jnp.sum((above_count > capacity).astype(jnp.int32), axis=1)
    kept_mask = priority_key >= jnp.sum(expert_hot * cutoff_key[None, :], axis=1)
    before_count = jnp.cumsum(expert_hot, axis=0) - expert_hot
    slot_index = jnp.sum(expert_hot * before_count, axis=1)
    slot_hot = (slot_index[:, None] == jnp.arange(slot_count, dtype=jnp.int32)[None, :]).astype(
        jnp.int32
    )
    place_map = (
        expert_hot[:, :, None] * slot_hot[:, None, :] * kept_mask.astype(jnp.int32)[:, None, None]
    )
    place_map = place_map.astype(jnp.bfloat16).reshape(2 * token_count, experts * slot_count)
    token_place = jnp.sum(place_map.reshape(token_count, 2, experts * slot_count), axis=1)
    grad_source = (
        gate_values.reshape(-1)[:, None] * jnp.repeat(cotangent, 2, axis=0).astype(jnp.float32)
    ).astype(jnp.bfloat16)
    wide_index = jnp.arange(row_total, dtype=jnp.int32)
    wide_index = wide_index // (HBLK * slot_count) * slot_count + wide_index % slot_count

    def widen(matrix):
        return jnp.take(matrix, wide_index, axis=0)

    send_rows = lax.dot_general(
        token_place, tokens, contract_first, preferred_element_type=jnp.float32
    ).astype(jnp.bfloat16)
    send_grads = lax.dot_general(
        place_map, grad_source, contract_first, preferred_element_type=jnp.float32
    ).astype(jnp.bfloat16)
    rows, grad_rows = (
        lax.all_to_all(widen(send_rows), "dp", split_axis=0, concat_axis=0, tiled=True),
        lax.all_to_all(widen(send_grads), "dp", split_axis=0, concat_axis=0, tiled=True),
    )
    matrix_in = weight_in[0]
    matrix_out = weight_out[0]
    hidden_pre = jnp.dot(rows, matrix_in, preferred_element_type=jnp.float32)
    activation, slope = gelu_parts(hidden_pre)
    activation = activation.astype(jnp.bfloat16)
    partial_out = jnp.dot(activation, matrix_out, preferred_element_type=jnp.float32).astype(
        jnp.bfloat16
    )
    grad_act = lax.dot_general(
        grad_rows, matrix_out, contract_last, preferred_element_type=jnp.float32
    )
    grad_pre = (grad_act * slope).astype(jnp.bfloat16)
    grad_in = lax.dot_general(
        rows, grad_pre, contract_first, preferred_element_type=jnp.float32
    ).astype(jnp.bfloat16)
    grad_out = lax.dot_general(
        activation, grad_rows, contract_first, preferred_element_type=jnp.float32
    ).astype(jnp.bfloat16)
    partial_dx = lax.dot_general(
        grad_pre, matrix_in, contract_last, preferred_element_type=jnp.float32
    ).astype(jnp.bfloat16)
    block_range = jnp.arange(HBLK, dtype=jnp.int32)
    pick_index = (
        (flat_expert[:, None] * HBLK + block_range[None, :]) * slot_count + slot_index[:, None]
    ).reshape(-1)

    def pick_rows(returned):
        width = returned.shape[-1]
        picked = jnp.take(returned, pick_index, axis=0)
        summed = jnp.sum(picked.reshape(2 * token_count, HBLK, width).astype(jnp.float32), axis=1)
        return jnp.where(kept_mask[:, None], summed, 0.0).reshape(token_count, 2, width)

    back_out, back_dx = (
        lax.all_to_all(partial_out, "dp", split_axis=0, concat_axis=0, tiled=True),
        lax.all_to_all(partial_dx, "dp", split_axis=0, concat_axis=0, tiled=True),
    )
    out_rows = pick_rows(back_out)
    dx_rows = pick_rows(back_dx)
    mixed = jnp.sum(gate_values[:, :, None] * out_rows, axis=1)
    token_grad = jnp.sum(dx_rows, axis=1)
    gate_grad = jnp.sum(cotangent.astype(jnp.float32)[:, None, :] * out_rows, axis=2)
    gate_grad = lax.psum_scatter(gate_grad, "rep", scatter_dimension=0, tiled=True)
    mixed, token_grad = (
        lax.psum_scatter(mixed.astype(jnp.bfloat16), "rep", scatter_dimension=1, tiled=True).astype(
            jnp.float32
        ),
        lax.psum_scatter(
            token_grad.astype(jnp.bfloat16), "rep", scatter_dimension=1, tiled=True
        ).astype(jnp.float32),
    )
    return (
        mixed.astype(jnp.bfloat16),
        token_grad.astype(jnp.bfloat16),
        gate_grad,
        grad_in[None],
        grad_out[None],
    )


GROUPS = ((0,), (1,), (3,), (2,))
MIB = 1024 * 1024
WLIM = 56
PLAN = (
    "Z 1",
    "D1 0",
    "Z 3",
    "Z 2",
    "D2 0",
    "L 0",
    "D1 1",
    "SEL 0 L0",
    "D2 1",
    "D1 2",
    "SEL 1",
    "D2 2",
    "D1 3 SEL0",
    "D2 3",
    "SEL 2",
    "E 0",
    "E 1 E0",
    "SEL 3 E0",
    "E 2 E1",
    "R1 1 E2",
    "E 3 R11",
    "CUT 0",
    "R1 2 E3",
    "R1 3 R12",
    "R2 1 R13",
    "R2 2 R21",
    "H 1 R22",
    "R1 0 H1",
    "R2 3 R10",
    "H 2 R23",
    "R2 0 H2",
    "H 3 R20",
    "W 0 H3",
    "H 0 W0",
)


def expert_kernel(near, far, matrix_in, matrix_out, near_parts, far_parts, act, pre):
    half = near.shape[0] // 2
    rows = jnp.concatenate([near[:half], far[:half]], axis=0)
    grads = jnp.concatenate([near[half:], far[half:]], axis=0)
    hidden_pre = jnp.dot(rows, matrix_in[...], preferred_element_type=jnp.float32)
    activation, slope = gelu_parts(hidden_pre)
    grad_act = lax.dot_general(
        grads, matrix_out[...], (((1,), (1,)), ((), ())), preferred_element_type=jnp.float32
    )
    act[...] = activation.astype(jnp.bfloat16)
    pre[...] = (grad_act * slope).astype(jnp.bfloat16)
    out = jnp.dot(act[...], matrix_out[...], preferred_element_type=jnp.float32)
    near_parts[:half] = out[:half].astype(jnp.bfloat16)
    far_parts[:half] = out[half:].astype(jnp.bfloat16)
    back = lax.dot_general(
        pre[...], matrix_in[...], (((1,), (1,)), ((), ())), preferred_element_type=jnp.float32
    )
    near_parts[half:] = back[:half].astype(jnp.bfloat16)
    far_parts[half:] = back[half:].astype(jnp.bfloat16)


def expert_call(near, far, matrix_in, matrix_out):
    rows, width = near.shape
    hidden = matrix_in.shape[1]
    vmem = pl.BlockSpec(memory_space=pltpu.VMEM)
    return pl.pallas_call(
        expert_kernel,
        out_shape=(
            jax.ShapeDtypeStruct((rows, width), jnp.bfloat16),
            jax.ShapeDtypeStruct((rows, width), jnp.bfloat16),
            jax.ShapeDtypeStruct((rows, hidden), jnp.bfloat16),
            jax.ShapeDtypeStruct((rows, hidden), jnp.bfloat16),
        ),
        in_specs=[vmem] * 4,
        out_specs=(vmem,) * 4,
        compiler_params=pltpu.CompilerParams(vmem_limit_bytes=16 * MIB),
        cost_estimate=pl.CostEstimate(flops=0, bytes_accessed=0, transcendentals=0),
    )(near, far, matrix_in, matrix_out)


def start_kernel(experts, ids_at, priority_at, gates_at, tokens_at, cotangent_at, places, *rest):
    blocks, (ids, priority, gates, source, sems) = rest[:experts], rest[experts:]
    slot_count, block_rows = places.shape[2], blocks[0].shape[0]
    token_count = source.shape[0]
    place_dp = lax.axis_index("dp")
    first_half = lax.axis_index("rep") == 0
    small = [
        pltpu.make_async_copy(whole, held, sems.at[i])
        for i, (whole, held) in enumerate(((ids_at, ids), (priority_at, priority), (gates_at, gates)))
    ]
    for copy in small:
        copy.start()

    @pl.when(first_half)
    def _():
        pltpu.make_async_copy(tokens_at, source, sems.at[3]).start()

    @pl.when(jnp.logical_not(first_half))
    def _():
        pltpu.make_async_copy(cotangent_at, source, sems.at[3]).start()

    for copy in small:
        copy.wait()
    row = lax.broadcasted_iota(jnp.int32, (experts, 1), 0)
    near = lax.rem(place_dp // HBLK + row, experts)
    chosen = [ids[j : j + 1] == near for j in range(2)]
    chosen_any = chosen[0] | chosen[1]
    early = lax.broadcasted_iota(jnp.int32, (token_count, token_count), 0)
    late = lax.broadcasted_iota(jnp.int32, (token_count, token_count), 1)
    rank = jnp.dot(
        chosen_any.astype(jnp.bfloat16),
        (early < late).astype(jnp.bfloat16),
        preferred_element_type=jnp.float32,
    ).astype(jnp.int32)
    rank = jnp.where(chosen_any, rank, -1)
    near_gate = jnp.where(chosen[0], gates[0:1], gates[1:2])
    slots = lax.broadcasted_iota(jnp.int32, (slot_count, token_count), 0)
    pltpu.make_async_copy(tokens_at, source, sems.at[3]).wait()
    for k in range(experts):
        spread = rank[k : k + 1] == slots
        rows = jnp.dot(spread.astype(jnp.bfloat16), source[...], preferred_element_type=jnp.float32)
        slot_gate = jnp.sum(jnp.where(spread, near_gate[k : k + 1], 0.0), axis=1, keepdims=True)
        key = 1 + priority[...] + jnp.where(chosen[0][k : k + 1], PRIO, 0)
        slot_key = lax.dot_general(
            key.astype(jnp.bfloat16),
            spread.astype(jnp.bfloat16),
            (((1,), (1,)), ((), ())),
            preferred_element_type=jnp.float32,
        )
        whole = (rows * jnp.where(first_half, 1.0, slot_gate)).astype(jnp.bfloat16)
        spare = jnp.zeros((block_rows - slot_count, rows.shape[1]), jnp.bfloat16)
        blocks[k][...] = jnp.concatenate([whole, spare], axis=0)
        blocks[k][slot_count : slot_count + 1, :slot_count] = slot_key.astype(jnp.bfloat16)
        for j in range(2):
            places[j, k] = (spread & chosen[j][k : k + 1]).astype(jnp.bfloat16)


def start_call(ids, priority, gates, tokens, cotangent, experts, slot_count):
    token_count, width = tokens.shape
    block_rows = (slot_count + 1 + 15) // 16 * 16
    vmem = pl.BlockSpec(memory_space=pltpu.VMEM)
    return pl.pallas_call(
        functools.partial(start_kernel, experts),
        out_shape=(
            jax.ShapeDtypeStruct((2, experts, slot_count, token_count), jnp.bfloat16),
        )
        + (jax.ShapeDtypeStruct((block_rows, width), jnp.bfloat16),) * experts,
        in_specs=[pl.BlockSpec(memory_space=pl.ANY)] * 5,
        out_specs=(vmem,) * (1 + experts),
        scratch_shapes=[
            pltpu.VMEM(ids.shape, jnp.int32),
            pltpu.VMEM(priority.shape, jnp.int32),
            pltpu.VMEM(gates.shape, jnp.float32),
            pltpu.VMEM(tokens.shape, jnp.bfloat16),
            pltpu.SemaphoreType.DMA((4,)),
        ],
        compiler_params=pltpu.CompilerParams(vmem_limit_bytes=56 * MIB),
        cost_estimate=pl.CostEstimate(flops=0, bytes_accessed=0, transcendentals=0),
    )(ids, priority, gates, tokens, cotangent)


def cut_kernel(slot_count, block_rows, capacity, *refs):
    group_count = len(refs) // 2 - 2
    pieces, (kept, mine, keys, sems) = refs[: 2 * group_count], refs[2 * group_count :]
    copies, at = [], 0
    for piece in pieces:
        for block in range(piece.shape[0] // 2 // block_rows):
            last = pl.ds((block + 1) * block_rows - 16, 16)
            copies.append(
                pltpu.make_async_copy(piece.at[last, pl.ds(0, 128)], keys.at[at], sems.at[at])
            )
            at += 1
    for copy in copies:
        copy.start()
    for copy in copies:
        copy.wait()
    row = slot_count - (block_rows - 16)
    rows = [keys[i, row : row + 1, :slot_count].astype(jnp.float32) - 1.0 for i in range(at)]
    levels = lax.broadcasted_iota(jnp.int32, (2 * PRIO, 1), 0).astype(jnp.float32)
    above = sum((one >= levels).astype(jnp.float32) for one in rows)
    above = jnp.sum(above, axis=1, keepdims=True)
    cutoff = jnp.sum((above > capacity).astype(jnp.float32), axis=0, keepdims=True)
    diagonal = lax.broadcasted_iota(
        jnp.int32, (block_rows, slot_count), 0
    ) == lax.broadcasted_iota(jnp.int32, (block_rows, slot_count), 1)
    for i, one in enumerate(rows):
        inside = jnp.where(diagonal & (one >= cutoff), 1.0, 0.0)
        column = jnp.sum(inside, axis=1, keepdims=True)
        kept[i * block_rows : (i + 1) * block_rows] = jnp.broadcast_to(column, (block_rows, 128)).astype(jnp.bfloat16)
        if i % (at // group_count) == 0:
            g = i // (at // group_count)
            mine[g] = jnp.broadcast_to(column, (block_rows, 128))


def cut_call(pieces, slot_count, block_rows, capacity):
    total = sum(piece.shape[0] // 2 for piece in pieces)
    vmem = pl.BlockSpec(memory_space=pltpu.VMEM)
    return pl.pallas_call(
        functools.partial(cut_kernel, slot_count, block_rows, capacity),
        out_shape=(
            jax.ShapeDtypeStruct((total, 128), jnp.bfloat16),
            jax.ShapeDtypeStruct((len(pieces) // 2, block_rows, 128), jnp.float32),
        ),
        in_specs=[pl.BlockSpec(memory_space=pl.ANY)] * len(pieces),
        out_specs=(vmem,) * 2,
        scratch_shapes=[
            pltpu.VMEM((total // block_rows, 16, 128), jnp.bfloat16),
            pltpu.SemaphoreType.DMA((total // block_rows,)),
        ],
        compiler_params=pltpu.CompilerParams(vmem_limit_bytes=8 * MIB),
        cost_estimate=pl.CostEstimate(flops=0, bytes_accessed=0, transcendentals=0),
    )(*pieces)


def weight_kernel(kept, *refs):
    group_count = (len(refs) - 10) // 4
    pieces, out_at = refs[: 4 * group_count], refs[4 * group_count : 4 * group_count + 2]
    rows, grads, act, pre, grad_in, grad_out, sems, out_sems = refs[4 * group_count + 2 :]
    steps, base = ([], [], [], []), 0
    for g in range(group_count):
        near, far, act_at, pre_at = pieces[4 * g : 4 * g + 4]
        count = near.shape[0]
        half = count // 2
        for slot, (whole, to) in enumerate(((pre_at, pre), (act_at, act))):
            steps[2 * slot].append(
                pltpu.make_async_copy(whole, to.at[pl.ds(base, count)], sems.at[g, 3 * slot])
            )
        for part, whole in enumerate((near, far)):
            for kind, to in enumerate((rows, grads)):
                steps[2 * kind + 1].append(
                    pltpu.make_async_copy(
                        whole.at[pl.ds(kind * half, half)],
                        to.at[pl.ds(base + part * half, half)],
                        sems.at[g, 3 * kind + 1 + part],
                    )
                )
        base += count
    for copies in steps:
        for copy in copies:
            copy.start()
    contract_first = (((0,), (0,)), ((), ()))
    keep = kept[:, 0:1]
    width = rows.shape[1]
    sent = []

    for copy in steps[0]:
        copy.wait()
    pre[...] = pre[...] * keep
    for copy in steps[1]:
        copy.wait()
    for first in range(0, width, 256):
        span = slice(first, min(width, first + 256))
        grad_in[span] = lax.dot_general(
            rows[:, span], pre[...], contract_first, preferred_element_type=jnp.float32
        ).astype(jnp.bfloat16)
    sent.append(pltpu.make_async_copy(grad_in, out_at[0], out_sems.at[0]))
    sent[-1].start()
    for copy in steps[2]:
        copy.wait()
    act[...] = act[...] * keep
    for copy in steps[3]:
        copy.wait()
    for first in range(0, width, 256):
        span = slice(first, min(width, first + 256))
        grad_out[:, span] = lax.dot_general(
            act[...], grads[:, span], contract_first, preferred_element_type=jnp.float32
        ).astype(jnp.bfloat16)
    sent.append(pltpu.make_async_copy(grad_out, out_at[1], out_sems.at[1]))
    sent[-1].start()
    for copy in sent:
        copy.wait()


def weight_call(kept, saved):
    pieces = [piece for one in saved for piece in one]
    width, hidden = pieces[0].shape[1], pieces[2].shape[1]
    all_rows = sum(one[2].shape[0] for one in saved)
    vmem, anywhere = pl.BlockSpec(memory_space=pltpu.VMEM), pl.BlockSpec(memory_space=pl.ANY)
    return pl.pallas_call(
        weight_kernel,
        out_shape=(
            jax.ShapeDtypeStruct((width, hidden), jnp.bfloat16),
            jax.ShapeDtypeStruct((hidden, width), jnp.bfloat16),
        ),
        in_specs=[vmem] + [anywhere] * len(pieces),
        out_specs=(anywhere,) * 2,
        scratch_shapes=[pltpu.VMEM((all_rows, width), jnp.bfloat16)] * 2
        + [pltpu.VMEM((all_rows, hidden), jnp.bfloat16)] * 2
        + [pltpu.VMEM((width, hidden), jnp.bfloat16), pltpu.VMEM((hidden, width), jnp.bfloat16)]
        + [pltpu.SemaphoreType.DMA((len(saved), 6)), pltpu.SemaphoreType.DMA((2,))],
        compiler_params=pltpu.CompilerParams(vmem_limit_bytes=WLIM * MIB),
        cost_estimate=pl.CostEstimate(flops=0, bytes_accessed=0, transcendentals=0),
    )(kept, *pieces)


def load_kernel(in_at, out_at, matrix_in, matrix_out, sems):
    copies = [
        pltpu.make_async_copy(in_at, matrix_in, sems.at[0]),
        pltpu.make_async_copy(out_at, matrix_out, sems.at[1]),
    ]
    for copy in copies:
        copy.start()
    for copy in copies:
        copy.wait()


def load_call(matrix_in, matrix_out):
    vmem, anywhere = pl.BlockSpec(memory_space=pltpu.VMEM), pl.BlockSpec(memory_space=pl.ANY)
    return pl.pallas_call(
        load_kernel,
        out_shape=tuple(
            jax.ShapeDtypeStruct(one.shape, one.dtype) for one in (matrix_in, matrix_out)
        ),
        in_specs=[anywhere] * 2,
        out_specs=(vmem,) * 2,
        scratch_shapes=[pltpu.SemaphoreType.DMA((2,))],
        compiler_params=pltpu.CompilerParams(vmem_limit_bytes=8 * MIB),
        cost_estimate=pl.CostEstimate(flops=0, bytes_accessed=0, transcendentals=0),
    )(matrix_in, matrix_out)


def token_kernel(gates, places, cotangent, *refs):
    homes, (away, stay, gate_grad) = refs[:-3], refs[-3:]
    first_half = lax.axis_index("rep") == 0
    token_count, width = cotangent.shape
    half = width // 2
    diagonal = lax.broadcasted_iota(
        jnp.int32, (token_count, token_count), 0
    ) == lax.broadcasted_iota(jnp.int32, (token_count, token_count), 1)
    back = jnp.concatenate([one[...] for one in homes], axis=0)
    mixed, sums = 0.0, []
    for j in range(2):
        picker = jnp.concatenate([places[j, k] for k in range(len(homes))], axis=0)
        picked = lax.dot_general(
            picker, back, (((0,), (0,)), ((), ())), preferred_element_type=jnp.float32
        )
        gate = jnp.sum(jnp.where(diagonal, gates[j : j + 1], 0.0), axis=1, keepdims=True)
        mixed = mixed + picked * jnp.where(first_half, gate, 1.0)
        inner = jnp.sum(picked * cotangent[...].astype(jnp.float32), axis=1, keepdims=True)
        sums.append(jnp.sum(jnp.where(diagonal, inner, 0.0), axis=0, keepdims=True))
    mixed = mixed.astype(jnp.bfloat16).T
    upper, lower = mixed[:half], mixed[half:]
    away[:half] = jnp.where(first_half, lower, upper)
    stay[...] = jnp.where(first_half, upper, lower)
    left = jnp.concatenate(sums, axis=0)
    gate_grad[...] = left
    terms = []
    for _ in range(3):
        terms.append(left.astype(jnp.bfloat16))
        left = left - terms[-1].astype(jnp.float32)
    terms.append(jnp.zeros((away.shape[0] - half - 6, token_count), jnp.bfloat16))
    away[half:] = jnp.concatenate(terms, axis=0)


def token_call(gates, places, cotangent, homes):
    token_count, width = cotangent.shape
    vmem = pl.BlockSpec(memory_space=pltpu.VMEM)
    return pl.pallas_call(
        token_kernel,
        out_shape=(
            jax.ShapeDtypeStruct((width // 2 + 16, token_count), jnp.bfloat16),
            jax.ShapeDtypeStruct((width // 2, token_count), jnp.bfloat16),
            jax.ShapeDtypeStruct((2, token_count), jnp.float32),
        ),
        in_specs=[vmem] * (3 + len(homes)),
        out_specs=(vmem,) * 3,
        compiler_params=pltpu.CompilerParams(vmem_limit_bytes=16 * MIB),
        cost_estimate=pl.CostEstimate(flops=0, bytes_accessed=0, transcendentals=0),
    )(gates, places, cotangent, *homes)


def end_kernel(stay, got, gate_grad, output, grad_tokens, grad_gates):
    first_half = lax.axis_index("rep") == 0
    half = stay.shape[0]
    mine, theirs = stay[...], got[:half]
    output[...] = jnp.where(first_half, mine, theirs)
    grad_tokens[...] = jnp.where(first_half, theirs, mine)
    terms = got[half:].astype(jnp.float32)
    got_gate = terms[0:2] + terms[2:4] + terms[4:6]
    rows_half = gate_grad.shape[1] // 2
    grad_gates[...] = jnp.where(first_half, gate_grad[:, :rows_half], got_gate[:, rows_half:])


def end_call(stay, got, gate_grad):
    half, token_count = stay.shape
    vmem = pl.BlockSpec(memory_space=pltpu.VMEM)
    return pl.pallas_call(
        end_kernel,
        out_shape=(
            jax.ShapeDtypeStruct((half, token_count), jnp.bfloat16),
            jax.ShapeDtypeStruct((half, token_count), jnp.bfloat16),
            jax.ShapeDtypeStruct((2, token_count // 2), jnp.float32),
        ),
        in_specs=[vmem] * 3,
        out_specs=(vmem,) * 3,
        compiler_params=pltpu.CompilerParams(vmem_limit_bytes=16 * MIB),
    )(stay, got, gate_grad)


def plane_body(tokens, expert_ids, priority, gate_values, weight_in, weight_out, cotangent):
    token_count, width = tokens.shape
    dp_count = lax.axis_size("dp")
    experts = dp_count // HBLK
    slot_count = min(token_count, 2 * token_count // experts + max(1, token_count // (4 * experts)))
    capacity = 2 * token_count * dp_count // experts
    contract_first = (((0,), (0,)), ((), ()))
    contract_last = (((1,), (1,)), ((), ()))
    place_dp = lax.axis_index("dp")
    first_half = lax.axis_index("rep") == 0
    plane, quarter = place_dp // HBLK, place_dp % HBLK
    core_zero = quarter % 2 == 0
    groups = GROUPS

    def permutation(move):
        pairs = []
        for z in range(experts):
            for q in range(HBLK):
                for x in range(2):
                    z2, q2, x2 = move(z, q, x)
                    pairs.append((2 * (z * HBLK + q) + x, 2 * (z2 * HBLK + q2) + x2))
        return pairs

    def send(array, move):
        return lax.ppermute(array, ("dp", "rep"), permutation(move))

    def along_first(z, q, x):
        return (z, q, 1 - x) if q % 2 == 0 else (z, q ^ 2, x)

    def along_second(z, q, x):
        return (z, q ^ 2, x) if q % 2 == 0 else (z, q, 1 - x)

    def other_core(z, q, x):
        return (z, q ^ 1, x)

    def other_row(z, q, x):
        return (z, q ^ 2, x)

    def planes_on(k):
        return lambda z, q, x: ((z + k) % experts, q, x)

    def add(*terms):
        return sum(term.astype(jnp.float32) for term in terms).astype(jnp.bfloat16)

    def step(made, *values):
        if made:
            values, _ = lax.optimization_barrier((values, made))
        return values if len(values) > 1 else values[0]

    def join(parts):
        return parts[0] if len(parts) == 1 else jnp.concatenate(parts, axis=0)

    ids, gates = expert_ids.T, gate_values.T
    places, *blocks = start_call(
        ids, priority[None, :], gates, tokens, cotangent, experts, slot_count
    )
    block_rows = blocks[0].shape[0]

    matrix_in = weight_in[0]
    matrix_out = weight_out[0]
    state = [{} for _ in groups]
    home = {}

    def spread_first(g, block):
        one = state[g]
        one["b00"] = block
        one["r1"] = send(block, along_first)
        one["r2"] = send(block, along_second)
        return [one["r1"]]

    def spread_second(g, made):
        one = state[g]
        one["r1"] = step(made, one["r1"])
        one["b11"] = send(one["r1"], along_second)
        return [one["b11"]]

    def gather_near(g, made):
        one = state[g]
        b00, r1, r2, b11 = step(made, one["b00"], one["r1"], one["r2"], one["b11"])
        b10 = jnp.where(core_zero, r2, r1)
        b01 = jnp.where(core_zero, r1, r2)
        one["near"] = jnp.concatenate(
            [
                jnp.where(first_half, b00, b01),
                jnp.where(first_half, b10, b11),
                jnp.where(first_half, b01, b00),
                jnp.where(first_half, b11, b10),
            ],
            axis=0,
        )
        one["far"] = send(one["near"], other_core)
        return [one["near"]]

    def expert_work(g, made, matrix_in, matrix_out):
        one = state[g]
        near_rows, far_rows = step(made, one["near"], one["far"])
        near_parts, far_parts, act, pre = expert_call(near_rows, far_rows, matrix_in, matrix_out)
        one["saved"] = (near_rows, far_rows, act, pre)
        one["near_parts"], one["far_parts"] = near_parts, send(far_parts, other_core)
        return [act]

    def reduce_first(g, made):
        one = state[g]
        sums = add(*step(made, one["near_parts"], one["far_parts"]))
        out0, out1, dx0, dx1 = [
            sums[at * block_rows : at * block_rows + slot_count] for at in range(4)
        ]
        a00, a10 = jnp.where(first_half, out0, dx0), jnp.where(first_half, out1, dx1)
        a01, a11 = jnp.where(first_half, dx0, out0), jnp.where(first_half, dx1, out1)
        away = jnp.concatenate([jnp.where(core_zero, a01, a10), a11], axis=0)
        one["a00"], one["rest"] = a00, jnp.where(core_zero, a10, a01)
        one["back"] = send(away, along_first)
        return [away]

    def reduce_second(g, made):
        one = state[g]
        one["back"], rest = step(made, one["back"], one["rest"])
        last = add(rest, one["back"][slot_count:])
        one["last"] = send(last, along_second)
        return [last]

    def go_home(g, made):
        one = state[g]
        a00, back, last = step(made, one["a00"], one["back"], one["last"])
        (k,) = groups[g]
        done = (
            (a00.astype(jnp.float32) + back[:slot_count].astype(jnp.float32) + last.astype(jnp.float32))
            * mine[g, :slot_count, 0:1]
        ).astype(jnp.bfloat16)
        home[k] = done if k == 0 else send(done, planes_on(experts - k))
        return [done]

    arrived, events = {}, {}
    for entry in PLAN:
        name, g, *after = entry.split()
        g = int(g)
        made = [value for one in after for value in events[one]]
        if name == "Z":
            arrived[g] = send(step(made, blocks[g]), planes_on(g))
            here = [arrived[g]]
        elif name == "D1":
            (k,) = groups[g]
            here = spread_first(g, step(made, arrived[k] if k else blocks[0]))
        elif name == "D2":
            here = spread_second(g, made)
        elif name == "SEL":
            here = gather_near(g, made)
        elif name == "L":
            matrix_in, matrix_out = load_call(matrix_in, matrix_out)
            here = [matrix_out]
        elif name == "E":
            here = expert_work(g, made, matrix_in, matrix_out)
        elif name == "CUT":
            pieces = [piece for one in state for piece in one["saved"][:2]]
            kept, mine = cut_call(step(made, *pieces), slot_count, block_rows, capacity)
            here = [mine]
        elif name == "R1":
            here = reduce_first(g, made)
        elif name == "R2":
            here = reduce_second(g, made)
        elif name == "H":
            here = go_home(g, made)
        elif name == "W":
            saved = [step(made, *one["saved"]) for one in state]
            grad_in, grad_out = weight_call(kept, saved)
            here = [grad_in]
        events[name + str(g)] = here

    away, stay, gate_grad = token_call(gates, places, cotangent, [home[k] for k in range(experts)])
    got = lax.ppermute(away, "rep", [(0, 1), (1, 0)])
    output, grad_tokens, grad_gates = end_call(stay, got, gate_grad)
    return output.T, grad_tokens.T, grad_gates.T, grad_in[None], grad_out[None]


def solution(mesh):
    placed = (
        P("dp", None),
        P("dp", None),
        P("dp"),
        P("dp", None),
        P("dp", None, "rep"),
        P("dp", "rep", None),
        P("dp", None),
    )
    body = plane_body if mesh.shape["rep"] == 2 and mesh.shape["dp"] == 4 * HBLK else general_body
    return jax.shard_map(
        body,
        mesh=mesh,
        in_specs=placed,
        out_specs=(
            P("dp", "rep"),
            P("dp", "rep"),
            P(("dp", "rep"), None),
            P("dp", None, "rep"),
            P("dp", "rep", None),
        ),
        check_vma=False,
    )
```

```python
import functools
import math

import jax
import jax.numpy as jnp
from jax import lax
from jax.experimental import pallas as pl
from jax.experimental.pallas import tpu as pltpu
from jax.sharding import PartitionSpec as P

HBLK = 4
PRIO = 64


def gelu_parts(hidden_pre):
    normal_cdf = 0.5 * (1.0 + jax.scipy.special.erf(hidden_pre * (1.0 / math.sqrt(2.0))))
    density = jnp.exp(-0.5 * hidden_pre * hidden_pre) * (1.0 / math.sqrt(2.0 * math.pi))
    return (hidden_pre * normal_cdf, normal_cdf + hidden_pre * density)


def general_body(tokens, expert_ids, priority, gate_values, weight_in, weight_out, cotangent):
    token_count = tokens.shape[0]
    dp_count = lax.axis_size("dp")
    experts = dp_count // HBLK
    slot_count = min(token_count, 2 * token_count // experts + max(1, token_count // (4 * experts)))
    capacity = 2 * token_count * dp_count // experts
    row_total = dp_count * slot_count
    contract_first = (((0,), (0,)), ((), ()))
    contract_last = (((1,), (1,)), ((), ()))
    priority_key = (
        priority[:, None] + PRIO * (1 - jnp.arange(2, dtype=jnp.int32))[None, :]
    ).reshape(-1)
    flat_expert = expert_ids.reshape(-1)
    expert_hot = (flat_expert[:, None] == jnp.arange(experts, dtype=jnp.int32)[None, :]).astype(
        jnp.int32
    )
    key_hot = (priority_key[:, None] == jnp.arange(2 * PRIO, dtype=jnp.int32)[None, :]).astype(
        jnp.int32
    )
    local_counts = jnp.dot(expert_hot.T, key_hot, preferred_element_type=jnp.int32)
    counts = lax.psum(local_counts, "dp")
    above_count = jnp.cumsum(counts[:, ::-1], axis=1)[:, ::-1]
    cutoff_key = jnp.sum((above_count > capacity).astype(jnp.int32), axis=1)
    kept_mask = priority_key >= jnp.sum(expert_hot * cutoff_key[None, :], axis=1)
    before_count = jnp.cumsum(expert_hot, axis=0) - expert_hot
    slot_index = jnp.sum(expert_hot * before_count, axis=1)
    slot_hot = (slot_index[:, None] == jnp.arange(slot_count, dtype=jnp.int32)[None, :]).astype(
        jnp.int32
    )
    place_map = (
        expert_hot[:, :, None] * slot_hot[:, None, :] * kept_mask.astype(jnp.int32)[:, None, None]
    )
    place_map = place_map.astype(jnp.bfloat16).reshape(2 * token_count, experts * slot_count)
    token_place = jnp.sum(place_map.reshape(token_count, 2, experts * slot_count), axis=1)
    grad_source = (
        gate_values.reshape(-1)[:, None] * jnp.repeat(cotangent, 2, axis=0).astype(jnp.float32)
    ).astype(jnp.bfloat16)
    wide_index = jnp.arange(row_total, dtype=jnp.int32)
    wide_index = wide_index // (HBLK * slot_count) * slot_count + wide_index % slot_count

    def widen(matrix):
        return jnp.take(matrix, wide_index, axis=0)

    send_rows = lax.dot_general(
        token_place, tokens, contract_first, preferred_element_type=jnp.float32
    ).astype(jnp.bfloat16)
    send_grads = lax.dot_general(
        place_map, grad_source, contract_first, preferred_element_type=jnp.float32
    ).astype(jnp.bfloat16)
    rows, grad_rows = (
        lax.all_to_all(widen(send_rows), "dp", split_axis=0, concat_axis=0, tiled=True),
        lax.all_to_all(widen(send_grads), "dp", split_axis=0, concat_axis=0, tiled=True),
    )
    matrix_in = weight_in[0]
    matrix_out = weight_out[0]
    hidden_pre = jnp.dot(rows, matrix_in, preferred_element_type=jnp.float32)
    activation, slope = gelu_parts(hidden_pre)
    activation = activation.astype(jnp.bfloat16)
    partial_out = jnp.dot(activation, matrix_out, preferred_element_type=jnp.float32).astype(
        jnp.bfloat16
    )
    grad_act = lax.dot_general(
        grad_rows, matrix_out, contract_last, preferred_element_type=jnp.float32
    )
    grad_pre = (grad_act * slope).astype(jnp.bfloat16)
    grad_in = lax.dot_general(
        rows, grad_pre, contract_first, preferred_element_type=jnp.float32
    ).astype(jnp.bfloat16)
    grad_out = lax.dot_general(
        activation, grad_rows, contract_first, preferred_element_type=jnp.float32
    ).astype(jnp.bfloat16)
    partial_dx = lax.dot_general(
        grad_pre, matrix_in, contract_last, preferred_element_type=jnp.float32
    ).astype(jnp.bfloat16)
    block_range = jnp.arange(HBLK, dtype=jnp.int32)
    pick_index = (
        (flat_expert[:, None] * HBLK + block_range[None, :]) * slot_count + slot_index[:, None]
    ).reshape(-1)

    def pick_rows(returned):
        width = returned.shape[-1]
        picked = jnp.take(returned, pick_index, axis=0)
        summed = jnp.sum(picked.reshape(2 * token_count, HBLK, width).astype(jnp.float32), axis=1)
        return jnp.where(kept_mask[:, None], summed, 0.0).reshape(token_count, 2, width)

    back_out, back_dx = (
        lax.all_to_all(partial_out, "dp", split_axis=0, concat_axis=0, tiled=True),
        lax.all_to_all(partial_dx, "dp", split_axis=0, concat_axis=0, tiled=True),
    )
    out_rows = pick_rows(back_out)
    dx_rows = pick_rows(back_dx)
    mixed = jnp.sum(gate_values[:, :, None] * out_rows, axis=1)
    token_grad = jnp.sum(dx_rows, axis=1)
    gate_grad = jnp.sum(cotangent.astype(jnp.float32)[:, None, :] * out_rows, axis=2)
    gate_grad = lax.psum_scatter(gate_grad, "rep", scatter_dimension=0, tiled=True)
    mixed, token_grad = (
        lax.psum_scatter(mixed.astype(jnp.bfloat16), "rep", scatter_dimension=1, tiled=True).astype(
            jnp.float32
        ),
        lax.psum_scatter(
            token_grad.astype(jnp.bfloat16), "rep", scatter_dimension=1, tiled=True
        ).astype(jnp.float32),
    )
    return (
        mixed.astype(jnp.bfloat16),
        token_grad.astype(jnp.bfloat16),
        gate_grad,
        grad_in[None],
        grad_out[None],
    )


GROUPS = ((0,), (1,), (3,), (2,))
MIB = 1024 * 1024
WLIM = 32
PLAN = (
    "Z 1",
    "D1 0",
    "Z 3",
    "Z 2",
    "D2 0",
    "L 0",
    "D1 1",
    "SEL 0 L0",
    "D2 1",
    "D1 2",
    "SEL 1",
    "D2 2",
    "D1 3 SEL0",
    "D2 3",
    "SEL 2",
    "E 0",
    "E 1 E0",
    "SEL 3 E0",
    "E 2 E1",
    "R1 1 E2",
    "E 3 R11",
    "CUT 0",
    "R1 2 E3",
    "R1 3 R12",
    "R2 1 R13",
    "R2 2 R21",
    "H 1 R22",
    "R1 0 H1",
    "R2 3 R10",
    "H 2 R23",
    "R2 0 H2",
    "H 3 R20",
    "W 0 H3",
    "H 0 W0",
)


def expert_kernel(near, far, matrix_in, matrix_out, near_parts, far_parts, act, pre):
    half = near.shape[0] // 2
    rows = jnp.concatenate([near[:half], far[:half]], axis=0)
    grads = jnp.concatenate([near[half:], far[half:]], axis=0)
    hidden_pre = jnp.dot(rows, matrix_in[...], preferred_element_type=jnp.float32)
    activation, slope = gelu_parts(hidden_pre)
    grad_act = lax.dot_general(
        grads, matrix_out[...], (((1,), (1,)), ((), ())), preferred_element_type=jnp.float32
    )
    act[...] = activation.astype(jnp.bfloat16)
    pre[...] = (grad_act * slope).astype(jnp.bfloat16)
    out = jnp.dot(act[...], matrix_out[...], preferred_element_type=jnp.float32)
    near_parts[:half] = out[:half].astype(jnp.bfloat16)
    far_parts[:half] = out[half:].astype(jnp.bfloat16)
    back = lax.dot_general(
        pre[...], matrix_in[...], (((1,), (1,)), ((), ())), preferred_element_type=jnp.float32
    )
    near_parts[half:] = back[:half].astype(jnp.bfloat16)
    far_parts[half:] = back[half:].astype(jnp.bfloat16)


def expert_call(near, far, matrix_in, matrix_out):
    rows, width = near.shape
    hidden = matrix_in.shape[1]
    vmem = pl.BlockSpec(memory_space=pltpu.VMEM)
    return pl.pallas_call(
        expert_kernel,
        out_shape=(
            jax.ShapeDtypeStruct((rows, width), jnp.bfloat16),
            jax.ShapeDtypeStruct((rows, width), jnp.bfloat16),
            jax.ShapeDtypeStruct((rows, hidden), jnp.bfloat16),
            jax.ShapeDtypeStruct((rows, hidden), jnp.bfloat16),
        ),
        in_specs=[vmem] * 4,
        out_specs=(vmem,) * 4,
        compiler_params=pltpu.CompilerParams(vmem_limit_bytes=16 * MIB),
        cost_estimate=pl.CostEstimate(flops=0, bytes_accessed=0, transcendentals=0),
    )(near, far, matrix_in, matrix_out)


def start_kernel(experts, ids_at, priority_at, gates_at, tokens_at, cotangent_at, places, *rest):
    blocks, (ids, priority, gates, source, sems) = rest[:experts], rest[experts:]
    slot_count, block_rows = places.shape[2], blocks[0].shape[0]
    token_count = source.shape[0]
    place_dp = lax.axis_index("dp")
    first_half = lax.axis_index("rep") == 0
    small = [
        pltpu.make_async_copy(whole, held, sems.at[i])
        for i, (whole, held) in enumerate(((ids_at, ids), (priority_at, priority), (gates_at, gates)))
    ]
    for copy in small:
        copy.start()

    @pl.when(first_half)
    def _():
        pltpu.make_async_copy(tokens_at, source, sems.at[3]).start()

    @pl.when(jnp.logical_not(first_half))
    def _():
        pltpu.make_async_copy(cotangent_at, source, sems.at[3]).start()

    for copy in small:
        copy.wait()
    row = lax.broadcasted_iota(jnp.int32, (experts, 1), 0)
    near = lax.rem(place_dp // HBLK + row, experts)
    chosen = [ids[j : j + 1] == near for j in range(2)]
    chosen_any = chosen[0] | chosen[1]
    early = lax.broadcasted_iota(jnp.int32, (token_count, token_count), 0)
    late = lax.broadcasted_iota(jnp.int32, (token_count, token_count), 1)
    rank = jnp.dot(
        chosen_any.astype(jnp.bfloat16),
        (early < late).astype(jnp.bfloat16),
        preferred_element_type=jnp.float32,
    ).astype(jnp.int32)
    rank = jnp.where(chosen_any, rank, -1)
    near_gate = jnp.where(chosen[0], gates[0:1], gates[1:2])
    slots = lax.broadcasted_iota(jnp.int32, (slot_count, token_count), 0)
    pltpu.make_async_copy(tokens_at, source, sems.at[3]).wait()
    for k in range(experts):
        spread = rank[k : k + 1] == slots
        rows = jnp.dot(spread.astype(jnp.bfloat16), source[...], preferred_element_type=jnp.float32)
        slot_gate = jnp.sum(jnp.where(spread, near_gate[k : k + 1], 0.0), axis=1, keepdims=True)
        key = 1 + priority[...] + jnp.where(chosen[0][k : k + 1], PRIO, 0)
        slot_key = lax.dot_general(
            key.astype(jnp.bfloat16),
            spread.astype(jnp.bfloat16),
            (((1,), (1,)), ((), ())),
            preferred_element_type=jnp.float32,
        )
        whole = (rows * jnp.where(first_half, 1.0, slot_gate)).astype(jnp.bfloat16)
        spare = jnp.zeros((block_rows - slot_count, rows.shape[1]), jnp.bfloat16)
        blocks[k][...] = jnp.concatenate([whole, spare], axis=0)
        blocks[k][slot_count : slot_count + 1, :slot_count] = slot_key.astype(jnp.bfloat16)
        for j in range(2):
            places[j, k] = (spread & chosen[j][k : k + 1]).astype(jnp.bfloat16)


def start_call(ids, priority, gates, tokens, cotangent, experts, slot_count):
    token_count, width = tokens.shape
    block_rows = (slot_count + 1 + 15) // 16 * 16
    vmem = pl.BlockSpec(memory_space=pltpu.VMEM)
    return pl.pallas_call(
        functools.partial(start_kernel, experts),
        out_shape=(
            jax.ShapeDtypeStruct((2, experts, slot_count, token_count), jnp.bfloat16),
        )
        + (jax.ShapeDtypeStruct((block_rows, width), jnp.bfloat16),) * experts,
        in_specs=[pl.BlockSpec(memory_space=pl.ANY)] * 5,
        out_specs=(vmem,) * (1 + experts),
        scratch_shapes=[
            pltpu.VMEM(ids.shape, jnp.int32),
            pltpu.VMEM(priority.shape, jnp.int32),
            pltpu.VMEM(gates.shape, jnp.float32),
            pltpu.VMEM(tokens.shape, jnp.bfloat16),
            pltpu.SemaphoreType.DMA((4,)),
        ],
        compiler_params=pltpu.CompilerParams(vmem_limit_bytes=56 * MIB),
        cost_estimate=pl.CostEstimate(flops=0, bytes_accessed=0, transcendentals=0),
    )(ids, priority, gates, tokens, cotangent)


def cut_kernel(slot_count, block_rows, capacity, *refs):
    group_count = len(refs) // 2 - 2
    pieces, (kept, mine, keys, sems) = refs[: 2 * group_count], refs[2 * group_count :]
    copies, at = [], 0
    for piece in pieces:
        for block in range(piece.shape[0] // 2 // block_rows):
            last = pl.ds((block + 1) * block_rows - 16, 16)
            copies.append(
                pltpu.make_async_copy(piece.at[last, pl.ds(0, 128)], keys.at[at], sems.at[at])
            )
            at += 1
    for copy in copies:
        copy.start()
    for copy in copies:
        copy.wait()
    row = slot_count - (block_rows - 16)
    rows = [keys[i, row : row + 1, :slot_count].astype(jnp.float32) - 1.0 for i in range(at)]
    levels = lax.broadcasted_iota(jnp.int32, (2 * PRIO, 1), 0).astype(jnp.float32)
    above = sum((one >= levels).astype(jnp.float32) for one in rows)
    above = jnp.sum(above, axis=1, keepdims=True)
    cutoff = jnp.sum((above > capacity).astype(jnp.float32), axis=0, keepdims=True)
    diagonal = lax.broadcasted_iota(
        jnp.int32, (block_rows, slot_count), 0
    ) == lax.broadcasted_iota(jnp.int32, (block_rows, slot_count), 1)
    for i, one in enumerate(rows):
        inside = jnp.where(diagonal & (one >= cutoff), 1.0, 0.0)
        column = jnp.sum(inside, axis=1, keepdims=True)
        kept[i * block_rows : (i + 1) * block_rows] = jnp.broadcast_to(column, (block_rows, 128)).astype(jnp.bfloat16)
        if i % (at // group_count) == 0:
            g = i // (at // group_count)
            mine[g] = jnp.broadcast_to(column, (block_rows, 128))


def cut_call(pieces, slot_count, block_rows, capacity):
    total = sum(piece.shape[0] // 2 for piece in pieces)
    vmem = pl.BlockSpec(memory_space=pltpu.VMEM)
    return pl.pallas_call(
        functools.partial(cut_kernel, slot_count, block_rows, capacity),
        out_shape=(
            jax.ShapeDtypeStruct((total, 128), jnp.bfloat16),
            jax.ShapeDtypeStruct((len(pieces) // 2, block_rows, 128), jnp.float32),
        ),
        in_specs=[pl.BlockSpec(memory_space=pl.ANY)] * len(pieces),
        out_specs=(vmem,) * 2,
        scratch_shapes=[
            pltpu.VMEM((total // block_rows, 16, 128), jnp.bfloat16),
            pltpu.SemaphoreType.DMA((total // block_rows,)),
        ],
        compiler_params=pltpu.CompilerParams(vmem_limit_bytes=8 * MIB),
        cost_estimate=pl.CostEstimate(flops=0, bytes_accessed=0, transcendentals=0),
    )(*pieces)


def weight_kernel(kept, *refs):
    group_count = (len(refs) - 10) // 4
    pieces, out_at = refs[: 4 * group_count], refs[4 * group_count : 4 * group_count + 2]
    rows, grads, act, pre, grad_in, grad_out, sems, out_sems = refs[4 * group_count + 2 :]
    steps, base = ([], [], [], []), 0
    for g in range(group_count):
        near, far, act_at, pre_at = pieces[4 * g : 4 * g + 4]
        count = near.shape[0]
        half = count // 2
        for slot, (whole, to) in enumerate(((pre_at, pre), (act_at, act))):
            steps[2 * slot].append(
                pltpu.make_async_copy(whole, to.at[pl.ds(base, count)], sems.at[g, 3 * slot])
            )
        for part, whole in enumerate((near, far)):
            for kind, to in enumerate((rows, grads)):
                steps[2 * kind + 1].append(
                    pltpu.make_async_copy(
                        whole.at[pl.ds(kind * half, half)],
                        to.at[pl.ds(base + part * half, half)],
                        sems.at[g, 3 * kind + 1 + part],
                    )
                )
        base += count
    for copies in steps:
        for copy in copies:
            copy.start()
    contract_first = (((0,), (0,)), ((), ()))
    keep = kept[:, 0:1]
    width = rows.shape[1]
    sent = []

    for copy in steps[0]:
        copy.wait()
    pre[...] = pre[...] * keep
    for copy in steps[1]:
        copy.wait()
    for first in range(0, width, 256):
        span = slice(first, min(width, first + 256))
        grad_in[span] = lax.dot_general(
            rows[:, span], pre[...], contract_first, preferred_element_type=jnp.float32
        ).astype(jnp.bfloat16)
    sent.append(pltpu.make_async_copy(grad_in, out_at[0], out_sems.at[0]))
    sent[-1].start()
    for copy in steps[2]:
        copy.wait()
    act[...] = act[...] * keep
    for copy in steps[3]:
        copy.wait()
    for first in range(0, width, 256):
        span = slice(first, min(width, first + 256))
        grad_out[:, span] = lax.dot_general(
            act[...], grads[:, span], contract_first, preferred_element_type=jnp.float32
        ).astype(jnp.bfloat16)
    sent.append(pltpu.make_async_copy(grad_out, out_at[1], out_sems.at[1]))
    sent[-1].start()
    for copy in sent:
        copy.wait()


def weight_call(kept, saved):
    pieces = [piece for one in saved for piece in one]
    width, hidden = pieces[0].shape[1], pieces[2].shape[1]
    all_rows = sum(one[2].shape[0] for one in saved)
    vmem, anywhere = pl.BlockSpec(memory_space=pltpu.VMEM), pl.BlockSpec(memory_space=pl.ANY)
    return pl.pallas_call(
        weight_kernel,
        out_shape=(
            jax.ShapeDtypeStruct((width, hidden), jnp.bfloat16),
            jax.ShapeDtypeStruct((hidden, width), jnp.bfloat16),
        ),
        in_specs=[vmem] + [anywhere] * len(pieces),
        out_specs=(anywhere,) * 2,
        scratch_shapes=[pltpu.VMEM((all_rows, width), jnp.bfloat16)] * 2
        + [pltpu.VMEM((all_rows, hidden), jnp.bfloat16)] * 2
        + [pltpu.VMEM((width, hidden), jnp.bfloat16), pltpu.VMEM((hidden, width), jnp.bfloat16)]
        + [pltpu.SemaphoreType.DMA((len(saved), 6)), pltpu.SemaphoreType.DMA((2,))],
        compiler_params=pltpu.CompilerParams(vmem_limit_bytes=WLIM * MIB),
        cost_estimate=pl.CostEstimate(flops=0, bytes_accessed=0, transcendentals=0),
    )(kept, *pieces)


def load_kernel(in_at, out_at, matrix_in, matrix_out, sems):
    copies = [
        pltpu.make_async_copy(in_at, matrix_in, sems.at[0]),
        pltpu.make_async_copy(out_at, matrix_out, sems.at[1]),
    ]
    for copy in copies:
        copy.start()
    for copy in copies:
        copy.wait()


def load_call(matrix_in, matrix_out):
    vmem, anywhere = pl.BlockSpec(memory_space=pltpu.VMEM), pl.BlockSpec(memory_space=pl.ANY)
    return pl.pallas_call(
        load_kernel,
        out_shape=tuple(
            jax.ShapeDtypeStruct(one.shape, one.dtype) for one in (matrix_in, matrix_out)
        ),
        in_specs=[anywhere] * 2,
        out_specs=(vmem,) * 2,
        scratch_shapes=[pltpu.SemaphoreType.DMA((2,))],
        compiler_params=pltpu.CompilerParams(vmem_limit_bytes=8 * MIB),
        cost_estimate=pl.CostEstimate(flops=0, bytes_accessed=0, transcendentals=0),
    )(matrix_in, matrix_out)


def token_kernel(gates, places, cotangent, *refs):
    homes, (away, stay, gate_grad) = refs[:-3], refs[-3:]
    first_half = lax.axis_index("rep") == 0
    token_count, width = cotangent.shape
    half = width // 2
    diagonal = lax.broadcasted_iota(
        jnp.int32, (token_count, token_count), 0
    ) == lax.broadcasted_iota(jnp.int32, (token_count, token_count), 1)
    back = jnp.concatenate([one[...] for one in homes], axis=0)
    mixed, sums = 0.0, []
    for j in range(2):
        picker = jnp.concatenate([places[j, k] for k in range(len(homes))], axis=0)
        picked = lax.dot_general(
            picker, back, (((0,), (0,)), ((), ())), preferred_element_type=jnp.float32
        )
        gate = jnp.sum(jnp.where(diagonal, gates[j : j + 1], 0.0), axis=1, keepdims=True)
        mixed = mixed + picked * jnp.where(first_half, gate, 1.0)
        inner = jnp.sum(picked * cotangent[...].astype(jnp.float32), axis=1, keepdims=True)
        sums.append(jnp.sum(jnp.where(diagonal, inner, 0.0), axis=0, keepdims=True))
    mixed = mixed.astype(jnp.bfloat16).T
    upper, lower = mixed[:half], mixed[half:]
    away[:half] = jnp.where(first_half, lower, upper)
    stay[...] = jnp.where(first_half, upper, lower)
    left = jnp.concatenate(sums, axis=0)
    gate_grad[...] = left
    terms = []
    for _ in range(3):
        terms.append(left.astype(jnp.bfloat16))
        left = left - terms[-1].astype(jnp.float32)
    terms.append(jnp.zeros((away.shape[0] - half - 6, token_count), jnp.bfloat16))
    away[half:] = jnp.concatenate(terms, axis=0)


def token_call(gates, places, cotangent, homes):
    token_count, width = cotangent.shape
    vmem = pl.BlockSpec(memory_space=pltpu.VMEM)
    return pl.pallas_call(
        token_kernel,
        out_shape=(
            jax.ShapeDtypeStruct((width // 2 + 16, token_count), jnp.bfloat16),
            jax.ShapeDtypeStruct((width // 2, token_count), jnp.bfloat16),
            jax.ShapeDtypeStruct((2, token_count), jnp.float32),
        ),
        in_specs=[vmem] * (3 + len(homes)),
        out_specs=(vmem,) * 3,
        compiler_params=pltpu.CompilerParams(vmem_limit_bytes=16 * MIB),
        cost_estimate=pl.CostEstimate(flops=0, bytes_accessed=0, transcendentals=0),
    )(gates, places, cotangent, *homes)


def end_kernel(stay, got, gate_grad, output, grad_tokens, grad_gates):
    first_half = lax.axis_index("rep") == 0
    half = stay.shape[0]
    mine, theirs = stay[...], got[:half]
    output[...] = jnp.where(first_half, mine, theirs)
    grad_tokens[...] = jnp.where(first_half, theirs, mine)
    terms = got[half:].astype(jnp.float32)
    got_gate = terms[0:2] + terms[2:4] + terms[4:6]
    rows_half = gate_grad.shape[1] // 2
    grad_gates[...] = jnp.where(first_half, gate_grad[:, :rows_half], got_gate[:, rows_half:])


def end_call(stay, got, gate_grad):
    half, token_count = stay.shape
    vmem = pl.BlockSpec(memory_space=pltpu.VMEM)
    return pl.pallas_call(
        end_kernel,
        out_shape=(
            jax.ShapeDtypeStruct((half, token_count), jnp.bfloat16),
            jax.ShapeDtypeStruct((half, token_count), jnp.bfloat16),
            jax.ShapeDtypeStruct((2, token_count // 2), jnp.float32),
        ),
        in_specs=[vmem] * 3,
        out_specs=(vmem,) * 3,
        compiler_params=pltpu.CompilerParams(vmem_limit_bytes=16 * MIB),
    )(stay, got, gate_grad)


def plane_body(tokens, expert_ids, priority, gate_values, weight_in, weight_out, cotangent):
    token_count, width = tokens.shape
    dp_count = lax.axis_size("dp")
    experts = dp_count // HBLK
    slot_count = min(token_count, 2 * token_count // experts + max(1, token_count // (4 * experts)))
    capacity = 2 * token_count * dp_count // experts
    contract_first = (((0,), (0,)), ((), ()))
    contract_last = (((1,), (1,)), ((), ()))
    place_dp = lax.axis_index("dp")
    first_half = lax.axis_index("rep") == 0
    plane, quarter = place_dp // HBLK, place_dp % HBLK
    core_zero = quarter % 2 == 0
    groups = GROUPS

    def permutation(move):
        pairs = []
        for z in range(experts):
            for q in range(HBLK):
                for x in range(2):
                    z2, q2, x2 = move(z, q, x)
                    pairs.append((2 * (z * HBLK + q) + x, 2 * (z2 * HBLK + q2) + x2))
        return pairs

    def send(array, move):
        return lax.ppermute(array, ("dp", "rep"), permutation(move))

    def along_first(z, q, x):
        return (z, q, 1 - x) if q % 2 == 0 else (z, q ^ 2, x)

    def along_second(z, q, x):
        return (z, q ^ 2, x) if q % 2 == 0 else (z, q, 1 - x)

    def other_core(z, q, x):
        return (z, q ^ 1, x)

    def other_row(z, q, x):
        return (z, q ^ 2, x)

    def planes_on(k):
        return lambda z, q, x: ((z + k) % experts, q, x)

    def add(*terms):
        return sum(term.astype(jnp.float32) for term in terms).astype(jnp.bfloat16)

    def step(made, *values):
        if made:
            values, _ = lax.optimization_barrier((values, made))
        return values if len(values) > 1 else values[0]

    def join(parts):
        return parts[0] if len(parts) == 1 else jnp.concatenate(parts, axis=0)

    ids, gates = expert_ids.T, gate_values.T
    places, *blocks = start_call(
        ids, priority[None, :], gates, tokens, cotangent, experts, slot_count
    )
    block_rows = blocks[0].shape[0]

    matrix_in = weight_in[0]
    matrix_out = weight_out[0]
    state = [{} for _ in groups]
    home = {}

    def spread_first(g, block):
        one = state[g]
        one["b00"] = block
        one["r1"] = send(block, along_first)
        one["r2"] = send(block, along_second)
        return [one["r1"]]

    def spread_second(g, made):
        one = state[g]
        one["r1"] = step(made, one["r1"])
        one["b11"] = send(one["r1"], along_second)
        return [one["b11"]]

    def gather_near(g, made):
        one = state[g]
        b00, r1, r2, b11 = step(made, one["b00"], one["r1"], one["r2"], one["b11"])
        b10 = jnp.where(core_zero, r2, r1)
        b01 = jnp.where(core_zero, r1, r2)
        one["near"] = jnp.concatenate(
            [
                jnp.where(first_half, b00, b01),
                jnp.where(first_half, b10, b11),
                jnp.where(first_half, b01, b00),
                jnp.where(first_half, b11, b10),
            ],
            axis=0,
        )
        one["far"] = send(one["near"], other_core)
        return [one["near"]]

    def expert_work(g, made, matrix_in, matrix_out):
        one = state[g]
        near_rows, far_rows = step(made, one["near"], one["far"])
        near_parts, far_parts, act, pre = expert_call(near_rows, far_rows, matrix_in, matrix_out)
        one["saved"] = (near_rows, far_rows, act, pre)
        one["near_parts"], one["far_parts"] = near_parts, send(far_parts, other_core)
        return [act]

    def reduce_first(g, made):
        one = state[g]
        sums = add(*step(made, one["near_parts"], one["far_parts"]))
        out0, out1, dx0, dx1 = [
            sums[at * block_rows : at * block_rows + slot_count] for at in range(4)
        ]
        a00, a10 = jnp.where(first_half, out0, dx0), jnp.where(first_half, out1, dx1)
        a01, a11 = jnp.where(first_half, dx0, out0), jnp.where(first_half, dx1, out1)
        away = jnp.concatenate([jnp.where(core_zero, a01, a10), a11], axis=0)
        one["a00"], one["rest"] = a00, jnp.where(core_zero, a10, a01)
        one["back"] = send(away, along_first)
        return [away]

    def reduce_second(g, made):
        one = state[g]
        one["back"], rest = step(made, one["back"], one["rest"])
        last = add(rest, one["back"][slot_count:])
        one["last"] = send(last, along_second)
        return [last]

    def go_home(g, made):
        one = state[g]
        a00, back, last = step(made, one["a00"], one["back"], one["last"])
        (k,) = groups[g]
        done = (
            (a00.astype(jnp.float32) + back[:slot_count].astype(jnp.float32) + last.astype(jnp.float32))
            * mine[g, :slot_count, 0:1]
        ).astype(jnp.bfloat16)
        home[k] = done if k == 0 else send(done, planes_on(experts - k))
        return [done]

    arrived, events = {}, {}
    for entry in PLAN:
        name, g, *after = entry.split()
        g = int(g)
        made = [value for one in after for value in events[one]]
        if name == "Z":
            arrived[g] = send(step(made, blocks[g]), planes_on(g))
            here = [arrived[g]]
        elif name == "D1":
            (k,) = groups[g]
            here = spread_first(g, step(made, arrived[k] if k else blocks[0]))
        elif name == "D2":
            here = spread_second(g, made)
        elif name == "SEL":
            here = gather_near(g, made)
        elif name == "L":
            matrix_in, matrix_out = load_call(matrix_in, matrix_out)
            here = [matrix_out]
        elif name == "E":
            here = expert_work(g, made, matrix_in, matrix_out)
        elif name == "CUT":
            pieces = [piece for one in state for piece in one["saved"][:2]]
            kept, mine = cut_call(step(made, *pieces), slot_count, block_rows, capacity)
            here = [mine]
        elif name == "R1":
            here = reduce_first(g, made)
        elif name == "R2":
            here = reduce_second(g, made)
        elif name == "H":
            here = go_home(g, made)
        elif name == "W":
            saved = [step(made, *one["saved"]) for one in state]
            grad_in, grad_out = weight_call(kept, saved)
            here = [grad_in]
        events[name + str(g)] = here

    away, stay, gate_grad = token_call(gates, places, cotangent, [home[k] for k in range(experts)])
    got = lax.ppermute(away, "rep", [(0, 1), (1, 0)])
    output, grad_tokens, grad_gates = end_call(stay, got, gate_grad)
    return output.T, grad_tokens.T, grad_gates.T, grad_in[None], grad_out[None]


def solution(mesh):
    placed = (
        P("dp", None),
        P("dp", None),
        P("dp"),
        P("dp", None),
        P("dp", None, "rep"),
        P("dp", "rep", None),
        P("dp", None),
    )
    body = plane_body if mesh.shape["rep"] == 2 and mesh.shape["dp"] == 4 * HBLK else general_body
    return jax.shard_map(
        body,
        mesh=mesh,
        in_specs=placed,
        out_specs=(
            P("dp", "rep"),
            P("dp", "rep"),
            P(("dp", "rep"), None),
            P("dp", None, "rep"),
            P("dp", "rep", None),
        ),
        check_vma=False,
    )
```

```python
import functools
import math

import jax
import jax.numpy as jnp
from jax import lax
from jax.experimental import pallas as pl
from jax.experimental.pallas import tpu as pltpu
from jax.sharding import PartitionSpec as P

HBLK = 4
PRIO = 64


def gelu_parts(hidden_pre):
    normal_cdf = 0.5 * (1.0 + jax.scipy.special.erf(hidden_pre * (1.0 / math.sqrt(2.0))))
    density = jnp.exp(-0.5 * hidden_pre * hidden_pre) * (1.0 / math.sqrt(2.0 * math.pi))
    return (hidden_pre * normal_cdf, normal_cdf + hidden_pre * density)


def general_body(tokens, expert_ids, priority, gate_values, weight_in, weight_out, cotangent):
    token_count = tokens.shape[0]
    dp_count = lax.axis_size("dp")
    experts = dp_count // HBLK
    slot_count = min(token_count, 2 * token_count // experts + max(1, token_count // (4 * experts)))
    capacity = 2 * token_count * dp_count // experts
    row_total = dp_count * slot_count
    contract_first = (((0,), (0,)), ((), ()))
    contract_last = (((1,), (1,)), ((), ()))
    priority_key = (
        priority[:, None] + PRIO * (1 - jnp.arange(2, dtype=jnp.int32))[None, :]
    ).reshape(-1)
    flat_expert = expert_ids.reshape(-1)
    expert_hot = (flat_expert[:, None] == jnp.arange(experts, dtype=jnp.int32)[None, :]).astype(
        jnp.int32
    )
    key_hot = (priority_key[:, None] == jnp.arange(2 * PRIO, dtype=jnp.int32)[None, :]).astype(
        jnp.int32
    )
    local_counts = jnp.dot(expert_hot.T, key_hot, preferred_element_type=jnp.int32)
    counts = lax.psum(local_counts, "dp")
    above_count = jnp.cumsum(counts[:, ::-1], axis=1)[:, ::-1]
    cutoff_key = jnp.sum((above_count > capacity).astype(jnp.int32), axis=1)
    kept_mask = priority_key >= jnp.sum(expert_hot * cutoff_key[None, :], axis=1)
    before_count = jnp.cumsum(expert_hot, axis=0) - expert_hot
    slot_index = jnp.sum(expert_hot * before_count, axis=1)
    slot_hot = (slot_index[:, None] == jnp.arange(slot_count, dtype=jnp.int32)[None, :]).astype(
        jnp.int32
    )
    place_map = (
        expert_hot[:, :, None] * slot_hot[:, None, :] * kept_mask.astype(jnp.int32)[:, None, None]
    )
    place_map = place_map.astype(jnp.bfloat16).reshape(2 * token_count, experts * slot_count)
    token_place = jnp.sum(place_map.reshape(token_count, 2, experts * slot_count), axis=1)
    grad_source = (
        gate_values.reshape(-1)[:, None] * jnp.repeat(cotangent, 2, axis=0).astype(jnp.float32)
    ).astype(jnp.bfloat16)
    wide_index = jnp.arange(row_total, dtype=jnp.int32)
    wide_index = wide_index // (HBLK * slot_count) * slot_count + wide_index % slot_count

    def widen(matrix):
        return jnp.take(matrix, wide_index, axis=0)

    send_rows = lax.dot_general(
        token_place, tokens, contract_first, preferred_element_type=jnp.float32
    ).astype(jnp.bfloat16)
    send_grads = lax.dot_general(
        place_map, grad_source, contract_first, preferred_element_type=jnp.float32
    ).astype(jnp.bfloat16)
    rows, grad_rows = (
        lax.all_to_all(widen(send_rows), "dp", split_axis=0, concat_axis=0, tiled=True),
        lax.all_to_all(widen(send_grads), "dp", split_axis=0, concat_axis=0, tiled=True),
    )
    matrix_in = weight_in[0]
    matrix_out = weight_out[0]
    hidden_pre = jnp.dot(rows, matrix_in, preferred_element_type=jnp.float32)
    activation, slope = gelu_parts(hidden_pre)
    activation = activation.astype(jnp.bfloat16)
    partial_out = jnp.dot(activation, matrix_out, preferred_element_type=jnp.float32).astype(
        jnp.bfloat16
    )
    grad_act = lax.dot_general(
        grad_rows, matrix_out, contract_last, preferred_element_type=jnp.float32
    )
    grad_pre = (grad_act * slope).astype(jnp.bfloat16)
    grad_in = lax.dot_general(
        rows, grad_pre, contract_first, preferred_element_type=jnp.float32
    ).astype(jnp.bfloat16)
    grad_out = lax.dot_general(
        activation, grad_rows, contract_first, preferred_element_type=jnp.float32
    ).astype(jnp.bfloat16)
    partial_dx = lax.dot_general(
        grad_pre, matrix_in, contract_last, preferred_element_type=jnp.float32
    ).astype(jnp.bfloat16)
    block_range = jnp.arange(HBLK, dtype=jnp.int32)
    pick_index = (
        (flat_expert[:, None] * HBLK + block_range[None, :]) * slot_count + slot_index[:, None]
    ).reshape(-1)

    def pick_rows(returned):
        width = returned.shape[-1]
        picked = jnp.take(returned, pick_index, axis=0)
        summed = jnp.sum(picked.reshape(2 * token_count, HBLK, width).astype(jnp.float32), axis=1)
        return jnp.where(kept_mask[:, None], summed, 0.0).reshape(token_count, 2, width)

    back_out, back_dx = (
        lax.all_to_all(partial_out, "dp", split_axis=0, concat_axis=0, tiled=True),
        lax.all_to_all(partial_dx, "dp", split_axis=0, concat_axis=0, tiled=True),
    )
    out_rows = pick_rows(back_out)
    dx_rows = pick_rows(back_dx)
    mixed = jnp.sum(gate_values[:, :, None] * out_rows, axis=1)
    token_grad = jnp.sum(dx_rows, axis=1)
    gate_grad = jnp.sum(cotangent.astype(jnp.float32)[:, None, :] * out_rows, axis=2)
    gate_grad = lax.psum_scatter(gate_grad, "rep", scatter_dimension=0, tiled=True)
    mixed, token_grad = (
        lax.psum_scatter(mixed.astype(jnp.bfloat16), "rep", scatter_dimension=1, tiled=True).astype(
            jnp.float32
        ),
        lax.psum_scatter(
            token_grad.astype(jnp.bfloat16), "rep", scatter_dimension=1, tiled=True
        ).astype(jnp.float32),
    )
    return (
        mixed.astype(jnp.bfloat16),
        token_grad.astype(jnp.bfloat16),
        gate_grad,
        grad_in[None],
        grad_out[None],
    )


GROUPS = ((0,), (1,), (3,), (2,))
MIB = 1024 * 1024
WLIM = 24
PLAN = (
    "Z 1",
    "D1 0",
    "Z 3",
    "Z 2",
    "D2 0",
    "L 0",
    "D1 1",
    "SEL 0 L0",
    "D2 1",
    "D1 2",
    "SEL 1",
    "D2 2",
    "D1 3 SEL0",
    "D2 3",
    "SEL 2",
    "E 0",
    "E 1 E0",
    "SEL 3 E0",
    "E 2 E1",
    "R1 1 E2",
    "E 3 R11",
    "CUT 0",
    "R1 2 E3",
    "R1 3 R12",
    "R2 1 R13",
    "R2 2 R21",
    "H 1 R22",
    "R1 0 H1",
    "R2 3 R10",
    "H 2 R23",
    "R2 0 H2",
    "H 3 R20",
    "W 0 H3",
    "H 0 W0",
)


def expert_kernel(near, far, matrix_in, matrix_out, near_parts, far_parts, act, pre):
    half = near.shape[0] // 2
    rows = jnp.concatenate([near[:half], far[:half]], axis=0)
    grads = jnp.concatenate([near[half:], far[half:]], axis=0)
    hidden_pre = jnp.dot(rows, matrix_in[...], preferred_element_type=jnp.float32)
    activation, slope = gelu_parts(hidden_pre)
    grad_act = lax.dot_general(
        grads, matrix_out[...], (((1,), (1,)), ((), ())), preferred_element_type=jnp.float32
    )
    act[...] = activation.astype(jnp.bfloat16)
    pre[...] = (grad_act * slope).astype(jnp.bfloat16)
    out = jnp.dot(act[...], matrix_out[...], preferred_element_type=jnp.float32)
    near_parts[:half] = out[:half].astype(jnp.bfloat16)
    far_parts[:half] = out[half:].astype(jnp.bfloat16)
    back = lax.dot_general(
        pre[...], matrix_in[...], (((1,), (1,)), ((), ())), preferred_element_type=jnp.float32
    )
    near_parts[half:] = back[:half].astype(jnp.bfloat16)
    far_parts[half:] = back[half:].astype(jnp.bfloat16)


def expert_call(near, far, matrix_in, matrix_out):
    rows, width = near.shape
    hidden = matrix_in.shape[1]
    vmem = pl.BlockSpec(memory_space=pltpu.VMEM)
    return pl.pallas_call(
        expert_kernel,
        out_shape=(
            jax.ShapeDtypeStruct((rows, width), jnp.bfloat16),
            jax.ShapeDtypeStruct((rows, width), jnp.bfloat16),
            jax.ShapeDtypeStruct((rows, hidden), jnp.bfloat16),
            jax.ShapeDtypeStruct((rows, hidden), jnp.bfloat16),
        ),
        in_specs=[vmem] * 4,
        out_specs=(vmem,) * 4,
        compiler_params=pltpu.CompilerParams(vmem_limit_bytes=16 * MIB),
        cost_estimate=pl.CostEstimate(flops=0, bytes_accessed=0, transcendentals=0),
    )(near, far, matrix_in, matrix_out)


def start_kernel(experts, ids_at, priority_at, gates_at, tokens_at, cotangent_at, places, *rest):
    blocks, (ids, priority, gates, source, sems) = rest[:experts], rest[experts:]
    slot_count, block_rows = places.shape[2], blocks[0].shape[0]
    token_count = source.shape[0]
    place_dp = lax.axis_index("dp")
    first_half = lax.axis_index("rep") == 0
    small = [
        pltpu.make_async_copy(whole, held, sems.at[i])
        for i, (whole, held) in enumerate(((ids_at, ids), (priority_at, priority), (gates_at, gates)))
    ]
    for copy in small:
        copy.start()

    @pl.when(first_half)
    def _():
        pltpu.make_async_copy(tokens_at, source, sems.at[3]).start()

    @pl.when(jnp.logical_not(first_half))
    def _():
        pltpu.make_async_copy(cotangent_at, source, sems.at[3]).start()

    for copy in small:
        copy.wait()
    row = lax.broadcasted_iota(jnp.int32, (experts, 1), 0)
    near = lax.rem(place_dp // HBLK + row, experts)
    chosen = [ids[j : j + 1] == near for j in range(2)]
    chosen_any = chosen[0] | chosen[1]
    early = lax.broadcasted_iota(jnp.int32, (token_count, token_count), 0)
    late = lax.broadcasted_iota(jnp.int32, (token_count, token_count), 1)
    rank = jnp.dot(
        chosen_any.astype(jnp.bfloat16),
        (early < late).astype(jnp.bfloat16),
        preferred_element_type=jnp.float32,
    ).astype(jnp.int32)
    rank = jnp.where(chosen_any, rank, -1)
    near_gate = jnp.where(chosen[0], gates[0:1], gates[1:2])
    slots = lax.broadcasted_iota(jnp.int32, (slot_count, token_count), 0)
    pltpu.make_async_copy(tokens_at, source, sems.at[3]).wait()
    for k in range(experts):
        spread = rank[k : k + 1] == slots
        rows = jnp.dot(spread.astype(jnp.bfloat16), source[...], preferred_element_type=jnp.float32)
        slot_gate = jnp.sum(jnp.where(spread, near_gate[k : k + 1], 0.0), axis=1, keepdims=True)
        key = 1 + priority[...] + jnp.where(chosen[0][k : k + 1], PRIO, 0)
        slot_key = lax.dot_general(
            key.astype(jnp.bfloat16),
            spread.astype(jnp.bfloat16),
            (((1,), (1,)), ((), ())),
            preferred_element_type=jnp.float32,
        )
        whole = (rows * jnp.where(first_half, 1.0, slot_gate)).astype(jnp.bfloat16)
        spare = jnp.zeros((block_rows - slot_count, rows.shape[1]), jnp.bfloat16)
        blocks[k][...] = jnp.concatenate([whole, spare], axis=0)
        blocks[k][slot_count : slot_count + 1, :slot_count] = slot_key.astype(jnp.bfloat16)
        for j in range(2):
            places[j, k] = (spread & chosen[j][k : k + 1]).astype(jnp.bfloat16)


def start_call(ids, priority, gates, tokens, cotangent, experts, slot_count):
    token_count, width = tokens.shape
    block_rows = (slot_count + 1 + 15) // 16 * 16
    vmem = pl.BlockSpec(memory_space=pltpu.VMEM)
    return pl.pallas_call(
        functools.partial(start_kernel, experts),
        out_shape=(
            jax.ShapeDtypeStruct((2, experts, slot_count, token_count), jnp.bfloat16),
        )
        + (jax.ShapeDtypeStruct((block_rows, width), jnp.bfloat16),) * experts,
        in_specs=[pl.BlockSpec(memory_space=pl.ANY)] * 5,
        out_specs=(vmem,) * (1 + experts),
        scratch_shapes=[
            pltpu.VMEM(ids.shape, jnp.int32),
            pltpu.VMEM(priority.shape, jnp.int32),
            pltpu.VMEM(gates.shape, jnp.float32),
            pltpu.VMEM(tokens.shape, jnp.bfloat16),
            pltpu.SemaphoreType.DMA((4,)),
        ],
        compiler_params=pltpu.CompilerParams(vmem_limit_bytes=56 * MIB),
        cost_estimate=pl.CostEstimate(flops=0, bytes_accessed=0, transcendentals=0),
    )(ids, priority, gates, tokens, cotangent)


def cut_kernel(slot_count, block_rows, capacity, *refs):
    group_count = len(refs) // 2 - 2
    pieces, (kept, mine, keys, sems) = refs[: 2 * group_count], refs[2 * group_count :]
    copies, at = [], 0
    for piece in pieces:
        for block in range(piece.shape[0] // 2 // block_rows):
            last = pl.ds((block + 1) * block_rows - 16, 16)
            copies.append(
                pltpu.make_async_copy(piece.at[last, pl.ds(0, 128)], keys.at[at], sems.at[at])
            )
            at += 1
    for copy in copies:
        copy.start()
    for copy in copies:
        copy.wait()
    row = slot_count - (block_rows - 16)
    rows = [keys[i, row : row + 1, :slot_count].astype(jnp.float32) - 1.0 for i in range(at)]
    levels = lax.broadcasted_iota(jnp.int32, (2 * PRIO, 1), 0).astype(jnp.float32)
    above = sum((one >= levels).astype(jnp.float32) for one in rows)
    above = jnp.sum(above, axis=1, keepdims=True)
    cutoff = jnp.sum((above > capacity).astype(jnp.float32), axis=0, keepdims=True)
    diagonal = lax.broadcasted_iota(
        jnp.int32, (block_rows, slot_count), 0
    ) == lax.broadcasted_iota(jnp.int32, (block_rows, slot_count), 1)
    for i, one in enumerate(rows):
        inside = jnp.where(diagonal & (one >= cutoff), 1.0, 0.0)
        column = jnp.sum(inside, axis=1, keepdims=True)
        kept[i * block_rows : (i + 1) * block_rows] = jnp.broadcast_to(column, (block_rows, 128)).astype(jnp.bfloat16)
        if i % (at // group_count) == 0:
            g = i // (at // group_count)
            mine[g] = jnp.broadcast_to(column, (block_rows, 128))


def cut_call(pieces, slot_count, block_rows, capacity):
    total = sum(piece.shape[0] // 2 for piece in pieces)
    vmem = pl.BlockSpec(memory_space=pltpu.VMEM)
    return pl.pallas_call(
        functools.partial(cut_kernel, slot_count, block_rows, capacity),
        out_shape=(
            jax.ShapeDtypeStruct((total, 128), jnp.bfloat16),
            jax.ShapeDtypeStruct((len(pieces) // 2, block_rows, 128), jnp.float32),
        ),
        in_specs=[pl.BlockSpec(memory_space=pl.ANY)] * len(pieces),
        out_specs=(vmem,) * 2,
        scratch_shapes=[
            pltpu.VMEM((total // block_rows, 16, 128), jnp.bfloat16),
            pltpu.SemaphoreType.DMA((total // block_rows,)),
        ],
        compiler_params=pltpu.CompilerParams(vmem_limit_bytes=8 * MIB),
        cost_estimate=pl.CostEstimate(flops=0, bytes_accessed=0, transcendentals=0),
    )(*pieces)


def weight_kernel(kept, *refs):
    group_count = (len(refs) - 10) // 4
    pieces, out_at = refs[: 4 * group_count], refs[4 * group_count : 4 * group_count + 2]
    rows, grads, act, pre, grad_in, grad_out, sems, out_sems = refs[4 * group_count + 2 :]
    steps, base = ([], [], [], []), 0
    for g in range(group_count):
        near, far, act_at, pre_at = pieces[4 * g : 4 * g + 4]
        count = near.shape[0]
        half = count // 2
        for slot, (whole, to) in enumerate(((pre_at, pre), (act_at, act))):
            steps[2 * slot].append(
                pltpu.make_async_copy(whole, to.at[pl.ds(base, count)], sems.at[g, 3 * slot])
            )
        for part, whole in enumerate((near, far)):
            for kind, to in enumerate((rows, grads)):
                steps[2 * kind + 1].append(
                    pltpu.make_async_copy(
                        whole.at[pl.ds(kind * half, half)],
                        to.at[pl.ds(base + part * half, half)],
                        sems.at[g, 3 * kind + 1 + part],
                    )
                )
        base += count
    for copies in steps:
        for copy in copies:
            copy.start()
    contract_first = (((0,), (0,)), ((), ()))
    keep = kept[:, 0:1]
    width = rows.shape[1]
    sent = []

    for copy in steps[0]:
        copy.wait()
    pre[...] = pre[...] * keep
    for copy in steps[1]:
        copy.wait()
    for first in range(0, width, 256):
        span = slice(first, min(width, first + 256))
        grad_in[span] = lax.dot_general(
            rows[:, span], pre[...], contract_first, preferred_element_type=jnp.float32
        ).astype(jnp.bfloat16)
    sent.append(pltpu.make_async_copy(grad_in, out_at[0], out_sems.at[0]))
    sent[-1].start()
    for copy in steps[2]:
        copy.wait()
    act[...] = act[...] * keep
    for copy in steps[3]:
        copy.wait()
    for first in range(0, width, 256):
        span = slice(first, min(width, first + 256))
        grad_out[:, span] = lax.dot_general(
            act[...], grads[:, span], contract_first, preferred_element_type=jnp.float32
        ).astype(jnp.bfloat16)
    sent.append(pltpu.make_async_copy(grad_out, out_at[1], out_sems.at[1]))
    sent[-1].start()
    for copy in sent:
        copy.wait()


def weight_call(kept, saved):
    pieces = [piece for one in saved for piece in one]
    width, hidden = pieces[0].shape[1], pieces[2].shape[1]
    all_rows = sum(one[2].shape[0] for one in saved)
    vmem, anywhere = pl.BlockSpec(memory_space=pltpu.VMEM), pl.BlockSpec(memory_space=pl.ANY)
    return pl.pallas_call(
        weight_kernel,
        out_shape=(
            jax.ShapeDtypeStruct((width, hidden), jnp.bfloat16),
            jax.ShapeDtypeStruct((hidden, width), jnp.bfloat16),
        ),
        in_specs=[vmem] + [anywhere] * len(pieces),
        out_specs=(anywhere,) * 2,
        scratch_shapes=[pltpu.VMEM((all_rows, width), jnp.bfloat16)] * 2
        + [pltpu.VMEM((all_rows, hidden), jnp.bfloat16)] * 2
        + [pltpu.VMEM((width, hidden), jnp.bfloat16), pltpu.VMEM((hidden, width), jnp.bfloat16)]
        + [pltpu.SemaphoreType.DMA((len(saved), 6)), pltpu.SemaphoreType.DMA((2,))],
        compiler_params=pltpu.CompilerParams(vmem_limit_bytes=WLIM * MIB),
        cost_estimate=pl.CostEstimate(flops=0, bytes_accessed=0, transcendentals=0),
    )(kept, *pieces)


def load_kernel(in_at, out_at, matrix_in, matrix_out, sems):
    copies = [
        pltpu.make_async_copy(in_at, matrix_in, sems.at[0]),
        pltpu.make_async_copy(out_at, matrix_out, sems.at[1]),
    ]
    for copy in copies:
        copy.start()
    for copy in copies:
        copy.wait()


def load_call(matrix_in, matrix_out):
    vmem, anywhere = pl.BlockSpec(memory_space=pltpu.VMEM), pl.BlockSpec(memory_space=pl.ANY)
    return pl.pallas_call(
        load_kernel,
        out_shape=tuple(
            jax.ShapeDtypeStruct(one.shape, one.dtype) for one in (matrix_in, matrix_out)
        ),
        in_specs=[anywhere] * 2,
        out_specs=(vmem,) * 2,
        scratch_shapes=[pltpu.SemaphoreType.DMA((2,))],
        compiler_params=pltpu.CompilerParams(vmem_limit_bytes=8 * MIB),
        cost_estimate=pl.CostEstimate(flops=0, bytes_accessed=0, transcendentals=0),
    )(matrix_in, matrix_out)


def token_kernel(gates, places, cotangent, *refs):
    homes, (away, stay, gate_grad) = refs[:-3], refs[-3:]
    first_half = lax.axis_index("rep") == 0
    token_count, width = cotangent.shape
    half = width // 2
    diagonal = lax.broadcasted_iota(
        jnp.int32, (token_count, token_count), 0
    ) == lax.broadcasted_iota(jnp.int32, (token_count, token_count), 1)
    back = jnp.concatenate([one[...] for one in homes], axis=0)
    mixed, sums = 0.0, []
    for j in range(2):
        picker = jnp.concatenate([places[j, k] for k in range(len(homes))], axis=0)
        picked = lax.dot_general(
            picker, back, (((0,), (0,)), ((), ())), preferred_element_type=jnp.float32
        )
        gate = jnp.sum(jnp.where(diagonal, gates[j : j + 1], 0.0), axis=1, keepdims=True)
        mixed = mixed + picked * jnp.where(first_half, gate, 1.0)
        inner = jnp.sum(picked * cotangent[...].astype(jnp.float32), axis=1, keepdims=True)
        sums.append(jnp.sum(jnp.where(diagonal, inner, 0.0), axis=0, keepdims=True))
    mixed = mixed.astype(jnp.bfloat16).T
    upper, lower = mixed[:half], mixed[half:]
    away[:half] = jnp.where(first_half, lower, upper)
    stay[...] = jnp.where(first_half, upper, lower)
    left = jnp.concatenate(sums, axis=0)
    gate_grad[...] = left
    terms = []
    for _ in range(3):
        terms.append(left.astype(jnp.bfloat16))
        left = left - terms[-1].astype(jnp.float32)
    terms.append(jnp.zeros((away.shape[0] - half - 6, token_count), jnp.bfloat16))
    away[half:] = jnp.concatenate(terms, axis=0)


def token_call(gates, places, cotangent, homes):
    token_count, width = cotangent.shape
    vmem = pl.BlockSpec(memory_space=pltpu.VMEM)
    return pl.pallas_call(
        token_kernel,
        out_shape=(
            jax.ShapeDtypeStruct((width // 2 + 16, token_count), jnp.bfloat16),
            jax.ShapeDtypeStruct((width // 2, token_count), jnp.bfloat16),
            jax.ShapeDtypeStruct((2, token_count), jnp.float32),
        ),
        in_specs=[vmem] * (3 + len(homes)),
        out_specs=(vmem,) * 3,
        compiler_params=pltpu.CompilerParams(vmem_limit_bytes=16 * MIB),
        cost_estimate=pl.CostEstimate(flops=0, bytes_accessed=0, transcendentals=0),
    )(gates, places, cotangent, *homes)


def end_kernel(stay, got, gate_grad, output, grad_tokens, grad_gates):
    first_half = lax.axis_index("rep") == 0
    half = stay.shape[0]
    mine, theirs = stay[...], got[:half]
    output[...] = jnp.where(first_half, mine, theirs)
    grad_tokens[...] = jnp.where(first_half, theirs, mine)
    terms = got[half:].astype(jnp.float32)
    got_gate = terms[0:2] + terms[2:4] + terms[4:6]
    rows_half = gate_grad.shape[1] // 2
    grad_gates[...] = jnp.where(first_half, gate_grad[:, :rows_half], got_gate[:, rows_half:])


def end_call(stay, got, gate_grad):
    half, token_count = stay.shape
    vmem = pl.BlockSpec(memory_space=pltpu.VMEM)
    return pl.pallas_call(
        end_kernel,
        out_shape=(
            jax.ShapeDtypeStruct((half, token_count), jnp.bfloat16),
            jax.ShapeDtypeStruct((half, token_count), jnp.bfloat16),
            jax.ShapeDtypeStruct((2, token_count // 2), jnp.float32),
        ),
        in_specs=[vmem] * 3,
        out_specs=(vmem,) * 3,
        compiler_params=pltpu.CompilerParams(vmem_limit_bytes=16 * MIB),
    )(stay, got, gate_grad)


def plane_body(tokens, expert_ids, priority, gate_values, weight_in, weight_out, cotangent):
    token_count, width = tokens.shape
    dp_count = lax.axis_size("dp")
    experts = dp_count // HBLK
    slot_count = min(token_count, 2 * token_count // experts + max(1, token_count // (4 * experts)))
    capacity = 2 * token_count * dp_count // experts
    contract_first = (((0,), (0,)), ((), ()))
    contract_last = (((1,), (1,)), ((), ()))
    place_dp = lax.axis_index("dp")
    first_half = lax.axis_index("rep") == 0
    plane, quarter = place_dp // HBLK, place_dp % HBLK
    core_zero = quarter % 2 == 0
    groups = GROUPS

    def permutation(move):
        pairs = []
        for z in range(experts):
            for q in range(HBLK):
                for x in range(2):
                    z2, q2, x2 = move(z, q, x)
                    pairs.append((2 * (z * HBLK + q) + x, 2 * (z2 * HBLK + q2) + x2))
        return pairs

    def send(array, move):
        return lax.ppermute(array, ("dp", "rep"), permutation(move))

    def along_first(z, q, x):
        return (z, q, 1 - x) if q % 2 == 0 else (z, q ^ 2, x)

    def along_second(z, q, x):
        return (z, q ^ 2, x) if q % 2 == 0 else (z, q, 1 - x)

    def other_core(z, q, x):
        return (z, q ^ 1, x)

    def other_row(z, q, x):
        return (z, q ^ 2, x)

    def planes_on(k):
        return lambda z, q, x: ((z + k) % experts, q, x)

    def add(*terms):
        return sum(term.astype(jnp.float32) for term in terms).astype(jnp.bfloat16)

    def step(made, *values):
        if made:
            values, _ = lax.optimization_barrier((values, made))
        return values if len(values) > 1 else values[0]

    def join(parts):
        return parts[0] if len(parts) == 1 else jnp.concatenate(parts, axis=0)

    ids, gates = expert_ids.T, gate_values.T
    places, *blocks = start_call(
        ids, priority[None, :], gates, tokens, cotangent, experts, slot_count
    )
    block_rows = blocks[0].shape[0]

    matrix_in = weight_in[0]
    matrix_out = weight_out[0]
    state = [{} for _ in groups]
    home = {}

    def spread_first(g, block):
        one = state[g]
        one["b00"] = block
        one["r1"] = send(block, along_first)
        one["r2"] = send(block, along_second)
        return [one["r1"]]

    def spread_second(g, made):
        one = state[g]
        one["r1"] = step(made, one["r1"])
        one["b11"] = send(one["r1"], along_second)
        return [one["b11"]]

    def gather_near(g, made):
        one = state[g]
        b00, r1, r2, b11 = step(made, one["b00"], one["r1"], one["r2"], one["b11"])
        b10 = jnp.where(core_zero, r2, r1)
        b01 = jnp.where(core_zero, r1, r2)
        one["near"] = jnp.concatenate(
            [
                jnp.where(first_half, b00, b01),
                jnp.where(first_half, b10, b11),
                jnp.where(first_half, b01, b00),
                jnp.where(first_half, b11, b10),
            ],
            axis=0,
        )
        one["far"] = send(one["near"], other_core)
        return [one["near"]]

    def expert_work(g, made, matrix_in, matrix_out):
        one = state[g]
        near_rows, far_rows = step(made, one["near"], one["far"])
        near_parts, far_parts, act, pre = expert_call(near_rows, far_rows, matrix_in, matrix_out)
        one["saved"] = (near_rows, far_rows, act, pre)
        one["near_parts"], one["far_parts"] = near_parts, send(far_parts, other_core)
        return [act]

    def reduce_first(g, made):
        one = state[g]
        sums = add(*step(made, one["near_parts"], one["far_parts"]))
        out0, out1, dx0, dx1 = [
            sums[at * block_rows : at * block_rows + slot_count] for at in range(4)
        ]
        a00, a10 = jnp.where(first_half, out0, dx0), jnp.where(first_half, out1, dx1)
        a01, a11 = jnp.where(first_half, dx0, out0), jnp.where(first_half, dx1, out1)
        away = jnp.concatenate([jnp.where(core_zero, a01, a10), a11], axis=0)
        one["a00"], one["rest"] = a00, jnp.where(core_zero, a10, a01)
        one["back"] = send(away, along_first)
        return [away]

    def reduce_second(g, made):
        one = state[g]
        one["back"], rest = step(made, one["back"], one["rest"])
        last = add(rest, one["back"][slot_count:])
        one["last"] = send(last, along_second)
        return [last]

    def go_home(g, made):
        one = state[g]
        a00, back, last = step(made, one["a00"], one["back"], one["last"])
        (k,) = groups[g]
        done = (
            (a00.astype(jnp.float32) + back[:slot_count].astype(jnp.float32) + last.astype(jnp.float32))
            * mine[g, :slot_count, 0:1]
        ).astype(jnp.bfloat16)
        home[k] = done if k == 0 else send(done, planes_on(experts - k))
        return [done]

    arrived, events = {}, {}
    for entry in PLAN:
        name, g, *after = entry.split()
        g = int(g)
        made = [value for one in after for value in events[one]]
        if name == "Z":
            arrived[g] = send(step(made, blocks[g]), planes_on(g))
            here = [arrived[g]]
        elif name == "D1":
            (k,) = groups[g]
            here = spread_first(g, step(made, arrived[k] if k else blocks[0]))
        elif name == "D2":
            here = spread_second(g, made)
        elif name == "SEL":
            here = gather_near(g, made)
        elif name == "L":
            matrix_in, matrix_out = load_call(matrix_in, matrix_out)
            here = [matrix_out]
        elif name == "E":
            here = expert_work(g, made, matrix_in, matrix_out)
        elif name == "CUT":
            pieces = [piece for one in state for piece in one["saved"][:2]]
            kept, mine = cut_call(step(made, *pieces), slot_count, block_rows, capacity)
            here = [mine]
        elif name == "R1":
            here = reduce_first(g, made)
        elif name == "R2":
            here = reduce_second(g, made)
        elif name == "H":
            here = go_home(g, made)
        elif name == "W":
            saved = [step(made, *one["saved"]) for one in state]
            grad_in, grad_out = weight_call(kept, saved)
            here = [grad_in]
        events[name + str(g)] = here

    away, stay, gate_grad = token_call(gates, places, cotangent, [home[k] for k in range(experts)])
    got = lax.ppermute(away, "rep", [(0, 1), (1, 0)])
    output, grad_tokens, grad_gates = end_call(stay, got, gate_grad)
    return output.T, grad_tokens.T, grad_gates.T, grad_in[None], grad_out[None]


def solution(mesh):
    placed = (
        P("dp", None),
        P("dp", None),
        P("dp"),
        P("dp", None),
        P("dp", None, "rep"),
        P("dp", "rep", None),
        P("dp", None),
    )
    body = plane_body if mesh.shape["rep"] == 2 and mesh.shape["dp"] == 4 * HBLK else general_body
    return jax.shard_map(
        body,
        mesh=mesh,
        in_specs=placed,
        out_specs=(
            P("dp", "rep"),
            P("dp", "rep"),
            P(("dp", "rep"), None),
            P("dp", None, "rep"),
            P("dp", "rep", None),
        ),
        check_vma=False,
    )
```
